32 devices in a mesh: seq: 16 (over z, x, core), head: 2 (over y).
Axes of the slice: x: 2, y: 2, z: 4, core: 2. Of those that a mesh axis runs over, the one named last changes fastest.
Arguments:
- draft_query: bfloat16 [1, 96, 8192], P(None, 'seq', 'head'), may hold values from -28 to 28
- draft_key: bfloat16 [1, 96, 1024], P(None, 'seq', 'head'), may hold values from -8 to 8
- draft_value: bfloat16 [1, 96, 1024], P(None, 'seq', 'head'), may hold values from -48 to 48
- cache_key: bfloat16 [1, 16384, 1024], P(None, 'seq', 'head'), may hold values from -16 to 16
- cache_value: bfloat16 [1, 16384, 1024], P(None, 'seq', 'head'), may hold values from -48 to 48
- accepted: int32 [1], replicated, may hold values from 0 to 96
- cache_len: int32 [1], replicated, may hold values from 4096 to 16288
- out_weight: bfloat16 [8192, 8192], P('head', 'seq'), may hold values from -0.0625 to 0.0625
Outputs:
- projected: bfloat16 [1, 96, 8192], P(None, 'head', 'seq')
- new_key: bfloat16 [1, 16384, 1024], P(None, 'seq', 'head')
- new_value: bfloat16 [1, 16384, 1024], P(None, 'seq', 'head')
The draws below stay inside these ranges and needn't reach their ends.
All inputs are finite; a program needn't handle non-finite values.
Results may differ from the reference program's by a relative error of at most 0.0052.
Values may be sent and summed in bfloat16 or wider, within the bound.
No kernel may reach another device: no remote copies, remote signals or barrier semaphores. Data moves between devices by JAX's collectives and lax.ppermute only.
A program may use at most 64 MiB of HBM per device.

```python
import math
import jax
import jax.numpy as jnp
from jax import lax

D = 8192
QH = 64
KVH = 8
HD = 128
REQUESTS = 1
CACHE_DEV = 1024
DRAFT_LEN = 96
CONTEXT = 16384
N_SEQ = 16


def draw_draft_query(key, part):
    sample = jax.random.normal(jax.random.fold_in(key, 11), (REQUESTS, DRAFT_LEN, QH, HD), jnp.float32)
    sample = jnp.clip(sample, -4.0, 4.0)
    return sample.reshape(REQUESTS, DRAFT_LEN, QH * HD).astype(jnp.bfloat16)


def draw_cache_key(key, part):
    sample = jax.random.normal(jax.random.fold_in(key, 21), (REQUESTS, CONTEXT, KVH, HD), jnp.float32)
    sample = jnp.clip(sample, -4.0, 4.0) * 2.0
    return sample.reshape(REQUESTS, CONTEXT, KVH * HD).astype(jnp.bfloat16)


def block_scale(rng, dims, split, smallest, high):
    def one(dim, parts):
        draws = jax.random.uniform(jax.random.fold_in(jax.random.fold_in(rng, 6), dim), (parts,), jnp.float32, smallest / len(split), high / len(split))
        return jnp.repeat(jnp.exp(draws), dims[dim] // parts).reshape((-1,) + (1,) * (len(dims) - dim - 1))

    loudness = one(*split[0])
    for cut in split[1:]:
        loudness = loudness * one(*cut)
    return loudness


def normal_values(key, shape, width, limit, pieces=(), kind=jnp.bfloat16):
    entries = jax.random.normal(key, shape, jnp.float32) * width
    if len(pieces) > 0:
        entries = block_scale(key, shape, pieces, -0.22, 0.18) * entries
    return jnp.clip(entries, min=-limit, max=limit).astype(kind)


def setup_inputs(seed: int = 0) -> dict:
    seeds = jax.random.split(jax.random.key(seed), 9)
    draft_query = draw_draft_query(jax.random.fold_in(seeds[8], 71), 0)
    draft_key = normal_values(seeds[1], (REQUESTS, DRAFT_LEN, KVH * HD), 2.0, 8.0, ((1, 16), (2, 2)))
    draft_value = normal_values(seeds[2], (REQUESTS, DRAFT_LEN, KVH * HD), 8.0, 48.0, ((1, 16), (2, 2)))
    cache_key = draw_cache_key(jax.random.fold_in(seeds[8], 71), 0)
    cache_value = normal_values(seeds[4], (REQUESTS, CONTEXT, KVH * HD), 8.0, 48.0, ((1, 16), (2, 2)))
    accepted = jax.random.randint(seeds[5], (REQUESTS,), 0, DRAFT_LEN + 1).astype(jnp.int32)
    cache_len = jax.random.randint(seeds[6], (REQUESTS,), CONTEXT // 4, CONTEXT - DRAFT_LEN + 1).astype(jnp.int32)
    out_weight = normal_values(seeds[7], (QH * HD, D), (QH * HD) ** -0.5, 0.0625, ((0, 2), (1, 16)))
    return dict(draft_query=draft_query, draft_key=draft_key, draft_value=draft_value, cache_key=cache_key, cache_value=cache_value, accepted=accepted, cache_len=cache_len, out_weight=out_weight)


masked_score = -1e+30

def block_partial(queries, keys_cache, values_cache, keys_draft, values_draft, live_cache, live_draft):
    scale_factor = 1.0 / math.sqrt(HD)
    cache_scores = jnp.einsum('tkgd,ckd->tkgc', queries, keys_cache) * scale_factor
    draft_scores = jnp.einsum('tkgd,ukd->tkgu', queries, keys_draft) * scale_factor
    cache_mask = live_cache[None, None, None, :]
    draft_mask = live_draft[:, None, None, :]
    maxima = jnp.maximum(lax.optimization_barrier(jnp.max(jnp.where(cache_mask, cache_scores, masked_score), axis=-1)), lax.optimization_barrier(jnp.max(jnp.where(draft_mask, draft_scores, masked_score), axis=-1)))
    cache_probs = jnp.where(cache_mask, jnp.exp(cache_scores - maxima[..., None]), 0.0).astype(jnp.bfloat16)
    draft_probs = jnp.where(draft_mask, jnp.exp(draft_scores - maxima[..., None]), 0.0).astype(jnp.bfloat16)
    cache_probs = lax.optimization_barrier(cache_probs).astype(jnp.float32)
    draft_probs = lax.optimization_barrier(draft_probs).astype(jnp.float32)
    totals = lax.optimization_barrier(jnp.sum(cache_probs, axis=-1)) + lax.optimization_barrier(jnp.sum(draft_probs, axis=-1))
    weighted = jnp.einsum('tkgc,ckd->tkgd', cache_probs, values_cache) + jnp.einsum('tkgu,ukd->tkgd', draft_probs, values_draft)
    return (maxima, totals, weighted)

def request_attention(request_data):
    queries, cache_keys, cache_values, draft_keys, draft_values, length = request_data
    group_size = QH // KVH
    queries = queries.astype(jnp.float32).reshape(DRAFT_LEN, KVH, group_size, HD)
    draft_rows = DRAFT_LEN // N_SEQ
    query_positions = jnp.arange(DRAFT_LEN, dtype=jnp.int32)

    def scan_block(running, block_index):
        running_max, numerator, denominator = running
        cache_start = (block_index * CACHE_DEV).astype(jnp.int32)
        draft_start = (block_index * draft_rows).astype(jnp.int32)
        keys_cache = lax.dynamic_slice_in_dim(cache_keys, cache_start, CACHE_DEV, 0).astype(jnp.float32).reshape(CACHE_DEV, KVH, HD)
        values_cache = lax.dynamic_slice_in_dim(cache_values, cache_start, CACHE_DEV, 0).astype(jnp.float32).reshape(CACHE_DEV, KVH, HD)
        keys_draft = lax.dynamic_slice_in_dim(draft_keys, draft_start, draft_rows, 0).astype(jnp.float32).reshape(draft_rows, KVH, HD)
        values_draft = lax.dynamic_slice_in_dim(draft_values, draft_start, draft_rows, 0).astype(jnp.float32).reshape(draft_rows, KVH, HD)
        live_cache = cache_start + jnp.arange(CACHE_DEV, dtype=jnp.int32) < length
        draft_positions = draft_start + jnp.arange(draft_rows, dtype=jnp.int32)
        live_draft = draft_positions[None, :] <= query_positions[:, None]
        maxima, totals, weighted = block_partial(queries, keys_cache, values_cache, keys_draft, values_draft, live_cache, live_draft)
        new_max = jnp.maximum(running_max, maxima)
        old_factor = jnp.exp(running_max - new_max)
        new_factor = jnp.exp(maxima - new_max)
        numerator = numerator * old_factor[..., None] + weighted * new_factor[..., None]
        denominator = denominator * old_factor + totals * new_factor
        return ((new_max, numerator, denominator), None)
    start_state = (jnp.full((DRAFT_LEN, KVH, group_size), masked_score, jnp.float32), jnp.zeros((DRAFT_LEN, KVH, group_size, HD), jnp.float32), jnp.zeros((DRAFT_LEN, KVH, group_size), jnp.float32))
    final_state, _ = lax.scan(scan_block, start_state, jnp.arange(N_SEQ, dtype=jnp.int32))
    running_max, numerator, denominator = final_state
    attention = numerator / denominator[..., None]
    return attention.reshape(DRAFT_LEN, QH * HD).astype(jnp.bfloat16)

def append_rows(cache_rows, draft_rows_all, accepted, cache_len):
    positions = jnp.arange(CONTEXT, dtype=jnp.int32)
    offsets = positions[None, :] - cache_len[:, None]
    chosen = (offsets >= 0) & (offsets < accepted[:, None])
    indices = jnp.clip(offsets, 0, DRAFT_LEN - 1).astype(jnp.int32)
    picked = jax.vmap(lambda rows_all, index_row: rows_all[index_row])(draft_rows_all, indices)
    return jnp.where(chosen[..., None], picked, cache_rows)

def reference(draft_query, draft_key, draft_value, cache_key, cache_value, accepted, cache_len, out_weight):
    attention = lax.map(request_attention, (draft_query, cache_key, cache_value, draft_key, draft_value, cache_len))
    flat_rows = attention.reshape(REQUESTS * DRAFT_LEN, QH * HD)
    projected = jnp.dot(flat_rows, out_weight, preferred_element_type=jnp.float32).astype(jnp.bfloat16)
    projected = projected.reshape(REQUESTS, DRAFT_LEN, D)
    new_key = append_rows(cache_key, draft_key, accepted, cache_len)
    new_value = append_rows(cache_value, draft_value, accepted, cache_len)
    return (projected, new_key, new_value)
```

```python
import functools
import math

import jax
import jax.numpy as jnp
from jax import lax
from jax.experimental import pallas as pl
from jax.experimental.pallas import tpu as pltpu
from jax.sharding import PartitionSpec as P

QH = 64
KVH = 8
HD = 128
GROUP = QH // KVH
LANES = 128

DEAD = -1e30
FLOOR = -1e29
LOG2_SCALE = math.log2(math.e) / math.sqrt(HD)
VMEM_BYTES = 48 * 1024 * 1024

bf16 = jnp.bfloat16
f32 = jnp.float32


def round_up(n, m):
    return -(-n // m) * m


def stat_rows(units):
    return round_up(3 * round_up(units, 8), 16)


def pad_rows(x, rows):
    if x.shape[0] == rows:
        return x
    return jnp.concatenate([x, jnp.zeros((rows - x.shape[0], x.shape[1]), x.dtype)], axis=0)


def columns_to_rows(columns, unit):
    lane = lax.broadcasted_iota(jnp.int32, (unit, LANES), 1)
    square = jnp.zeros((unit, LANES), f32)
    for place, column in columns:
        square = jnp.where(lane == place, column, square)
    return jnp.transpose(pad_rows(square, LANES))


def split_total(total):
    high = total.astype(bf16)
    return high, (total - high.astype(f32)).astype(bf16)


def write_message(out_ref, row, shift, total):
    high, low = split_total(total)
    rows = jnp.concatenate([shift, high.astype(f32), low.astype(f32)], axis=0)
    out_ref[row : row + stat_rows(shift.shape[0]), :] = pad_rows(
        rows, stat_rows(shift.shape[0])
    ).astype(bf16)


def attend_kernel(rel, unit_rows, split, as_message, scal, q_ref, k_ref, v_ref, *rest):
    if split == 2:
        kv_ref, d_ref, *outs = rest
    else:
        d_ref, *outs = rest
    units, heads, unit, _ = q_ref.shape
    keys = k_ref.shape[0]
    seq, length = scal[0], scal[1]
    chip = lax.div(seq, split)
    count = units * heads
    count8 = round_up(count, 8)
    step = max(n for n in range(1, units + 1) if units % n == 0 and n * unit <= 384)
    columns = []
    out_ref = outs[0]
    key_index = lax.broadcasted_iota(jnp.int32, (1, keys), 1)
    for head in range(heads):
        lanes = slice(head * HD, (head + 1) * HD)
        pieces = [(k_ref[:, lanes], v_ref[:, lanes], key_index + seq * keys < length)]
        if split == 2:
            values = slice((heads + head) * HD, (heads + head + 1) * HD)
            other = seq + 1 - 2 * lax.rem(seq, 2)
            pieces.append(
                (kv_ref[:, lanes], kv_ref[:, values], key_index + other * keys < length)
            )
        for start in range(0, units, step):
            rows = step * unit
            queries = q_ref[start : start + step, head].reshape(rows, HD)
            time = jnp.concatenate(
                [
                    lax.shift_right_logical(lax.broadcasted_iota(jnp.int32, (unit, LANES), 0), 3)
                    + unit_rows * jnp.bitwise_xor(chip, rel[start + n])
                    for n in range(step)
                ],
                axis=0,
            )
            draft = lax.broadcasted_iota(jnp.int32, (rows, LANES), 1)
            causal = (draft < unit_rows) & (draft + unit_rows * chip <= time)
            scores, rhs = [], []
            for keys_piece, values_piece, live in pieces + [
                (d_ref[head, :LANES], d_ref[head, LANES:], causal)
            ]:
                score = lax.dot_general(
                    queries, keys_piece, (((1,), (1,)), ((), ())), preferred_element_type=f32
                )
                scores.append(jnp.where(live, score * LOG2_SCALE, DEAD))
                rhs.append(values_piece)
            top = functools.reduce(
                jnp.maximum, [jnp.max(s, axis=1, keepdims=True) for s in scores]
            )
            shift = jnp.maximum(top, FLOOR).astype(bf16).astype(f32)
            probs = [jnp.exp2(s - shift).astype(bf16) for s in scores]
            total = sum(jnp.sum(p.astype(f32), axis=1, keepdims=True) for p in probs)
            weighted = sum(
                jnp.dot(p, v, preferred_element_type=f32) for p, v in zip(probs, rhs)
            )
            for n in range(step):
                place = (start + n) * heads + head
                part = slice(n * unit, (n + 1) * unit)
                out_ref[place * unit : (place + 1) * unit, :] = weighted[part].astype(out_ref.dtype)
                columns.append((place, shift[part]))
                columns.append((count8 + place, total[part]))
    stats = columns_to_rows(columns, unit)
    if as_message:
        write_message(out_ref, count * unit, stats[:count8], stats[count8 : 2 * count8])
    else:
        outs[1][...] = stats[: 2 * count8]


def attend(scal, q, rel, unit_rows, split, cache_k, cache_v, kv_other, drafts, as_message):
    units, heads, unit, _ = q.shape
    keys = cache_k.shape[0]
    count = units * heads
    if as_message:
        out_shape = jax.ShapeDtypeStruct((count * unit + stat_rows(count), LANES), bf16)
        out_specs = pl.BlockSpec(out_shape.shape, lambda i, s: (0, 0))
    else:
        out_shape = (
            jax.ShapeDtypeStruct((count * unit, LANES), f32),
            jax.ShapeDtypeStruct((2 * round_up(count, 8), LANES), f32),
        )
        out_specs = tuple(pl.BlockSpec(o.shape, lambda i, s: (0, 0)) for o in out_shape)
    cache_spec = pl.BlockSpec((keys, heads * HD), lambda i, s: (0, lax.rem(s[0], split)))
    in_specs = [pl.BlockSpec(q.shape, lambda i, s: (0, 0, 0, 0)), cache_spec, cache_spec]
    operands = [q, cache_k, cache_v]
    if split == 2:
        in_specs.append(pl.BlockSpec(kv_other.shape, lambda i, s: (0, 0)))
        operands.append(kv_other)
    in_specs.append(pl.BlockSpec(drafts.shape, lambda i, s: (0, 0, 0)))
    operands.append(drafts)
    scores = count * unit * (split * keys + LANES)
    return pl.pallas_call(
        functools.partial(attend_kernel, rel, unit_rows, split, as_message),
        grid_spec=pltpu.PrefetchScalarGridSpec(
            num_scalar_prefetch=1, grid=(1,), in_specs=in_specs, out_specs=out_specs
        ),
        out_shape=out_shape,
        compiler_params=pltpu.CompilerParams(vmem_limit_bytes=VMEM_BYTES),
        cost_estimate=pl.CostEstimate(
            flops=4 * scores * HD, bytes_accessed=4 * split * keys * heads * HD, transcendentals=scores
        ),
    )(scal, *operands)


def merge_kernel(unit, mode, num_ref, stat_ref, msg_ref, *outs):
    rows = num_ref.shape[0]
    count = rows // unit
    count8 = stat_ref.shape[0] // 2
    own_shift, own_total = stat_ref[:count8], stat_ref[count8:]
    sent = msg_ref[rows:, :].astype(f32)
    shift = sent[:count8]
    total = sent[count8 : 2 * count8] + sent[2 * count8 : 3 * count8]
    half = count // 2
    if mode == "final":
        shift = pad_rows(jnp.concatenate([shift[half:count], shift[:half]], axis=0), count8)
        total = pad_rows(jnp.concatenate([total[half:count], total[:half]], axis=0), count8)
    new_shift = jnp.maximum(own_shift, shift)
    own_factor = jnp.exp2(own_shift - new_shift)
    factor = jnp.exp2(shift - new_shift)
    new_total = own_total * own_factor + total * factor
    if mode == "final":
        new_total = jnp.where(new_total > 0, new_total, 1.0)
        own_factor = own_factor / new_total
        factor = factor / new_total
    factors = jnp.transpose(pad_rows(jnp.concatenate([own_factor, factor], axis=0), LANES))
    for n in range(count):
        source = (n + half) % count if mode == "final" else n
        merged = num_ref[n * unit : (n + 1) * unit, :] * factors[:unit, n : n + 1]
        merged = merged + (
            msg_ref[source * unit : (source + 1) * unit, :].astype(f32)
            * factors[:unit, count8 + n : count8 + n + 1]
        )
        here = slice(n * unit, (n + 1) * unit)
        if mode == "final":
            outs[0][here, :] = merged.astype(bf16)
        elif mode == "all":
            outs[0][here, :] = merged
            outs[2][here, :] = merged.astype(bf16)
        elif n < half:
            outs[0][here, :] = merged
        else:
            outs[2][(n - half) * unit : (n - half + 1) * unit, :] = merged.astype(bf16)
    if mode == "all":
        outs[1][...] = jnp.concatenate([new_shift, new_total], axis=0)
        write_message(outs[2], rows, new_shift, new_total)
    elif mode == "half":
        half8 = round_up(half, 8)
        outs[1][...] = jnp.concatenate(
            [pad_rows(new_shift[:half], half8), pad_rows(new_total[:half], half8)], axis=0
        )
        write_message(
            outs[2],
            half * unit,
            pad_rows(new_shift[half:count], half8),
            pad_rows(new_total[half:count], half8),
        )


def merge(unit, mode, num, stats, message):
    rows = num.shape[0]
    if mode == "final":
        out_shape = jax.ShapeDtypeStruct((rows, LANES), bf16)
    else:
        rows = rows // 2 if mode == "half" else rows
        count = rows // unit
        out_shape = (
            jax.ShapeDtypeStruct((rows, LANES), f32),
            jax.ShapeDtypeStruct((2 * round_up(count, 8), LANES), f32),
            jax.ShapeDtypeStruct((rows + stat_rows(count), LANES), bf16),
        )
    return pl.pallas_call(
        functools.partial(merge_kernel, unit, mode),
        out_shape=out_shape,
        compiler_params=pltpu.CompilerParams(vmem_limit_bytes=VMEM_BYTES),
    )(num, stats, message)


def project_kernel(rel, split, n_head, scal, *refs):
    sources = refs[: 2 * split]
    w_ref = refs[2 * split]
    outs = refs[2 * split + 1 : -2]
    rows_ref, lhs_ref = refs[-2:]
    seq, head = scal[0], scal[2]
    chip = lax.div(seq, split)
    core = lax.rem(seq, split)
    heads_kv = rows_ref.shape[0]
    units, heads, unit, _ = sources[0].shape
    chips = 2 * units
    first = head * (chips // n_head) if n_head == 2 else 0
    for side in range(split):
        owner = core if side == 0 else 1 - core
        for part in range(2):
            x_ref = sources[2 * side + part]
            for n in range(units):
                place = lax.rem(jnp.bitwise_xor(chip, rel[part][n]) - first + chips, chips)
                for h in range(heads):
                    rows_ref[
                        owner * heads + h, pl.ds(pl.multiple_of(place * unit, unit), unit), :
                    ] = x_ref[n, h].astype(f32)
    rows = lhs_ref.shape[0]
    for kv in range(heads_kv):
        for g in range(GROUP):
            lanes = slice((kv * GROUP + g) * HD, (kv * GROUP + g + 1) * HD)
            lhs_ref[:, lanes] = rows_ref[kv, pl.ds(g, rows, stride=GROUP), :].astype(bf16)
    result = jnp.dot(lhs_ref[...], w_ref[...], preferred_element_type=f32)
    if n_head == 2:
        outs[0][...] = result[: rows // 2]
        outs[1][...] = result[rows // 2 :]
    else:
        outs[0][...] = result


def project(scal, rel, split, n_head, sources, weight):
    units, heads, unit, _ = sources[0].shape
    heads_kv = heads * split
    rows = 2 * units * unit // GROUP
    columns = weight.shape[1]
    if n_head == 2:
        out_shape = (jax.ShapeDtypeStruct((rows // 2, columns), f32),) * 2
    else:
        out_shape = (jax.ShapeDtypeStruct((rows, columns), f32),)
    return pl.pallas_call(
        functools.partial(project_kernel, rel, split, n_head),
        in_specs=[pl.BlockSpec(memory_space=pltpu.SMEM)]
        + [pl.BlockSpec(memory_space=pltpu.VMEM)] * (2 * split + 1),
        out_shape=out_shape,
        scratch_shapes=[
            pltpu.VMEM((heads_kv, 2 * units * unit, LANES), f32),
            pltpu.VMEM((rows, heads_kv * GROUP * HD), bf16),
        ],
        compiler_params=pltpu.CompilerParams(vmem_limit_bytes=VMEM_BYTES),
    )(scal, *sources, weight)


def one_request(n_seq, n_head, dq, dk, dv, ck, cv, accepted, length, weight):
    seq = lax.axis_index("seq")
    local_rows = dq.shape[0]
    heads_kv = dk.shape[1] // HD
    cache_rows = ck.shape[0]
    split = 2 if heads_kv % 2 == 0 else 1
    heads = heads_kv // split
    unit_rows = local_rows * split
    unit = unit_rows * GROUP
    n_bits = n_seq.bit_length() - 1
    bits = list(range(n_bits - 1, split - 2, -1))

    def swap(x, bit):
        return lax.ppermute(x, "seq", [(i, i ^ (1 << bit)) for i in range(n_seq)])

    scal = jnp.stack([seq, length, lax.axis_index("head")]).astype(jnp.int32)
    chip = seq // split
    core = seq % split

    q4 = dq.reshape(local_rows, heads_kv, GROUP * HD // LANES, LANES).transpose(1, 0, 2, 3)
    q4 = q4.reshape(heads_kv, local_rows * GROUP, LANES)
    dk4 = dk.reshape(local_rows, heads_kv, HD).transpose(1, 0, 2)
    dv4 = dv.reshape(local_rows, heads_kv, HD).transpose(1, 0, 2)
    pack = jnp.concatenate([q4, dk4, dv4], axis=1)
    kv_other = None
    if split == 2:
        mine = lax.dynamic_slice_in_dim(pack, core * heads, heads, 0)
        recv = swap(lax.dynamic_slice_in_dim(pack, (1 - core) * heads, heads, 0), 0)
        parts = [jnp.where(core == 0, mine, recv), jnp.where(core == 0, recv, mine)]
        width = heads * HD
        kv_other = swap(
            jnp.concatenate(
                [
                    lax.dynamic_slice_in_dim(ck, (1 - core) * width, width, 1),
                    lax.dynamic_slice_in_dim(cv, (1 - core) * width, width, 1),
                ],
                axis=1,
            ),
            0,
        )
    else:
        parts = [pack]
    cut = local_rows * GROUP
    q = jnp.concatenate([p[:, :cut] for p in parts], axis=1)[None]
    d_key = jnp.concatenate([p[:, cut : cut + local_rows] for p in parts], axis=1)
    d_value = jnp.concatenate([p[:, cut + local_rows :] for p in parts], axis=1)
    spare = ((0, 0), (0, LANES - unit_rows), (0, 0))
    drafts = jnp.concatenate([jnp.pad(d_key, spare), jnp.pad(d_value, spare)], axis=1)

    rel = [0]
    for bit in bits[:-1]:
        q = jnp.concatenate([q, swap(q, bit)], axis=0)
        rel = rel + [r | (1 << bit) // split for r in rel]
    near = bits[-1]
    rel_far = [r | (1 << near) // split for r in rel]
    q_far = swap(q, near)

    run = functools.partial(attend, scal)
    message = run(q, rel, unit_rows, split, ck, cv, kv_other, drafts, True)
    num, stats = run(q_far, rel_far, unit_rows, split, ck, cv, kv_other, drafts, False)
    message = swap(message, near)
    for bit in reversed(bits[:-1]):
        mode = "all" if bit == bits[0] else "half"
        num, stats, message = merge(unit, mode, num, stats, message)
        message = swap(message, bit)
    att = merge(unit, "final", num, stats, message).reshape(-1, heads, unit, LANES)
    for bit in bits[1:-1]:
        att = jnp.concatenate([att, swap(att, bit)], axis=0)
    att_near = swap(att, near)
    sources = [att, att_near]
    if split == 2:
        sources += [swap(att, 0), swap(att_near, 0)]
    result = project(scal, (rel_far, rel), split, n_head, sources, weight)
    if n_head == 2:
        keep, send = result
        projected = keep + lax.ppermute(send, "head", [(0, 1), (1, 0)])
    else:
        projected = lax.psum_scatter(result[0], "head", scatter_dimension=0, tiled=True)

    dkv = jnp.concatenate([d_key, d_value], axis=1)[None]
    for bit in bits:
        dkv = jnp.concatenate([dkv, swap(dkv, bit)], axis=0)
    if split == 2:
        other = swap(dkv, 0)
        dkv = jnp.concatenate(
            [jnp.where(core == 0, dkv, other), jnp.where(core == 0, other, dkv)], axis=1
        )
    every = jnp.asarray(rel + rel_far, jnp.int32)
    source = (chip ^ every)[:, None] * unit_rows + jnp.arange(unit_rows, dtype=jnp.int32)
    source = source.reshape(-1)
    place = seq * cache_rows + jnp.arange(cache_rows, dtype=jnp.int32) - length
    pick = (place[:, None] == source[None, :]) & (source < accepted)[None, :]
    chosen = ((place >= 0) & (place < accepted))[:, None]

    def append(cache, rows):
        rows = rows.transpose(0, 2, 1, 3).reshape(-1, heads_kv * HD)
        moved = jnp.dot(pick.astype(bf16), rows, preferred_element_type=f32).astype(bf16)
        return jnp.where(chosen, moved, cache)

    new_key = append(ck, dkv[:, :, :unit_rows])
    new_value = append(cv, dkv[:, :, unit_rows:])
    return projected.astype(bf16), new_key, new_value


def on_device(n_seq, n_head, dq, dk, dv, ck, cv, accepted, cache_len, weight):
    results = [
        one_request(
            n_seq, n_head, dq[r], dk[r], dv[r], ck[r], cv[r], accepted[r], cache_len[r], weight
        )
        for r in range(dq.shape[0])
    ]
    return tuple(jnp.stack(parts) for parts in zip(*results))


def solution(mesh):
    in_specs = (
        P(None, "seq", "head"),
        P(None, "seq", "head"),
        P(None, "seq", "head"),
        P(None, "seq", "head"),
        P(None, "seq", "head"),
        P(),
        P(),
        P("head", "seq"),
    )
    out_specs = (P(None, "head", "seq"), P(None, "seq", "head"), P(None, "seq", "head"))
    return jax.shard_map(
        functools.partial(on_device, mesh.shape["seq"], mesh.shape["head"]),
        mesh=mesh,
        in_specs=in_specs,
        out_specs=out_specs,
        check_vma=False,
    )
```

```python
import functools
import math

import jax
import jax.numpy as jnp
from jax import lax
from jax.experimental import pallas as pl
from jax.experimental.pallas import tpu as pltpu
from jax.sharding import PartitionSpec as P

QH = 64
KVH = 8
HD = 128
GROUP = QH // KVH
LANES = 128

DEAD = -1e30
FLOOR = -(2.0**96)
LOG2_SCALE = math.log2(math.e) / math.sqrt(HD)
VMEM_BYTES = 48 * 1024 * 1024

bf16 = jnp.bfloat16
f32 = jnp.float32


def round_up(n, m):
    return -(-n // m) * m


def stat_rows(units):
    return round_up(3 * round_up(units, 8), 16)


def pad_rows(x, rows):
    if x.shape[0] == rows:
        return x
    return jnp.concatenate([x, jnp.zeros((rows - x.shape[0], x.shape[1]), x.dtype)], axis=0)


def columns_to_rows(columns, unit):
    lane = lax.broadcasted_iota(jnp.int32, (unit, LANES), 1)
    square = jnp.zeros((unit, LANES), f32)
    for place, column in columns:
        square = jnp.where(lane == place, column, square)
    return jnp.transpose(pad_rows(square, LANES))


def split_total(total):
    high = total.astype(bf16)
    return high, (total - high.astype(f32)).astype(bf16)


def write_message(out_ref, row, shift, total):
    high, low = split_total(total)
    rows = jnp.concatenate([shift, high.astype(f32), low.astype(f32)], axis=0)
    out_ref[row : row + stat_rows(shift.shape[0]), :] = pad_rows(
        rows, stat_rows(shift.shape[0])
    ).astype(bf16)


def row_of(place, local_rows, core):
    return place + jnp.where(place < local_rows, core, -core) * local_rows


def attend_kernel(rel, unit_rows, split, as_message, n_after, len_ref, q_ref, *rest):
    caches = rest[: 2 * split]
    d_ref = rest[2 * split]
    outs = rest[2 * split + 1 + n_after :]
    units, heads = q_ref.shape[:2]
    unit = unit_rows * GROUP
    keys = caches[0].shape[0]
    seq, length = lax.axis_index("seq"), len_ref[0]
    chip = lax.div(seq, split)
    count = units * heads
    count8 = round_up(count, 8)
    step = max(n for n in range(1, units + 1) if units % n == 0 and n * unit <= 384)
    columns = []
    out_ref = outs[0]
    key_index = lax.broadcasted_iota(jnp.int32, (1, keys), 1)
    core = lax.rem(seq, split)
    local_rows = unit_rows // split
    ones = jnp.ones((keys, LANES), bf16)
    draft = lax.broadcasted_iota(jnp.int32, (1, LANES), 1)
    draft_row = unit_rows * chip + row_of(draft, local_rows, core)
    unit_row = row_of(
        lax.shift_right_logical(lax.broadcasted_iota(jnp.int32, (unit, LANES), 0), 3),
        local_rows,
        core,
    )
    for head in range(heads):
        lanes = slice(head * HD, (head + 1) * HD)
        draft_values = jnp.concatenate([d_ref[head, LANES:], ones[:LANES]], axis=1)
        for start in range(0, units, step):
            rows = step * unit
            queries = q_ref[start : start + step, head].reshape(rows, HD)
            time = jnp.concatenate(
                [
                    unit_row + unit_rows * jnp.bitwise_xor(chip, rel[start + n])
                    for n in range(step)
                ],
                axis=0,
            )
            draft_scores = lax.dot_general(
                queries, d_ref[head, :LANES], (((1,), (1,)), ((), ())), preferred_element_type=f32
            )
            draft_scores = jnp.where(draft_row <= time, draft_scores * LOG2_SCALE, DEAD)
            tops, sums = [], []
            for side in range(split):
                k_ref, v_ref = caches[2 * side : 2 * side + 2]
                block = seq if side == 0 else seq + 1 - 2 * core
                score = lax.dot_general(
                    queries, k_ref[:, lanes], (((1,), (1,)), ((), ())), preferred_element_type=f32
                )
                score = jnp.where(key_index + block * keys < length, score * LOG2_SCALE, DEAD)
                inside = (draft >= side * local_rows) & (draft < (side + 1) * local_rows)
                own_drafts = jnp.where(inside, draft_scores, DEAD)
                top = jnp.maximum(
                    jnp.max(score, axis=1, keepdims=True), jnp.max(own_drafts, axis=1, keepdims=True)
                )
                top = jnp.maximum(top, FLOOR)
                tops.append(top)
                values_ones = jnp.concatenate([v_ref[:, lanes], ones], axis=1)
                sums.append(
                    jnp.dot(
                        jnp.exp2(score - top).astype(bf16), values_ones, preferred_element_type=f32
                    )
                    + jnp.dot(
                        jnp.exp2(own_drafts - top).astype(bf16),
                        draft_values,
                        preferred_element_type=f32,
                    )
                )
            shift = functools.reduce(jnp.maximum, tops).astype(bf16).astype(f32)
            both = sum(part * jnp.exp2(top - shift) for part, top in zip(sums, tops))
            weighted, total = both[:, :HD], both[:, HD : HD + 1]
            for n in range(step):
                place = (start + n) * heads + head
                part = slice(n * unit, (n + 1) * unit)
                out_ref[place * unit : (place + 1) * unit, :] = weighted[part].astype(out_ref.dtype)
                columns.append((place, shift[part]))
                columns.append((count8 + place, total[part]))
    stats = columns_to_rows(columns, unit)
    if as_message:
        write_message(out_ref, count * unit, stats[:count8], stats[count8 : 2 * count8])
    else:
        outs[1][...] = stats[: 2 * count8]


def attend(length, q, rel, unit_rows, split, caches, drafts, as_message, after=()):
    units, heads = q.shape[:2]
    unit = unit_rows * GROUP
    keys = caches[0].shape[0]
    count = units * heads
    if as_message:
        out_shape = (jax.ShapeDtypeStruct((count * unit + stat_rows(count), LANES), bf16),)
    else:
        out_shape = (
            jax.ShapeDtypeStruct((count * unit, LANES), f32),
            jax.ShapeDtypeStruct((2 * round_up(count, 8), LANES), f32),
        )
    cache_spec = pl.BlockSpec((keys, heads * HD), lambda i, s: (0, 0))
    other_spec = pl.BlockSpec(
        (keys, heads * HD), lambda i, s: (0, lax.rem(lax.axis_index("seq"), split))
    )
    in_specs = [pl.BlockSpec(q.shape, lambda i, s: (0, 0, 0, 0))]
    in_specs += [cache_spec] * 2 + [other_spec] * (len(caches) - 2)
    in_specs += [pl.BlockSpec(drafts.shape, lambda i, s: (0, 0, 0))]
    in_specs += [pl.BlockSpec(memory_space=pl.ANY)] * len(after)
    scores = count * unit * (split * keys + LANES)
    return pl.pallas_call(
        functools.partial(attend_kernel, rel, unit_rows, split, as_message, len(after)),
        grid_spec=pltpu.PrefetchScalarGridSpec(
            num_scalar_prefetch=1,
            grid=(1,),
            in_specs=in_specs,
            out_specs=tuple(pl.BlockSpec(o.shape, lambda i, s: (0, 0)) for o in out_shape),
        ),
        out_shape=out_shape,
        compiler_params=pltpu.CompilerParams(vmem_limit_bytes=VMEM_BYTES),
        cost_estimate=pl.CostEstimate(
            flops=4 * scores * HD, bytes_accessed=4 * split * keys * heads * HD, transcendentals=scores
        ),
    )(length, q, *caches, drafts, *after)


def merge_kernel(unit, mode, num_ref, stat_ref, msg_ref, *outs):
    rows = num_ref.shape[0]
    count = rows // unit
    count8 = stat_ref.shape[0] // 2
    own_shift, own_total = stat_ref[:count8], stat_ref[count8:]
    sent = msg_ref[rows:, :].astype(f32)
    shift = sent[:count8]
    total = sent[count8 : 2 * count8] + sent[2 * count8 : 3 * count8]
    half = count // 2
    if mode == "final":
        shift = pad_rows(jnp.concatenate([shift[half:count], shift[:half]], axis=0), count8)
        total = pad_rows(jnp.concatenate([total[half:count], total[:half]], axis=0), count8)
    new_shift = jnp.maximum(own_shift, shift)
    own_factor = jnp.exp2(own_shift - new_shift)
    factor = jnp.exp2(shift - new_shift)
    new_total = own_total * own_factor + total * factor
    if mode == "final":
        new_total = jnp.where(new_total > 0, new_total, 1.0)
        own_factor = own_factor / new_total
        factor = factor / new_total
    factors = jnp.transpose(pad_rows(jnp.concatenate([own_factor, factor], axis=0), LANES))
    for n in range(count):
        source = (n + half) % count if mode == "final" else n
        merged = num_ref[n * unit : (n + 1) * unit, :] * factors[:unit, n : n + 1]
        merged = merged + (
            msg_ref[source * unit : (source + 1) * unit, :].astype(f32)
            * factors[:unit, count8 + n : count8 + n + 1]
        )
        here = slice(n * unit, (n + 1) * unit)
        if mode == "final":
            outs[0][here, :] = merged.astype(bf16)
        elif mode == "all":
            outs[0][here, :] = merged
            outs[2][here, :] = merged.astype(bf16)
        elif n < half:
            outs[0][here, :] = merged
        else:
            outs[2][(n - half) * unit : (n - half + 1) * unit, :] = merged.astype(bf16)
    if mode == "all":
        outs[1][...] = jnp.concatenate([new_shift, new_total], axis=0)
        write_message(outs[2], rows, new_shift, new_total)
    elif mode == "half":
        half8 = round_up(half, 8)
        outs[1][...] = jnp.concatenate(
            [pad_rows(new_shift[:half], half8), pad_rows(new_total[:half], half8)], axis=0
        )
        write_message(
            outs[2],
            half * unit,
            pad_rows(new_shift[half:count], half8),
            pad_rows(new_total[half:count], half8),
        )


def merge(unit, mode, num, stats, message):
    rows = num.shape[0]
    if mode == "final":
        out_shape = jax.ShapeDtypeStruct((rows, LANES), bf16)
    else:
        rows = rows // 2 if mode == "half" else rows
        count = rows // unit
        out_shape = (
            jax.ShapeDtypeStruct((rows, LANES), f32),
            jax.ShapeDtypeStruct((2 * round_up(count, 8), LANES), f32),
            jax.ShapeDtypeStruct((rows + stat_rows(count), LANES), bf16),
        )
    return pl.pallas_call(
        functools.partial(merge_kernel, unit, mode),
        out_shape=out_shape,
        compiler_params=pltpu.CompilerParams(vmem_limit_bytes=VMEM_BYTES),
    )(num, stats, message)


def project_kernel(rel, split, n_head, *refs):
    sources = refs[: 2 * split]
    w_ref = refs[2 * split]
    outs = refs[2 * split + 1 : -2]
    rows_ref, lhs_ref = refs[-2:]
    seq, head = lax.axis_index("seq"), lax.axis_index("head")
    chip = lax.div(seq, split)
    core = lax.rem(seq, split)
    heads_kv = rows_ref.shape[0]
    units, heads, unit, _ = sources[0].shape
    chips = 2 * units
    piece = unit // split
    first = head * (chips // n_head) if n_head == 2 else 0
    for side in range(split):
        owner = core if side == 0 else 1 - core
        for part in range(2):
            x_ref = sources[2 * side + part]
            for n in range(units):
                place = lax.rem(jnp.bitwise_xor(chip, rel[part][n]) - first + chips, chips)
                for part_of in range(split):
                    row = place * unit + (owner if part_of == 0 else 1 - owner) * piece
                    for h in range(heads):
                        rows_ref[owner * heads + h, pl.ds(pl.multiple_of(row, 16), piece), :] = (
                            x_ref[n, h, part_of * piece : (part_of + 1) * piece].astype(f32)
                        )
    rows = lhs_ref.shape[0]
    for kv in range(heads_kv):
        for g in range(GROUP):
            lanes = slice((kv * GROUP + g) * HD, (kv * GROUP + g + 1) * HD)
            lhs_ref[:, lanes] = rows_ref[kv, pl.ds(g, rows, stride=GROUP), :].astype(bf16)
    result = jnp.dot(lhs_ref[...], w_ref[...], preferred_element_type=f32)
    if n_head == 2:
        outs[0][...] = result[: rows // 2]
        outs[1][...] = result[rows // 2 :]
    else:
        outs[0][...] = result


def project(rel, split, n_head, sources, weight):
    units, heads, unit, _ = sources[0].shape
    heads_kv = heads * split
    rows = 2 * units * unit // GROUP
    columns = weight.shape[1]
    if n_head == 2:
        out_shape = (jax.ShapeDtypeStruct((rows // 2, columns), f32),) * 2
    else:
        out_shape = (jax.ShapeDtypeStruct((rows, columns), f32),)
    return pl.pallas_call(
        functools.partial(project_kernel, rel, split, n_head),
        in_specs=[pl.BlockSpec(memory_space=pltpu.VMEM)] * (2 * split + 1),
        out_shape=out_shape,
        scratch_shapes=[
            pltpu.VMEM((heads_kv, 2 * units * unit, LANES), f32),
            pltpu.VMEM((rows, heads_kv * GROUP * HD), bf16),
        ],
        compiler_params=pltpu.CompilerParams(vmem_limit_bytes=VMEM_BYTES),
    )(*sources, weight)


def append_kernel(rel, split, unit_rows, len_ref, acc_ref, ck_ref, cv_ref, mine_ref, other_ref, *rest):
    nk_ref, nv_ref = rest[-2:]
    rows, width = ck_ref.shape
    chips, heads, both, _ = mine_ref.shape
    local_rows = unit_rows // split
    seq = lax.axis_index("seq")
    chip, core = lax.div(seq, split), lax.rem(seq, split)
    length, accepted = len_ref[0], acc_ref[0]
    first = (seq * pl.num_programs(0) + pl.program_id(0)) * rows - length
    touched = (first < accepted) & (first + rows > 0)

    @pl.when(jnp.logical_not(touched))
    def _():
        nk_ref[...] = ck_ref[...]
        nv_ref[...] = cv_ref[...]

    @pl.when(touched)
    def _():
        place = first + lax.broadcasted_iota(jnp.int32, (rows, both), 0)
        lane = lax.broadcasted_iota(jnp.int32, (rows, both), 1)
        inside = (place >= 0) & (place < accepted)
        chosen = first + lax.broadcasted_iota(jnp.int32, (rows, HD), 0)
        chosen = (chosen >= 0) & (chosen < accepted)
        for side in range(split):
            drafts = mine_ref if side == 0 else other_ref
            source_core = core if side == 0 else 1 - core
            for cache_ref, new_ref, start in ((ck_ref, nk_ref, 0), (cv_ref, nv_ref, unit_rows)):
                sums = [jnp.zeros((rows, HD), f32)] * heads
                here = (lane >= start) & (lane < start + unit_rows) & inside
                row = row_of(lane - start, local_rows, source_core)
                for n in range(chips):
                    source = jnp.bitwise_xor(chip, rel[n]) * unit_rows + row
                    pick = jnp.where(here & (source == place), 1.0, 0.0).astype(bf16)
                    for h in range(heads):
                        sums[h] = sums[h] + jnp.dot(
                            pick, drafts[n, h], preferred_element_type=f32
                        )
                for h in range(heads):
                    lanes = pl.ds(pl.multiple_of((source_core * heads + h) * HD, HD), HD)
                    new_ref[:, lanes] = jnp.where(
                        chosen, sums[h], cache_ref[:, lanes].astype(f32)
                    ).astype(bf16)


def append(rel, split, unit_rows, length, accepted, ck, cv, drafts, after):
    rows = ck.shape[0]
    block = rows // 4 if rows % 64 == 0 else rows
    cache_spec = pl.BlockSpec((block, ck.shape[1]), lambda i: (i, 0))
    mine, other = drafts[0], drafts[-1]
    draft_spec = pl.BlockSpec(mine.shape, lambda i: (0, 0, 0, 0))
    shape = jax.ShapeDtypeStruct(ck.shape, bf16)
    return pl.pallas_call(
        functools.partial(append_kernel, rel, split, unit_rows),
        grid=(rows // block,),
        in_specs=[pl.BlockSpec(memory_space=pltpu.SMEM)] * 2
        + [cache_spec, cache_spec, draft_spec, draft_spec]
        + [pl.BlockSpec(memory_space=pl.ANY)] * len(after),
        out_specs=(cache_spec, cache_spec),
        out_shape=(shape, shape),
        compiler_params=pltpu.CompilerParams(vmem_limit_bytes=VMEM_BYTES),
        cost_estimate=pl.CostEstimate(flops=0, bytes_accessed=8 * ck.size, transcendentals=0),
    )(length, accepted, ck, cv, mine, other, *after)


def one_request(n_seq, n_head, dq, dk, dv, ck, cv, accepted, length, weight):
    seq = lax.axis_index("seq")
    local_rows = dq.shape[0]
    heads_kv = dk.shape[1] // HD
    split = 2 if heads_kv % 2 == 0 else 1
    heads = heads_kv // split
    unit_rows = local_rows * split
    unit = unit_rows * GROUP
    n_bits = n_seq.bit_length() - 1
    bits = list(range(n_bits - 1, split - 2, -1))

    def swap(x, bit):
        return lax.ppermute(x, "seq", [(i, i ^ (1 << bit)) for i in range(n_seq)])

    core = seq % split

    q4 = dq.reshape(local_rows, heads_kv, GROUP, LANES).transpose(1, 0, 2, 3)
    q4 = q4.reshape(heads_kv, local_rows * GROUP, LANES)
    dk4 = dk.reshape(local_rows, heads_kv, HD).transpose(1, 0, 2)
    dv4 = dv.reshape(local_rows, heads_kv, HD).transpose(1, 0, 2)
    pack = jnp.concatenate([q4, dk4, dv4], axis=1)
    parts, caches = [pack], [ck, cv]
    if split == 2:
        mine = lax.dynamic_slice_in_dim(pack, core * heads, heads, 0)
        parts = [mine, swap(lax.dynamic_slice_in_dim(pack, (1 - core) * heads, heads, 0), 0)]
    cut = local_rows * GROUP
    second = cut + local_rows
    pieces = [p[:, :cut] for p in parts]
    pieces += [p[:, cut : cut + local_rows] for p in parts]
    pieces += [p[:, second : second + local_rows] for p in parts]
    q = jnp.concatenate(pieces, axis=1)
    d_key, d_value = q[:, unit : unit + unit_rows], q[:, unit + unit_rows :]
    spare = ((0, 0), (0, LANES - unit_rows), (0, 0))
    drafts = jnp.concatenate([jnp.pad(d_key, spare), jnp.pad(d_value, spare)], axis=1)
    q = q[None]
    if split == 2:
        q, ck_late, cv_late = lax.optimization_barrier((q, ck, cv))
        caches += [swap(ck_late, 0), swap(cv_late, 0)]

    rel = [0]
    for bit in bits[:-1]:
        q = jnp.concatenate([q, swap(q, bit)], axis=0)
        if split == 2 and bit == bits[0]:
            q, *own = lax.optimization_barrier((q, ck, cv))
            caches[:2] = [
                lax.dynamic_slice_in_dim(c, core * heads * HD, heads * HD, 1) for c in own
            ]
        rel = rel + [r | (1 << bit) // split for r in rel]
    q, dkv = q[:, :, :unit], q[:, :, unit:]
    near = bits[-1]
    rel_far = [r | (1 << near) // split for r in rel]
    q_far = swap(q, near)

    run = functools.partial(attend, length)
    (message,) = run(q, rel, unit_rows, split, caches, drafts, True)
    num, stats = run(q_far, rel_far, unit_rows, split, caches, drafts, False, (message,))
    message = swap(message, near)

    dkv = jnp.concatenate([dkv, swap(dkv, near)], axis=0)

    for bit in reversed(bits[:-1]):
        mode = "all" if bit == bits[0] else "half"
        num, stats, message = merge(unit, mode, num, stats, message)
        message = swap(message, bit)

    att = merge(unit, "final", num, stats, message).reshape(-1, heads, unit, LANES)
    att, dkv = lax.optimization_barrier((att, dkv))
    every = [dkv, swap(dkv, 0)] if split == 2 else [dkv]
    for bit in bits[1:-1]:
        att = jnp.concatenate([att, swap(att, bit)], axis=0)
    att, every = lax.optimization_barrier((att, every))
    att_near = swap(att, near)
    sources = [att, att_near]
    if split == 2:
        sources += [swap(att, 0), swap(att_near, 0)]
    result = project((rel_far, rel), split, n_head, sources, weight)
    if n_head == 2:
        keep, send = result
        projected = keep + lax.ppermute(send, "head", [(0, 1), (1, 0)])
    else:
        projected = lax.psum_scatter(result[0], "head", scatter_dimension=0, tiled=True)
    new_key, new_value = append(
        rel + rel_far, split, unit_rows, length, accepted, ck, cv, every, (result[-1],)
    )
    return projected.astype(bf16), new_key, new_value


def on_device(n_seq, n_head, dq, dk, dv, ck, cv, accepted, cache_len, weight):
    results = [
        one_request(
            n_seq, n_head, dq[r], dk[r], dv[r], ck[r], cv[r], accepted[r : r + 1], cache_len[r : r + 1], weight
        )
        for r in range(dq.shape[0])
    ]
    return tuple(jnp.stack(parts) for parts in zip(*results))


def solution(mesh):
    in_specs = (
        P(None, "seq", "head"),
        P(None, "seq", "head"),
        P(None, "seq", "head"),
        P(None, "seq", "head"),
        P(None, "seq", "head"),
        P(),
        P(),
        P("head", "seq"),
    )
    out_specs = (P(None, "head", "seq"), P(None, "seq", "head"), P(None, "seq", "head"))
    return jax.shard_map(
        functools.partial(on_device, mesh.shape["seq"], mesh.shape["head"]),
        mesh=mesh,
        in_specs=in_specs,
        out_specs=out_specs,
        check_vma=False,
    )
```

```python
import functools
import math

import jax
import jax.numpy as jnp
from jax import lax
from jax.experimental import pallas as pl
from jax.experimental.pallas import tpu as pltpu
from jax.sharding import PartitionSpec as P

QH = 64
KVH = 8
HD = 128
GROUP = QH // KVH
LANES = 128

DEAD = -1e30
FLOOR = -(2.0**96)
LOG2_SCALE = math.log2(math.e) / math.sqrt(HD)
VMEM_BYTES = 48 * 1024 * 1024

bf16 = jnp.bfloat16
f32 = jnp.float32


def round_up(n, m):
    return -(-n // m) * m


def stat_rows(units):
    return round_up(3 * round_up(units, 8), 16)


def pad_rows(x, rows):
    if x.shape[0] == rows:
        return x
    return jnp.concatenate([x, jnp.zeros((rows - x.shape[0], x.shape[1]), x.dtype)], axis=0)


def columns_to_rows(columns, unit):
    lane = lax.broadcasted_iota(jnp.int32, (unit, LANES), 1)
    square = jnp.zeros((unit, LANES), f32)
    for place, column in columns:
        square = jnp.where(lane == place, column, square)
    return jnp.transpose(pad_rows(square, LANES))


def split_total(total):
    high = total.astype(bf16)
    return high, (total - high.astype(f32)).astype(bf16)


def write_message(out_ref, row, shift, total):
    high, low = split_total(total)
    rows = jnp.concatenate([shift, high.astype(f32), low.astype(f32)], axis=0)
    out_ref[row : row + stat_rows(shift.shape[0]), :] = pad_rows(
        rows, stat_rows(shift.shape[0])
    ).astype(bf16)


def row_of(place, local_rows, core):
    return place + jnp.where(place < local_rows, core, -core) * local_rows


def attend_kernel(rel, unit_rows, split, as_message, n_after, scal, q_ref, *rest):
    caches = rest[: 2 * split]
    d_ref = rest[2 * split]
    outs = rest[2 * split + 1 + n_after :]
    units, heads = q_ref.shape[:2]
    unit = unit_rows * GROUP
    keys = caches[0].shape[0]
    seq, length = lax.axis_index("seq"), scal[0:1, 0:1]
    chip = lax.div(seq, split)
    count = units * heads
    count8 = round_up(count, 8)
    step = max(n for n in range(1, units + 1) if units % n == 0 and n * unit <= 384)
    columns = []
    out_ref = outs[0]
    key_index = lax.broadcasted_iota(jnp.int32, (1, keys), 1)
    core = lax.rem(seq, split)
    local_rows = unit_rows // split
    ones = jnp.ones((keys, LANES), bf16)
    draft = lax.broadcasted_iota(jnp.int32, (1, LANES), 1)
    draft_row = unit_rows * chip + row_of(draft, local_rows, core)
    unit_row = row_of(
        lax.shift_right_logical(lax.broadcasted_iota(jnp.int32, (unit, LANES), 0), 3),
        local_rows,
        core,
    )
    for head in range(heads):
        lanes = slice(head * HD, (head + 1) * HD)
        draft_values = jnp.concatenate([d_ref[head, LANES:], ones[:LANES]], axis=1)
        for start in range(0, units, step):
            rows = step * unit
            queries = q_ref[start : start + step, head].reshape(rows, HD)
            time = jnp.concatenate(
                [
                    unit_row + unit_rows * jnp.bitwise_xor(chip, rel[start + n])
                    for n in range(step)
                ],
                axis=0,
            )
            draft_scores = lax.dot_general(
                queries, d_ref[head, :LANES], (((1,), (1,)), ((), ())), preferred_element_type=f32
            )
            draft_scores = jnp.where(draft_row <= time, draft_scores * LOG2_SCALE, DEAD)
            tops, sums = [], []
            for side in range(split):
                k_ref, v_ref = caches[2 * side : 2 * side + 2]
                block = seq if side == 0 else seq + 1 - 2 * core
                score = lax.dot_general(
                    queries, k_ref[:, lanes], (((1,), (1,)), ((), ())), preferred_element_type=f32
                )
                score = jnp.where(key_index + block * keys < length, score * LOG2_SCALE, DEAD)
                inside = (draft >= side * local_rows) & (draft < (side + 1) * local_rows)
                own_drafts = jnp.where(inside, draft_scores, DEAD)
                top = jnp.maximum(
                    jnp.max(score, axis=1, keepdims=True), jnp.max(own_drafts, axis=1, keepdims=True)
                )
                top = jnp.maximum(top, FLOOR)
                tops.append(top)
                values_ones = jnp.concatenate([v_ref[:, lanes], ones], axis=1)
                sums.append(
                    jnp.dot(
                        jnp.exp2(score - top).astype(bf16), values_ones, preferred_element_type=f32
                    )
                    + jnp.dot(
                        jnp.exp2(own_drafts - top).astype(bf16),
                        draft_values,
                        preferred_element_type=f32,
                    )
                )
            shift = functools.reduce(jnp.maximum, tops).astype(bf16).astype(f32)
            both = sum(part * jnp.exp2(top - shift) for part, top in zip(sums, tops))
            weighted, total = both[:, :HD], both[:, HD : HD + 1]
            for n in range(step):
                place = (start + n) * heads + head
                part = slice(n * unit, (n + 1) * unit)
                out_ref[place * unit : (place + 1) * unit, :] = weighted[part].astype(out_ref.dtype)
                columns.append((place, shift[part]))
                columns.append((count8 + place, total[part]))
    stats = columns_to_rows(columns, unit)
    if as_message:
        write_message(out_ref, count * unit, stats[:count8], stats[count8 : 2 * count8])
    else:
        outs[1][...] = stats[: 2 * count8]


def attend(scal, q, rel, unit_rows, split, caches, drafts, as_message, after=()):
    units, heads = q.shape[:2]
    unit = unit_rows * GROUP
    keys = caches[0].shape[0]
    count = units * heads
    if as_message:
        out_shape = (jax.ShapeDtypeStruct((count * unit + stat_rows(count), LANES), bf16),)
    else:
        out_shape = (
            jax.ShapeDtypeStruct((count * unit, LANES), f32),
            jax.ShapeDtypeStruct((2 * round_up(count, 8), LANES), f32),
        )
    whole = pl.BlockSpec(memory_space=pltpu.VMEM)
    cache_spec = pl.BlockSpec((keys, heads * HD), lambda i: (0, 0))
    other_spec = pl.BlockSpec(
        (keys, heads * HD), lambda i: (0, lax.rem(lax.axis_index("seq"), split))
    )
    in_specs = [whole, pl.BlockSpec(q.shape, lambda i: (0, 0, 0, 0))]
    in_specs += [cache_spec] * 2 + [other_spec] * (len(caches) - 2)
    in_specs += [pl.BlockSpec(drafts.shape, lambda i: (0, 0, 0))]
    in_specs += [pl.BlockSpec(memory_space=pl.ANY)] * len(after)
    scores = count * unit * (split * keys + LANES)
    return pl.pallas_call(
        functools.partial(attend_kernel, rel, unit_rows, split, as_message, len(after)),
        grid=(1,),
        in_specs=in_specs,
        out_specs=tuple(pl.BlockSpec(o.shape, lambda i: (0, 0)) for o in out_shape),
        out_shape=out_shape,
        compiler_params=pltpu.CompilerParams(vmem_limit_bytes=VMEM_BYTES),
        cost_estimate=pl.CostEstimate(
            flops=4 * scores * HD, bytes_accessed=4 * split * keys * heads * HD, transcendentals=scores
        ),
    )(scal, q, *caches, drafts, *after)


def merge_kernel(unit, mode, num_ref, stat_ref, msg_ref, *outs):
    rows = num_ref.shape[0]
    count = rows // unit
    count8 = stat_ref.shape[0] // 2
    own_shift, own_total = stat_ref[:count8], stat_ref[count8:]
    sent = msg_ref[rows:, :].astype(f32)
    shift = sent[:count8]
    total = sent[count8 : 2 * count8] + sent[2 * count8 : 3 * count8]
    half = count // 2
    if mode == "final":
        shift = pad_rows(jnp.concatenate([shift[half:count], shift[:half]], axis=0), count8)
        total = pad_rows(jnp.concatenate([total[half:count], total[:half]], axis=0), count8)
    new_shift = jnp.maximum(own_shift, shift)
    own_factor = jnp.exp2(own_shift - new_shift)
    factor = jnp.exp2(shift - new_shift)
    new_total = own_total * own_factor + total * factor
    if mode == "final":
        new_total = jnp.where(new_total > 0, new_total, 1.0)
        own_factor = own_factor / new_total
        factor = factor / new_total
    factors = jnp.transpose(pad_rows(jnp.concatenate([own_factor, factor], axis=0), LANES))
    for n in range(count):
        source = (n + half) % count if mode == "final" else n
        merged = num_ref[n * unit : (n + 1) * unit, :] * factors[:unit, n : n + 1]
        merged = merged + (
            msg_ref[source * unit : (source + 1) * unit, :].astype(f32)
            * factors[:unit, count8 + n : count8 + n + 1]
        )
        here = slice(n * unit, (n + 1) * unit)
        if mode == "final":
            outs[0][here, :] = merged.astype(bf16)
        elif mode == "all":
            outs[0][here, :] = merged
            outs[2][here, :] = merged.astype(bf16)
        elif n < half:
            outs[0][here, :] = merged
        else:
            outs[2][(n - half) * unit : (n - half + 1) * unit, :] = merged.astype(bf16)
    if mode == "all":
        outs[1][...] = jnp.concatenate([new_shift, new_total], axis=0)
        write_message(outs[2], rows, new_shift, new_total)
    elif mode == "half":
        half8 = round_up(half, 8)
        outs[1][...] = jnp.concatenate(
            [pad_rows(new_shift[:half], half8), pad_rows(new_total[:half], half8)], axis=0
        )
        write_message(
            outs[2],
            half * unit,
            pad_rows(new_shift[half:count], half8),
            pad_rows(new_total[half:count], half8),
        )


def merge(unit, mode, num, stats, message):
    rows = num.shape[0]
    if mode == "final":
        out_shape = jax.ShapeDtypeStruct((rows, LANES), bf16)
    else:
        rows = rows // 2 if mode == "half" else rows
        count = rows // unit
        out_shape = (
            jax.ShapeDtypeStruct((rows, LANES), f32),
            jax.ShapeDtypeStruct((2 * round_up(count, 8), LANES), f32),
            jax.ShapeDtypeStruct((rows + stat_rows(count), LANES), bf16),
        )
    return pl.pallas_call(
        functools.partial(merge_kernel, unit, mode),
        out_shape=out_shape,
        compiler_params=pltpu.CompilerParams(vmem_limit_bytes=VMEM_BYTES),
    )(num, stats, message)


def project_kernel(rel, split, n_head, *refs):
    sources = refs[: 2 * split]
    w_ref = refs[2 * split]
    outs = refs[2 * split + 1 : -2]
    rows_ref, lhs_ref = refs[-2:]
    seq, head = lax.axis_index("seq"), lax.axis_index("head")
    chip = lax.div(seq, split)
    core = lax.rem(seq, split)
    heads_kv = rows_ref.shape[0]
    units, heads, unit, _ = sources[0].shape
    chips = 2 * units
    piece = unit // split
    first = head * (chips // n_head) if n_head == 2 else 0
    for side in range(split):
        owner = core if side == 0 else 1 - core
        for part in range(2):
            x_ref = sources[2 * side + part]
            for n in range(units):
                place = lax.rem(jnp.bitwise_xor(chip, rel[part][n]) - first + chips, chips)
                for part_of in range(split):
                    row = place * unit + (owner if part_of == 0 else 1 - owner) * piece
                    for h in range(heads):
                        rows_ref[owner * heads + h, pl.ds(pl.multiple_of(row, 16), piece), :] = (
                            x_ref[n, h, part_of * piece : (part_of + 1) * piece].astype(f32)
                        )
    rows = lhs_ref.shape[0]
    for kv in range(heads_kv):
        for g in range(GROUP):
            lanes = slice((kv * GROUP + g) * HD, (kv * GROUP + g + 1) * HD)
            lhs_ref[:, lanes] = rows_ref[kv, pl.ds(g, rows, stride=GROUP), :].astype(bf16)
    result = jnp.dot(lhs_ref[...], w_ref[...], preferred_element_type=f32)
    if n_head == 2:
        outs[0][...] = result[: rows // 2]
        outs[1][...] = result[rows // 2 :].astype(bf16)
    else:
        outs[0][...] = result


def project(rel, split, n_head, sources, weight):
    units, heads, unit, _ = sources[0].shape
    heads_kv = heads * split
    rows = 2 * units * unit // GROUP
    columns = weight.shape[1]
    if n_head == 2:
        out_shape = tuple(jax.ShapeDtypeStruct((rows // 2, columns), t) for t in (f32, bf16))
    else:
        out_shape = (jax.ShapeDtypeStruct((rows, columns), f32),)
    return pl.pallas_call(
        functools.partial(project_kernel, rel, split, n_head),
        in_specs=[pl.BlockSpec(memory_space=pltpu.VMEM)] * (2 * split + 1),
        out_shape=out_shape,
        scratch_shapes=[
            pltpu.VMEM((heads_kv, 2 * units * unit, LANES), f32),
            pltpu.VMEM((rows, heads_kv * GROUP * HD), bf16),
        ],
        compiler_params=pltpu.CompilerParams(vmem_limit_bytes=VMEM_BYTES),
    )(*sources, weight)


def append_kernel(rel, split, unit_rows, scal, ck_ref, cv_ref, mine_ref, other_ref, *rest):
    nk_ref, nv_ref = rest[-2:]
    rows, width = ck_ref.shape
    chips, heads, both, _ = mine_ref.shape
    local_rows = unit_rows // split
    seq = lax.axis_index("seq")
    chip, core = lax.div(seq, split), lax.rem(seq, split)
    length, accepted = jnp.max(scal[0:1]), jnp.max(scal[1:2])
    first = (seq * pl.num_programs(0) + pl.program_id(0)) * rows - length
    touched = (first < accepted) & (first + rows > 0)

    @pl.when(jnp.logical_not(touched))
    def _():
        nk_ref[...] = ck_ref[...]
        nv_ref[...] = cv_ref[...]

    @pl.when(touched)
    def _():
        place = first + lax.broadcasted_iota(jnp.int32, (rows, both), 0)
        lane = lax.broadcasted_iota(jnp.int32, (rows, both), 1)
        inside = (place >= 0) & (place < accepted)
        chosen = first + lax.broadcasted_iota(jnp.int32, (rows, HD), 0)
        chosen = (chosen >= 0) & (chosen < accepted)
        for side in range(split):
            drafts = mine_ref if side == 0 else other_ref
            source_core = core if side == 0 else 1 - core
            for cache_ref, new_ref, start in ((ck_ref, nk_ref, 0), (cv_ref, nv_ref, unit_rows)):
                sums = [jnp.zeros((rows, HD), f32)] * heads
                here = (lane >= start) & (lane < start + unit_rows) & inside
                row = row_of(lane - start, local_rows, source_core)
                for n in range(chips):
                    source = jnp.bitwise_xor(chip, rel[n]) * unit_rows + row
                    pick = jnp.where(here & (source == place), 1.0, 0.0).astype(bf16)
                    for h in range(heads):
                        sums[h] = sums[h] + jnp.dot(
                            pick, drafts[n, h], preferred_element_type=f32
                        )
                for h in range(heads):
                    lanes = pl.ds(pl.multiple_of((source_core * heads + h) * HD, HD), HD)
                    new_ref[:, lanes] = jnp.where(
                        chosen, sums[h], cache_ref[:, lanes].astype(f32)
                    ).astype(bf16)


def append(rel, split, unit_rows, scal, ck, cv, drafts, after):
    rows = ck.shape[0]
    block = rows // 4 if rows % 64 == 0 else rows
    cache_spec = pl.BlockSpec((block, ck.shape[1]), lambda i: (i, 0))
    mine, other = drafts[0], drafts[-1]
    draft_spec = pl.BlockSpec(mine.shape, lambda i: (0, 0, 0, 0))
    shape = jax.ShapeDtypeStruct(ck.shape, bf16)
    return pl.pallas_call(
        functools.partial(append_kernel, rel, split, unit_rows),
        grid=(rows // block,),
        in_specs=[pl.BlockSpec(memory_space=pltpu.VMEM)]
        + [cache_spec, cache_spec, draft_spec, draft_spec]
        + [pl.BlockSpec(memory_space=pl.ANY)] * len(after),
        out_specs=(cache_spec, cache_spec),
        out_shape=(shape, shape),
        compiler_params=pltpu.CompilerParams(vmem_limit_bytes=VMEM_BYTES),
        cost_estimate=pl.CostEstimate(flops=0, bytes_accessed=8 * ck.size, transcendentals=0),
    )(scal, ck, cv, mine, other, *after)


def one_request(n_seq, n_head, dq, dk, dv, ck, cv, accepted, length, weight):
    seq = lax.axis_index("seq")
    local_rows = dq.shape[0]
    heads_kv = dk.shape[1] // HD
    split = 2 if heads_kv % 2 == 0 else 1
    heads = heads_kv // split
    unit_rows = local_rows * split
    unit = unit_rows * GROUP
    n_bits = n_seq.bit_length() - 1
    bits = list(range(n_bits - 1, split - 2, -1))

    def swap(x, bit):
        return lax.ppermute(x, "seq", [(i, i ^ (1 << bit)) for i in range(n_seq)])

    core = seq % split

    q4 = dq.reshape(local_rows, heads_kv, GROUP, LANES).transpose(1, 0, 2, 3)
    q4 = q4.reshape(heads_kv, local_rows * GROUP, LANES)
    dk4 = dk.reshape(local_rows, heads_kv, HD).transpose(1, 0, 2)
    dv4 = dv.reshape(local_rows, heads_kv, HD).transpose(1, 0, 2)
    pack = jnp.concatenate([q4, dk4, dv4], axis=1)
    parts, caches = [pack], [ck, cv]
    if split == 2:
        mine = lax.dynamic_slice_in_dim(pack, core * heads, heads, 0)
        parts = [mine, swap(lax.dynamic_slice_in_dim(pack, (1 - core) * heads, heads, 0), 0)]
    cut = local_rows * GROUP
    second = cut + local_rows
    pieces = [p[:, :cut] for p in parts]
    pieces += [p[:, cut : cut + local_rows] for p in parts]
    pieces += [p[:, second : second + local_rows] for p in parts]
    q = jnp.concatenate(pieces, axis=1)
    d_key, d_value = q[:, unit : unit + unit_rows], q[:, unit + unit_rows :]
    spare = ((0, 0), (0, LANES - unit_rows), (0, 0))
    drafts = jnp.concatenate([jnp.pad(d_key, spare), jnp.pad(d_value, spare)], axis=1)
    q, scal = lax.optimization_barrier(
        (q[None], jnp.broadcast_to(jnp.stack([length, accepted]), (2, LANES)))
    )
    if split == 2:
        q, ck_late, cv_late = lax.optimization_barrier((q, ck, cv))
        caches += [swap(ck_late, 0), swap(cv_late, 0)]

    rel, near = [0], bits[-1]
    for bit in bits[:-1]:
        new = swap(q, bit)
        q = jnp.concatenate([q, new], axis=0)
        if split == 2 and bit == bits[0]:
            q, *own = lax.optimization_barrier((q, ck, cv))
            caches[:2] = [
                lax.dynamic_slice_in_dim(c, core * heads * HD, heads * HD, 1) for c in own
            ]
        rel = rel + [r | (1 << bit) // split for r in rel]
    q, dkv = q[:, :, :unit], q[:, :, unit:]
    rel_far = [r | (1 << near) // split for r in rel]
    q_far = swap(q, near)

    run = functools.partial(attend, scal)
    (message,) = run(q, rel, unit_rows, split, caches, drafts, True)
    num, stats = run(q_far, rel_far, unit_rows, split, caches, drafts, False, (message,))
    message = swap(message, near)

    dkv = jnp.concatenate([dkv, swap(dkv, near)], axis=0)

    for bit in reversed(bits[:-1]):
        mode = "all" if bit == bits[0] else "half"
        num, stats, message = merge(unit, mode, num, stats, message)
        message = swap(message, bit)

    att = merge(unit, "final", num, stats, message).reshape(-1, heads, unit, LANES)
    att, dkv = lax.optimization_barrier((att, dkv))
    every = [dkv, swap(dkv, 0)] if split == 2 else [dkv]
    for bit in bits[1:-1]:
        att = jnp.concatenate([att, swap(att, bit)], axis=0)
    att, every = lax.optimization_barrier((att, every))
    att_near = swap(att, near)
    sources = [att, att_near]
    if split == 2:
        sources += [swap(att, 0), swap(att_near, 0)]
    result = project((rel_far, rel), split, n_head, sources, weight)
    if n_head == 2:
        keep, send = result
        projected = keep + lax.ppermute(send, "head", [(0, 1), (1, 0)]).astype(f32)
    else:
        projected = lax.psum_scatter(result[0], "head", scatter_dimension=0, tiled=True)
    new_key, new_value = append(
        rel + rel_far, split, unit_rows, scal, ck, cv, every, (result[-1],)
    )
    return projected.astype(bf16), new_key, new_value


def on_device(n_seq, n_head, dq, dk, dv, ck, cv, accepted, cache_len, weight):
    results = [
        one_request(
            n_seq, n_head, dq[r], dk[r], dv[r], ck[r], cv[r], accepted[r : r + 1], cache_len[r : r + 1], weight
        )
        for r in range(dq.shape[0])
    ]
    return tuple(jnp.stack(parts) for parts in zip(*results))


def solution(mesh):
    in_specs = (
        P(None, "seq", "head"),
        P(None, "seq", "head"),
        P(None, "seq", "head"),
        P(None, "seq", "head"),
        P(None, "seq", "head"),
        P(),
        P(),
        P("head", "seq"),
    )
    out_specs = (P(None, "head", "seq"), P(None, "seq", "head"), P(None, "seq", "head"))
    return jax.shard_map(
        functools.partial(on_device, mesh.shape["seq"], mesh.shape["head"]),
        mesh=mesh,
        in_specs=in_specs,
        out_specs=out_specs,
        check_vma=False,
    )
```

```python
import functools
import math

import jax
import jax.numpy as jnp
from jax import lax
from jax.experimental import pallas as pl
from jax.experimental.pallas import tpu as pltpu
from jax.sharding import PartitionSpec as P

QH = 64
KVH = 8
HD = 128
GROUP = QH // KVH
LANES = 128

DEAD = -1e30
FLOOR = -(2.0**96)
LOG2_SCALE = math.log2(math.e) / math.sqrt(HD)
VMEM_BYTES = 48 * 1024 * 1024

bf16 = jnp.bfloat16
f32 = jnp.float32


def round_up(n, m):
    return -(-n // m) * m


def stat_rows(units):
    return round_up(3 * round_up(units, 8), 16)


def pad_rows(x, rows):
    if x.shape[0] == rows:
        return x
    return jnp.concatenate([x, jnp.zeros((rows - x.shape[0], x.shape[1]), x.dtype)], axis=0)


def columns_to_rows(columns, unit):
    lane = lax.broadcasted_iota(jnp.int32, (unit, LANES), 1)
    square = jnp.zeros((unit, LANES), f32)
    for place, column in columns:
        square = jnp.where(lane == place, column, square)
    return jnp.transpose(pad_rows(square, LANES))


def split_total(total):
    high = total.astype(bf16)
    return high, (total - high.astype(f32)).astype(bf16)


def write_message(out_ref, row, shift, total):
    high, low = split_total(total)
    rows = jnp.concatenate([shift, high.astype(f32), low.astype(f32)], axis=0)
    out_ref[row : row + stat_rows(shift.shape[0]), :] = pad_rows(
        rows, stat_rows(shift.shape[0])
    ).astype(bf16)


def row_of(place, local_rows, core):
    return place + jnp.where(place < local_rows, core, -core) * local_rows


def attend_kernel(rel, unit_rows, split, as_message, n_after, scal, q_ref, *rest):
    caches = rest[: 2 * split]
    d_ref = rest[2 * split]
    outs = rest[2 * split + 1 + n_after :]
    units, heads = q_ref.shape[:2]
    unit = unit_rows * GROUP
    keys = caches[0].shape[0]
    seq, length = lax.axis_index("seq"), scal[0:1, 0:1]
    chip = lax.div(seq, split)
    count = units * heads
    count8 = round_up(count, 8)
    step = max(n for n in range(1, units + 1) if units % n == 0 and n * unit <= 384)
    columns = []
    out_ref = outs[0]
    key_index = lax.broadcasted_iota(jnp.int32, (1, keys), 1)
    core = lax.rem(seq, split)
    local_rows = unit_rows // split
    ones = jnp.ones((keys, LANES), bf16)
    draft = lax.broadcasted_iota(jnp.int32, (1, LANES), 1)
    draft_row = unit_rows * chip + row_of(draft, local_rows, core)
    unit_row = row_of(
        lax.shift_right_logical(lax.broadcasted_iota(jnp.int32, (unit, LANES), 0), 3),
        local_rows,
        core,
    )
    def lanes_of(head, side):
        if side == 0:
            return slice(head * HD, (head + 1) * HD)
        return pl.ds(pl.multiple_of((core * heads + head) * HD, HD), HD)

    def score_of(chunk):
        head, start, side = chunk
        queries = q_ref[start : start + step, head].reshape(step * unit, HD)
        return lax.dot_general(
            queries, caches[2 * side][:, lanes_of(head, side)], (((1,), (1,)), ((), ())), preferred_element_type=f32
        )

    chunks = [
        (head, start, side)
        for head in range(heads)
        for start in range(0, units, step)
        for side in range(split)
    ]
    tops, sums = [], []
    following = score_of(chunks[0])
    for at, (head, start, side) in enumerate(chunks):
        raw = following
        if at + 1 < len(chunks):
            following = score_of(chunks[at + 1])
        draft_values = jnp.concatenate([d_ref[head, LANES:], ones[:LANES]], axis=1)
        if side == 0:
            time = jnp.concatenate(
                [
                    unit_row + unit_rows * jnp.bitwise_xor(chip, rel[start + n])
                    for n in range(step)
                ],
                axis=0,
            )
            draft_scores = lax.dot_general(
                q_ref[start : start + step, head].reshape(step * unit, HD),
                d_ref[head, :LANES],
                (((1,), (1,)), ((), ())),
                preferred_element_type=f32,
            )
            draft_scores = jnp.where(draft_row <= time, draft_scores * LOG2_SCALE, DEAD)
        block = seq if side == 0 else seq + 1 - 2 * core
        score = jnp.where(key_index + block * keys < length, raw * LOG2_SCALE, DEAD)
        inside = (draft >= side * local_rows) & (draft < (side + 1) * local_rows)
        own_drafts = jnp.where(inside, draft_scores, DEAD)
        top = jnp.maximum(
            jnp.max(score, axis=1, keepdims=True), jnp.max(own_drafts, axis=1, keepdims=True)
        )
        top = jnp.maximum(top, FLOOR)
        tops.append(top)
        values_ones = jnp.concatenate(
            [caches[2 * side + 1][:, lanes_of(head, side)], ones], axis=1
        )
        sums.append(
            jnp.dot(jnp.exp2(score - top).astype(bf16), values_ones, preferred_element_type=f32)
            + jnp.dot(
                jnp.exp2(own_drafts - top).astype(bf16), draft_values, preferred_element_type=f32
            )
        )
        if side + 1 < split:
            continue
        shift = functools.reduce(jnp.maximum, tops).astype(bf16).astype(f32)
        both = sum(part * jnp.exp2(top - shift) for part, top in zip(sums, tops))
        weighted, total = both[:, :HD], both[:, HD : HD + 1]
        for n in range(step):
            place = (start + n) * heads + head
            part = slice(n * unit, (n + 1) * unit)
            out_ref[place * unit : (place + 1) * unit, :] = weighted[part].astype(out_ref.dtype)
            columns.append((place, shift[part]))
            columns.append((count8 + place, total[part]))
        tops, sums = [], []
    stats = columns_to_rows(columns, unit)
    if as_message:
        write_message(out_ref, count * unit, stats[:count8], stats[count8 : 2 * count8])
    else:
        outs[1][...] = stats[: 2 * count8]


def attend(scal, q, rel, unit_rows, split, caches, drafts, as_message, after=()):
    units, heads = q.shape[:2]
    unit = unit_rows * GROUP
    keys = caches[0].shape[0]
    count = units * heads
    if as_message:
        out_shape = (jax.ShapeDtypeStruct((count * unit + stat_rows(count), LANES), bf16),)
    else:
        out_shape = (
            jax.ShapeDtypeStruct((count * unit, LANES), f32),
            jax.ShapeDtypeStruct((2 * round_up(count, 8), LANES), f32),
        )
    whole = pl.BlockSpec(memory_space=pltpu.VMEM)
    in_specs = [whole] * (3 + len(caches))
    in_specs += [pl.BlockSpec(memory_space=pl.ANY)] * len(after)
    scores = count * unit * (split * keys + LANES)
    return pl.pallas_call(
        functools.partial(attend_kernel, rel, unit_rows, split, as_message, len(after)),
        in_specs=in_specs,
        out_specs=(whole,) * len(out_shape),
        out_shape=out_shape,
        compiler_params=pltpu.CompilerParams(vmem_limit_bytes=VMEM_BYTES),
        cost_estimate=pl.CostEstimate(
            flops=4 * scores * HD, bytes_accessed=4 * split * keys * heads * HD, transcendentals=scores
        ),
    )(scal, q, *caches, drafts, *after)


def merge_kernel(unit, mode, num_ref, stat_ref, msg_ref, *outs):
    rows = num_ref.shape[0]
    count = rows // unit
    count8 = stat_ref.shape[0] // 2
    own_shift, own_total = stat_ref[:count8], stat_ref[count8:]
    sent = msg_ref[rows:, :].astype(f32)
    shift = sent[:count8]
    total = sent[count8 : 2 * count8] + sent[2 * count8 : 3 * count8]
    half = count // 2
    if mode == "final":
        shift = pad_rows(jnp.concatenate([shift[half:count], shift[:half]], axis=0), count8)
        total = pad_rows(jnp.concatenate([total[half:count], total[:half]], axis=0), count8)
    new_shift = jnp.maximum(own_shift, shift)
    own_factor = jnp.exp2(own_shift - new_shift)
    factor = jnp.exp2(shift - new_shift)
    new_total = own_total * own_factor + total * factor
    if mode == "final":
        new_total = jnp.where(new_total > 0, new_total, 1.0)
        own_factor = own_factor / new_total
        factor = factor / new_total
    factors = jnp.transpose(pad_rows(jnp.concatenate([own_factor, factor], axis=0), LANES))
    for n in range(count):
        source = (n + half) % count if mode == "final" else n
        merged = num_ref[n * unit : (n + 1) * unit, :] * factors[:unit, n : n + 1]
        merged = merged + (
            msg_ref[source * unit : (source + 1) * unit, :].astype(f32)
            * factors[:unit, count8 + n : count8 + n + 1]
        )
        here = slice(n * unit, (n + 1) * unit)
        if mode == "final":
            outs[0][here, :] = merged.astype(bf16)
        elif mode == "all":
            outs[0][here, :] = merged
            outs[2][here, :] = merged.astype(bf16)
        elif n < half:
            outs[0][here, :] = merged
        else:
            outs[2][(n - half) * unit : (n - half + 1) * unit, :] = merged.astype(bf16)
    if mode == "all":
        outs[1][...] = jnp.concatenate([new_shift, new_total], axis=0)
        write_message(outs[2], rows, new_shift, new_total)
    elif mode == "half":
        half8 = round_up(half, 8)
        outs[1][...] = jnp.concatenate(
            [pad_rows(new_shift[:half], half8), pad_rows(new_total[:half], half8)], axis=0
        )
        write_message(
            outs[2],
            half * unit,
            pad_rows(new_shift[half:count], half8),
            pad_rows(new_total[half:count], half8),
        )


def merge(unit, mode, num, stats, message):
    rows = num.shape[0]
    if mode == "final":
        out_shape = jax.ShapeDtypeStruct((rows, LANES), bf16)
    else:
        rows = rows // 2 if mode == "half" else rows
        count = rows // unit
        out_shape = (
            jax.ShapeDtypeStruct((rows, LANES), f32),
            jax.ShapeDtypeStruct((2 * round_up(count, 8), LANES), f32),
            jax.ShapeDtypeStruct((rows + stat_rows(count), LANES), bf16),
        )
    return pl.pallas_call(
        functools.partial(merge_kernel, unit, mode),
        out_shape=out_shape,
        compiler_params=pltpu.CompilerParams(vmem_limit_bytes=VMEM_BYTES),
    )(num, stats, message)


def project_kernel(rel, split, n_head, parts, n_partial, *refs):
    sources, w_ref = refs[: len(parts)], refs[len(parts)]
    partial = refs[len(parts) + 1 : len(parts) + 1 + n_partial]
    outs, (rows_ref, lhs_ref) = refs[len(parts) + 1 + n_partial : -2], refs[-2:]
    seq, head = lax.axis_index("seq"), lax.axis_index("head")
    chip = lax.div(seq, split)
    core = lax.rem(seq, split)
    units, heads, unit, _ = sources[0].shape
    chips = 2 * units
    piece = unit // split
    first = head * (chips // n_head) if n_head == 2 else 0
    slots = rows_ref.shape[0] // heads
    if len(parts) < 2 * slots:
        rows_ref[...] = jnp.zeros_like(rows_ref)
    for (side, part), x_ref in zip(parts, sources):
        owner = core if side == 0 else 1 - core
        slot = owner if slots == split else 0
        for n in range(units):
            place = lax.rem(jnp.bitwise_xor(chip, rel[part][n]) - first + chips, chips)
            for part_of in range(split):
                row = place * unit + (owner if part_of == 0 else 1 - owner) * piece
                for h in range(heads):
                    rows_ref[slot * heads + h, pl.ds(pl.multiple_of(row, 16), piece), :] = x_ref[
                        n, h, part_of * piece : (part_of + 1) * piece
                    ].astype(f32)
    rows, depth = lhs_ref.shape
    for kv in range(rows_ref.shape[0]):
        for g in range(GROUP):
            lanes = slice((kv * GROUP + g) * HD, (kv * GROUP + g + 1) * HD)
            lhs_ref[:, lanes] = rows_ref[kv, pl.ds(g, rows, stride=GROUP), :].astype(bf16)
    if slots == split:
        weight = w_ref[...]
    else:
        weight = w_ref[pl.ds(pl.multiple_of((1 - core) * depth, LANES), depth), :]
    result = jnp.dot(lhs_ref[...], weight, preferred_element_type=f32)
    for ref in partial:
        result = result + ref[...]
    if len(outs) == 2:
        outs[0][...] = result[: rows // 2]
        outs[1][...] = result[rows // 2 :].astype(bf16)
    else:
        outs[0][...] = result


def project(rel, split, n_head, parts, sources, weight, partial=(), whole=False):
    units, heads, unit, _ = sources[0].shape
    slots = 1 if partial else split
    rows = 2 * units * unit // GROUP
    columns = weight.shape[1]
    if n_head == 2 and whole:
        out_shape = tuple(jax.ShapeDtypeStruct((rows // 2, columns), t) for t in (f32, bf16))
    else:
        out_shape = (jax.ShapeDtypeStruct((rows, columns), f32),)
    return pl.pallas_call(
        functools.partial(project_kernel, rel, split, n_head, parts, len(partial)),
        in_specs=[pl.BlockSpec(memory_space=pltpu.VMEM)] * (len(sources) + 1 + len(partial)),
        out_shape=out_shape,
        scratch_shapes=[
            pltpu.VMEM((heads * slots, 2 * units * unit, LANES), f32),
            pltpu.VMEM((rows, heads * slots * GROUP * HD), bf16),
        ],
        compiler_params=pltpu.CompilerParams(vmem_limit_bytes=VMEM_BYTES),
        cost_estimate=pl.CostEstimate(
            flops=2 * rows * columns * heads * slots * GROUP * HD,
            bytes_accessed=2 * columns * heads * slots * GROUP * HD,
            transcendentals=0,
        ),
    )(*sources, weight, *partial)


def append_kernel(rel, split, unit_rows, scal, ck_ref, cv_ref, mine_ref, other_ref, *rest):
    nk_ref, nv_ref = rest[-2:]
    rows, width = ck_ref.shape
    chips, heads, both, _ = mine_ref.shape
    local_rows = unit_rows // split
    seq = lax.axis_index("seq")
    chip, core = lax.div(seq, split), lax.rem(seq, split)
    length, accepted = jnp.max(scal[0:1]), jnp.max(scal[1:2])
    first = (seq * pl.num_programs(0) + pl.program_id(0)) * rows - length
    touched = (first < accepted) & (first + rows > 0)

    @pl.when(jnp.logical_not(touched))
    def _():
        nk_ref[...] = ck_ref[...]
        nv_ref[...] = cv_ref[...]

    @pl.when(touched)
    def _():
        place = first + lax.broadcasted_iota(jnp.int32, (rows, both), 0)
        lane = lax.broadcasted_iota(jnp.int32, (rows, both), 1)
        inside = (place >= 0) & (place < accepted)
        chosen = first + lax.broadcasted_iota(jnp.int32, (rows, HD), 0)
        chosen = (chosen >= 0) & (chosen < accepted)
        for side in range(split):
            drafts = mine_ref if side == 0 else other_ref
            source_core = core if side == 0 else 1 - core
            for cache_ref, new_ref, start in ((ck_ref, nk_ref, 0), (cv_ref, nv_ref, unit_rows)):
                sums = [jnp.zeros((rows, HD), f32)] * heads
                here = (lane >= start) & (lane < start + unit_rows) & inside
                row = row_of(lane - start, local_rows, source_core)
                for n in range(chips):
                    source = jnp.bitwise_xor(chip, rel[n]) * unit_rows + row
                    pick = jnp.where(here & (source == place), 1.0, 0.0).astype(bf16)
                    for h in range(heads):
                        sums[h] = sums[h] + jnp.dot(
                            pick, drafts[n, h], preferred_element_type=f32
                        )
                for h in range(heads):
                    lanes = pl.ds(pl.multiple_of((source_core * heads + h) * HD, HD), HD)
                    new_ref[:, lanes] = jnp.where(
                        chosen, sums[h], cache_ref[:, lanes].astype(f32)
                    ).astype(bf16)


def append(rel, split, unit_rows, scal, ck, cv, drafts, after):
    rows = ck.shape[0]
    block = rows // 4 if rows % 64 == 0 else rows
    cache_spec = pl.BlockSpec((block, ck.shape[1]), lambda i: (i, 0))
    mine, other = drafts[0], drafts[-1]
    draft_spec = pl.BlockSpec(mine.shape, lambda i: (0, 0, 0, 0))
    shape = jax.ShapeDtypeStruct(ck.shape, bf16)
    return pl.pallas_call(
        functools.partial(append_kernel, rel, split, unit_rows),
        grid=(rows // block,),
        in_specs=[pl.BlockSpec(memory_space=pltpu.VMEM)]
        + [cache_spec, cache_spec, draft_spec, draft_spec]
        + [pl.BlockSpec(memory_space=pl.ANY)] * len(after),
        out_specs=(cache_spec, cache_spec),
        out_shape=(shape, shape),
        compiler_params=pltpu.CompilerParams(vmem_limit_bytes=VMEM_BYTES),
        cost_estimate=pl.CostEstimate(flops=0, bytes_accessed=8 * ck.size, transcendentals=0),
    )(scal, ck, cv, mine, other, *after)


def one_request(n_seq, n_head, dq, dk, dv, ck, cv, accepted, length, weight):
    seq = lax.axis_index("seq")
    local_rows = dq.shape[0]
    heads_kv = dk.shape[1] // HD
    split = 2 if heads_kv % 2 == 0 else 1
    heads = heads_kv // split
    unit_rows = local_rows * split
    unit = unit_rows * GROUP
    n_bits = n_seq.bit_length() - 1
    bits = list(range(n_bits - 1, split - 2, -1))

    def swap(x, bit):
        return lax.ppermute(x, "seq", [(i, i ^ (1 << bit)) for i in range(n_seq)])

    core = seq % split

    q4 = dq.reshape(local_rows, heads_kv, GROUP, LANES).transpose(1, 0, 2, 3)
    q4 = q4.reshape(heads_kv, local_rows * GROUP, LANES)
    dk4 = dk.reshape(local_rows, heads_kv, HD).transpose(1, 0, 2)
    dv4 = dv.reshape(local_rows, heads_kv, HD).transpose(1, 0, 2)
    pack = jnp.concatenate([q4, dk4, dv4], axis=1)
    parts, caches = [pack], [ck, cv]
    if split == 2:
        mine = lax.dynamic_slice_in_dim(pack, core * heads, heads, 0)
        parts = [mine, swap(lax.dynamic_slice_in_dim(pack, (1 - core) * heads, heads, 0), 0)]
    cut = local_rows * GROUP
    second = cut + local_rows
    pieces = [p[:, :cut] for p in parts]
    pieces += [p[:, cut : cut + local_rows] for p in parts]
    pieces += [p[:, second : second + local_rows] for p in parts]
    q = jnp.concatenate(pieces, axis=1)
    d_key, d_value = q[:, unit : unit + unit_rows], q[:, unit + unit_rows :]
    spare = ((0, 0), (0, LANES - unit_rows), (0, 0))
    drafts = jnp.concatenate([jnp.pad(d_key, spare), jnp.pad(d_value, spare)], axis=1)
    q, scal = lax.optimization_barrier(
        (q[None], jnp.broadcast_to(jnp.stack([length, accepted]), (2, LANES)))
    )
    if split == 2:
        q, ck_late, cv_late = lax.optimization_barrier((q, ck, cv))
        caches += [swap(ck_late, 0), swap(cv_late, 0)]

    rel, near = [0], bits[-1]
    for bit in bits[:-1]:
        new = swap(q, bit)
        q = jnp.concatenate([q, new], axis=0)
        if split == 2 and bit == bits[0]:
            q, *own = lax.optimization_barrier((q, ck, cv))
            caches[:2] = [
                lax.dynamic_slice_in_dim(c, core * heads * HD, heads * HD, 1) for c in own
            ]
        rel = rel + [r | (1 << bit) // split for r in rel]
    q, dkv = q[:, :, :unit], q[:, :, unit:]
    rel_far = [r | (1 << near) // split for r in rel]
    q_far = swap(q, near)

    run = functools.partial(attend, scal)
    (message,) = run(q, rel, unit_rows, split, caches, drafts, True)
    num, stats = run(q_far, rel_far, unit_rows, split, caches, drafts, False, (message,))
    message = swap(message, near)

    dkv = jnp.concatenate([dkv, swap(dkv, near)], axis=0)

    for bit in reversed(bits[:-1]):
        mode = "all" if bit == bits[0] else "half"
        num, stats, message = merge(unit, mode, num, stats, message)
        message = swap(message, bit)

    att = merge(unit, "final", num, stats, message).reshape(-1, heads, unit, LANES)
    att, dkv = lax.optimization_barrier((att, dkv))
    every = [dkv, swap(dkv, 0)] if split == 2 else [dkv]
    for bit in bits[1:-1]:
        att = jnp.concatenate([att, swap(att, bit)], axis=0)
    att, every = lax.optimization_barrier((att, every))
    att_near = swap(att, near)
    halves = (rel_far, rel)
    if split == 2:
        begun = project(
            halves,
            split,
            n_head,
            ((0, 0), (0, 1), (1, 0)),
            [att, att_near, swap(att, 0)],
            weight,
        )
        result = project(
            halves, split, n_head, ((1, 1),), [swap(att_near, 0)], weight, begun, True
        )
    else:
        result = project(
            halves, split, n_head, ((0, 0), (0, 1)), [att, att_near], weight, (), True
        )
    if n_head == 2:
        keep, send = result
        projected = keep + lax.ppermute(send, "head", [(0, 1), (1, 0)]).astype(f32)
    else:
        projected = lax.psum_scatter(result[0], "head", scatter_dimension=0, tiled=True)
    new_key, new_value = append(
        rel + rel_far, split, unit_rows, scal, ck, cv, every, (result[-1],)
    )
    return projected.astype(bf16), new_key, new_value


def on_device(n_seq, n_head, dq, dk, dv, ck, cv, accepted, cache_len, weight):
    results = [
        one_request(
            n_seq, n_head, dq[r], dk[r], dv[r], ck[r], cv[r], accepted[r : r + 1], cache_len[r : r + 1], weight
        )
        for r in range(dq.shape[0])
    ]
    return tuple(jnp.stack(parts) for parts in zip(*results))


def solution(mesh):
    in_specs = (
        P(None, "seq", "head"),
        P(None, "seq", "head"),
        P(None, "seq", "head"),
        P(None, "seq", "head"),
        P(None, "seq", "head"),
        P(),
        P(),
        P("head", "seq"),
    )
    out_specs = (P(None, "head", "seq"), P(None, "seq", "head"), P(None, "seq", "head"))
    return jax.shard_map(
        functools.partial(on_device, mesh.shape["seq"], mesh.shape["head"]),
        mesh=mesh,
        in_specs=in_specs,
        out_specs=out_specs,
        check_vma=False,
    )
```

```python
import functools
import math

import jax
import jax.numpy as jnp
from jax import lax
from jax.experimental import pallas as pl
from jax.experimental.pallas import tpu as pltpu
from jax.sharding import PartitionSpec as P

QH = 64
KVH = 8
HD = 128
GROUP = QH // KVH
LANES = 128

DEAD = -1e30
FLOOR = -(2.0**96)
LOG2_SCALE = math.log2(math.e) / math.sqrt(HD)
VMEM_BYTES = 48 * 1024 * 1024

bf16 = jnp.bfloat16
f32 = jnp.float32


def round_up(n, m):
    return -(-n // m) * m


def stat_rows(units):
    return round_up(3 * round_up(units, 8), 16)


def pad_rows(x, rows):
    if x.shape[0] == rows:
        return x
    return jnp.concatenate([x, jnp.zeros((rows - x.shape[0], x.shape[1]), x.dtype)], axis=0)


def columns_to_rows(columns, unit):
    lane = lax.broadcasted_iota(jnp.int32, (unit, LANES), 1)
    square = jnp.zeros((unit, LANES), f32)
    for place, column in columns:
        square = jnp.where(lane == place, column, square)
    return jnp.transpose(pad_rows(square, LANES))


def split_total(total):
    high = total.astype(bf16)
    return high, (total - high.astype(f32)).astype(bf16)


def write_message(out_ref, row, shift, total):
    high, low = split_total(total)
    rows = jnp.concatenate([shift, high.astype(f32), low.astype(f32)], axis=0)
    out_ref[row : row + stat_rows(shift.shape[0]), :] = pad_rows(
        rows, stat_rows(shift.shape[0])
    ).astype(bf16)


def row_of(place, local_rows, core):
    return place + jnp.where(place < local_rows, core, -core) * local_rows


def attend_kernel(rel, unit_rows, split, as_message, n_after, scal, q_ref, *rest):
    caches = rest[: 2 * split]
    d_ref = rest[2 * split]
    outs = rest[2 * split + 1 + n_after :]
    units, heads = q_ref.shape[:2]
    unit = unit_rows * GROUP
    keys = caches[0].shape[0]
    seq, length = lax.axis_index("seq"), scal[0:1, 0:1]
    chip = lax.div(seq, split)
    count = units * heads
    count8 = round_up(count, 8)
    step = max(n for n in range(1, units + 1) if units % n == 0 and n * unit <= 384)
    columns = []
    out_ref = outs[0]
    key_index = lax.broadcasted_iota(jnp.int32, (1, keys), 1)
    core = lax.rem(seq, split)
    local_rows = unit_rows // split
    ones = jnp.ones((keys, LANES), bf16)
    draft = lax.broadcasted_iota(jnp.int32, (1, LANES), 1)
    draft_row = unit_rows * chip + row_of(draft, local_rows, core)
    unit_row = row_of(
        lax.shift_right_logical(lax.broadcasted_iota(jnp.int32, (unit, LANES), 0), 3),
        local_rows,
        core,
    )
    def lanes_of(head, side):
        if side == 0:
            return slice(head * HD, (head + 1) * HD)
        return pl.ds(pl.multiple_of((core * heads + head) * HD, HD), HD)

    def score_of(chunk):
        head, start, side = chunk
        queries = q_ref[start : start + step, head].reshape(step * unit, HD)
        return lax.dot_general(
            queries, caches[2 * side][:, lanes_of(head, side)], (((1,), (1,)), ((), ())), preferred_element_type=f32
        )

    chunks = [
        (head, start, side)
        for head in range(heads)
        for start in range(0, units, step)
        for side in range(split)
    ]
    tops, sums = [], []
    following = score_of(chunks[0])
    for at, (head, start, side) in enumerate(chunks):
        raw = following
        if at + 1 < len(chunks):
            following = score_of(chunks[at + 1])
        draft_values = jnp.concatenate([d_ref[head, LANES:], ones[:LANES]], axis=1)
        if side == 0:
            time = jnp.concatenate(
                [
                    unit_row + unit_rows * jnp.bitwise_xor(chip, rel[start + n])
                    for n in range(step)
                ],
                axis=0,
            )
            draft_scores = lax.dot_general(
                q_ref[start : start + step, head].reshape(step * unit, HD),
                d_ref[head, :LANES],
                (((1,), (1,)), ((), ())),
                preferred_element_type=f32,
            )
            draft_scores = jnp.where(draft_row <= time, draft_scores * LOG2_SCALE, DEAD)
        block = seq if side == 0 else seq + 1 - 2 * core
        score = jnp.where(key_index + block * keys < length, raw * LOG2_SCALE, DEAD)
        inside = (draft >= side * local_rows) & (draft < (side + 1) * local_rows)
        own_drafts = jnp.where(inside, draft_scores, DEAD)
        top = jnp.maximum(
            jnp.max(score, axis=1, keepdims=True), jnp.max(own_drafts, axis=1, keepdims=True)
        )
        top = jnp.maximum(top, FLOOR)
        tops.append(top)
        values_ones = jnp.concatenate(
            [caches[2 * side + 1][:, lanes_of(head, side)], ones], axis=1
        )
        sums.append(
            jnp.dot(jnp.exp2(score - top).astype(bf16), values_ones, preferred_element_type=f32)
            + jnp.dot(
                jnp.exp2(own_drafts - top).astype(bf16), draft_values, preferred_element_type=f32
            )
        )
        if side + 1 < split:
            continue
        shift = functools.reduce(jnp.maximum, tops).astype(bf16).astype(f32)
        both = sum(part * jnp.exp2(top - shift) for part, top in zip(sums, tops))
        weighted, total = both[:, :HD], both[:, HD : HD + 1]
        for n in range(step):
            place = (start + n) * heads + head
            part = slice(n * unit, (n + 1) * unit)
            out_ref[place * unit : (place + 1) * unit, :] = weighted[part].astype(out_ref.dtype)
            columns.append((place, shift[part]))
            columns.append((count8 + place, total[part]))
        tops, sums = [], []
    stats = columns_to_rows(columns, unit)
    if as_message:
        write_message(out_ref, count * unit, stats[:count8], stats[count8 : 2 * count8])
    else:
        outs[1][...] = stats[: 2 * count8]


def attend(scal, q, rel, unit_rows, split, caches, drafts, as_message, after=()):
    units, heads = q.shape[:2]
    unit = unit_rows * GROUP
    keys = caches[0].shape[0]
    count = units * heads
    if as_message:
        out_shape = (jax.ShapeDtypeStruct((count * unit + stat_rows(count), LANES), bf16),)
    else:
        out_shape = (
            jax.ShapeDtypeStruct((count * unit, LANES), f32),
            jax.ShapeDtypeStruct((2 * round_up(count, 8), LANES), f32),
        )
    whole = pl.BlockSpec(memory_space=pltpu.VMEM)
    in_specs = [whole] * (3 + len(caches))
    in_specs += [pl.BlockSpec(memory_space=pl.ANY)] * len(after)
    scores = count * unit * (split * keys + LANES)
    return pl.pallas_call(
        functools.partial(attend_kernel, rel, unit_rows, split, as_message, len(after)),
        in_specs=in_specs,
        out_specs=(whole,) * len(out_shape),
        out_shape=out_shape,
        compiler_params=pltpu.CompilerParams(vmem_limit_bytes=VMEM_BYTES),
        cost_estimate=pl.CostEstimate(
            flops=4 * scores * HD, bytes_accessed=4 * split * keys * heads * HD, transcendentals=scores
        ),
    )(scal, q, *caches, drafts, *after)


def merge_kernel(unit, mode, num_ref, stat_ref, msg_ref, *outs):
    rows = num_ref.shape[0]
    count = rows // unit
    count8 = stat_ref.shape[0] // 2
    own_shift, own_total = stat_ref[:count8], stat_ref[count8:]
    sent = msg_ref[rows:, :].astype(f32)
    shift = sent[:count8]
    total = sent[count8 : 2 * count8] + sent[2 * count8 : 3 * count8]
    half = count // 2
    if mode == "final":
        shift = pad_rows(jnp.concatenate([shift[half:count], shift[:half]], axis=0), count8)
        total = pad_rows(jnp.concatenate([total[half:count], total[:half]], axis=0), count8)
    new_shift = jnp.maximum(own_shift, shift)
    own_factor = jnp.exp2(own_shift - new_shift)
    factor = jnp.exp2(shift - new_shift)
    new_total = own_total * own_factor + total * factor
    if mode == "final":
        new_total = jnp.where(new_total > 0, new_total, 1.0)
        own_factor = own_factor / new_total
        factor = factor / new_total
    factors = jnp.transpose(pad_rows(jnp.concatenate([own_factor, factor], axis=0), LANES))
    for n in range(count):
        source = (n + half) % count if mode == "final" else n
        merged = num_ref[n * unit : (n + 1) * unit, :] * factors[:unit, n : n + 1]
        merged = merged + (
            msg_ref[source * unit : (source + 1) * unit, :].astype(f32)
            * factors[:unit, count8 + n : count8 + n + 1]
        )
        here = slice(n * unit, (n + 1) * unit)
        if mode == "final":
            outs[0][here, :] = merged.astype(bf16)
        elif mode == "all":
            outs[0][here, :] = merged
            outs[2][here, :] = merged.astype(bf16)
        elif n < half:
            outs[0][here, :] = merged
        else:
            outs[2][(n - half) * unit : (n - half + 1) * unit, :] = merged.astype(bf16)
    if mode == "all":
        outs[1][...] = jnp.concatenate([new_shift, new_total], axis=0)
        write_message(outs[2], rows, new_shift, new_total)
    elif mode == "half":
        half8 = round_up(half, 8)
        outs[1][...] = jnp.concatenate(
            [pad_rows(new_shift[:half], half8), pad_rows(new_total[:half], half8)], axis=0
        )
        write_message(
            outs[2],
            half * unit,
            pad_rows(new_shift[half:count], half8),
            pad_rows(new_total[half:count], half8),
        )


def merge(unit, mode, num, stats, message):
    rows = num.shape[0]
    if mode == "final":
        out_shape = jax.ShapeDtypeStruct((rows, LANES), bf16)
    else:
        rows = rows // 2 if mode == "half" else rows
        count = rows // unit
        out_shape = (
            jax.ShapeDtypeStruct((rows, LANES), f32),
            jax.ShapeDtypeStruct((2 * round_up(count, 8), LANES), f32),
            jax.ShapeDtypeStruct((rows + stat_rows(count), LANES), bf16),
        )
    return pl.pallas_call(
        functools.partial(merge_kernel, unit, mode),
        out_shape=out_shape,
        compiler_params=pltpu.CompilerParams(vmem_limit_bytes=VMEM_BYTES),
    )(num, stats, message)


def project_kernel(rel, split, n_head, parts, n_partial, *refs):
    sources, w_ref = refs[: len(parts)], refs[len(parts)]
    partial = refs[len(parts) + 1 : len(parts) + 1 + n_partial]
    outs, (rows_ref, lhs_ref) = refs[len(parts) + 1 + n_partial : -2], refs[-2:]
    seq, head = lax.axis_index("seq"), lax.axis_index("head")
    chip = lax.div(seq, split)
    core = lax.rem(seq, split)
    units, heads, unit, _ = sources[0].shape
    chips = 2 * units
    piece = unit // split
    first = head * (chips // n_head) if n_head == 2 else 0
    slots = rows_ref.shape[0] // heads
    if len(parts) < 2 * slots:
        rows_ref[...] = jnp.zeros_like(rows_ref)
    for (side, part), x_ref in zip(parts, sources):
        owner = core if side == 0 else 1 - core
        slot = owner if slots == split else 0
        for n in range(units):
            place = lax.rem(jnp.bitwise_xor(chip, rel[part][n]) - first + chips, chips)
            for part_of in range(split):
                row = place * unit + (owner if part_of == 0 else 1 - owner) * piece
                for h in range(heads):
                    rows_ref[slot * heads + h, pl.ds(pl.multiple_of(row, 16), piece), :] = x_ref[
                        n, h, part_of * piece : (part_of + 1) * piece
                    ].astype(f32)
    rows, depth = lhs_ref.shape
    for kv in range(rows_ref.shape[0]):
        for g in range(GROUP):
            lanes = slice((kv * GROUP + g) * HD, (kv * GROUP + g + 1) * HD)
            lhs_ref[:, lanes] = rows_ref[kv, pl.ds(g, rows, stride=GROUP), :].astype(bf16)
    if slots == split:
        weight = w_ref[...]
    else:
        weight = w_ref[pl.ds(pl.multiple_of((1 - core) * depth, LANES), depth), :]
    result = jnp.dot(lhs_ref[...], weight, preferred_element_type=f32)
    for ref in partial:
        result = result + ref[...]
    if len(outs) == 2:
        outs[0][...] = result[: rows // 2]
        outs[1][...] = result[rows // 2 :].astype(bf16)
    else:
        outs[0][...] = result


def project(rel, split, n_head, parts, sources, weight, partial=(), whole=False):
    units, heads, unit, _ = sources[0].shape
    slots = 1 if partial else split
    rows = 2 * units * unit // GROUP
    columns = weight.shape[1]
    if n_head == 2 and whole:
        out_shape = tuple(jax.ShapeDtypeStruct((rows // 2, columns), t) for t in (f32, bf16))
    else:
        out_shape = (jax.ShapeDtypeStruct((rows, columns), f32),)
    return pl.pallas_call(
        functools.partial(project_kernel, rel, split, n_head, parts, len(partial)),
        in_specs=[pl.BlockSpec(memory_space=pltpu.VMEM)] * (len(sources) + 1 + len(partial)),
        out_shape=out_shape,
        scratch_shapes=[
            pltpu.VMEM((heads * slots, 2 * units * unit, LANES), f32),
            pltpu.VMEM((rows, heads * slots * GROUP * HD), bf16),
        ],
        compiler_params=pltpu.CompilerParams(vmem_limit_bytes=VMEM_BYTES),
        cost_estimate=pl.CostEstimate(
            flops=2 * rows * columns * heads * slots * GROUP * HD,
            bytes_accessed=2 * columns * heads * slots * GROUP * HD,
            transcendentals=0,
        ),
    )(*sources, weight, *partial)


def drafts_kernel(split, own_ref, *rest):
    others, (draft_ref, unit_ref, rows_ref) = rest[:-3], rest[-3:]
    rows, width = own_ref.shape
    heads = draft_ref.shape[0]
    core = lax.rem(lax.axis_index("seq"), split)
    rows_ref[...] = jnp.zeros_like(rows_ref)
    for n, ref in enumerate((own_ref, *others)):
        rows_ref[n * rows : (n + 1) * rows, :] = ref[...].astype(f32)
    unit_rows = rows * (1 + len(others))
    for h in range(heads):
        for n in range(2):
            lanes = pl.ds(pl.multiple_of(n * (width // 2) + (core * heads + h) * HD, HD), HD)
            draft_ref[h, n * LANES : (n + 1) * LANES, :] = rows_ref[:, lanes].astype(bf16)
        unit_ref[h] = jnp.concatenate(
            [
                rows_ref[
                    :unit_rows,
                    pl.ds(pl.multiple_of(n * (width // 2) + (core * heads + h) * HD, HD), HD),
                ]
                for n in range(2)
            ],
            axis=0,
        ).astype(bf16)


def chip_drafts(split, heads, own, others):
    rows, width = own.shape
    return pl.pallas_call(
        functools.partial(drafts_kernel, split),
        in_specs=[pl.BlockSpec(memory_space=pltpu.VMEM)] * (1 + len(others)),
        out_shape=(
            jax.ShapeDtypeStruct((heads, 2 * LANES, HD), bf16),
            jax.ShapeDtypeStruct((heads, 2 * rows * split, HD), bf16),
        ),
        scratch_shapes=[pltpu.VMEM((LANES, width), f32)],
        compiler_params=pltpu.CompilerParams(vmem_limit_bytes=VMEM_BYTES),
    )(own, *others)


def append_kernel(rel, split, unit_rows, scal, ck_ref, cv_ref, mine_ref, other_ref, *rest):
    nk_ref, nv_ref = rest[-2:]
    rows, width = ck_ref.shape
    chips, heads, both, _ = mine_ref.shape
    local_rows = unit_rows // split
    seq = lax.axis_index("seq")
    chip, core = lax.div(seq, split), lax.rem(seq, split)
    length, accepted = jnp.max(scal[0:1]), jnp.max(scal[1:2])
    first = (seq * pl.num_programs(0) + pl.program_id(0)) * rows - length
    touched = (first < accepted) & (first + rows > 0)

    @pl.when(jnp.logical_not(touched))
    def _():
        nk_ref[...] = ck_ref[...]
        nv_ref[...] = cv_ref[...]

    @pl.when(touched)
    def _():
        place = first + lax.broadcasted_iota(jnp.int32, (rows, both), 0)
        lane = lax.broadcasted_iota(jnp.int32, (rows, both), 1)
        inside = (place >= 0) & (place < accepted)
        chosen = first + lax.broadcasted_iota(jnp.int32, (rows, HD), 0)
        chosen = (chosen >= 0) & (chosen < accepted)
        for side in range(split):
            drafts = mine_ref if side == 0 else other_ref
            source_core = core if side == 0 else 1 - core
            for cache_ref, new_ref, start in ((ck_ref, nk_ref, 0), (cv_ref, nv_ref, unit_rows)):
                sums = [jnp.zeros((rows, HD), f32)] * heads
                here = (lane >= start) & (lane < start + unit_rows) & inside
                row = row_of(lane - start, local_rows, source_core)
                for n in range(chips):
                    source = jnp.bitwise_xor(chip, rel[n]) * unit_rows + row
                    pick = jnp.where(here & (source == place), 1.0, 0.0).astype(bf16)
                    for h in range(heads):
                        sums[h] = sums[h] + jnp.dot(
                            pick, drafts[n, h], preferred_element_type=f32
                        )
                for h in range(heads):
                    lanes = pl.ds(pl.multiple_of((source_core * heads + h) * HD, HD), HD)
                    new_ref[:, lanes] = jnp.where(
                        chosen, sums[h], cache_ref[:, lanes].astype(f32)
                    ).astype(bf16)


def append(rel, split, unit_rows, scal, ck, cv, drafts, after):
    rows = ck.shape[0]
    block = rows // 4 if rows % 64 == 0 else rows
    cache_spec = pl.BlockSpec((block, ck.shape[1]), lambda i: (i, 0))
    mine, other = drafts[0], drafts[-1]
    draft_spec = pl.BlockSpec(mine.shape, lambda i: (0, 0, 0, 0))
    shape = jax.ShapeDtypeStruct(ck.shape, bf16)
    return pl.pallas_call(
        functools.partial(append_kernel, rel, split, unit_rows),
        grid=(rows // block,),
        in_specs=[pl.BlockSpec(memory_space=pltpu.VMEM)]
        + [cache_spec, cache_spec, draft_spec, draft_spec]
        + [pl.BlockSpec(memory_space=pl.ANY)] * len(after),
        out_specs=(cache_spec, cache_spec),
        out_shape=(shape, shape),
        compiler_params=pltpu.CompilerParams(vmem_limit_bytes=VMEM_BYTES),
        cost_estimate=pl.CostEstimate(flops=0, bytes_accessed=8 * ck.size, transcendentals=0),
    )(scal, ck, cv, mine, other, *after)


def one_request(n_seq, n_head, dq, dk, dv, ck, cv, accepted, length, weight):
    seq = lax.axis_index("seq")
    local_rows = dq.shape[0]
    heads_kv = dk.shape[1] // HD
    split = 2 if heads_kv % 2 == 0 else 1
    heads = heads_kv // split
    unit_rows = local_rows * split
    unit = unit_rows * GROUP
    n_bits = n_seq.bit_length() - 1
    bits = list(range(n_bits - 1, split - 2, -1))

    def swap(x, bit):
        return lax.ppermute(x, "seq", [(i, i ^ (1 << bit)) for i in range(n_seq)])

    core = seq % split

    q4 = dq.reshape(local_rows, heads_kv, GROUP, LANES).transpose(1, 0, 2, 3)
    q4 = q4.reshape(heads_kv, local_rows * GROUP, LANES)
    drafts_own = jnp.concatenate([dk, dv], axis=1)
    caches, drafts_other = [ck, cv], []
    q = q4
    if split == 2:
        mine = lax.dynamic_slice_in_dim(q4, core * heads, heads, 0)
        sent = lax.dynamic_slice_in_dim(q4, (1 - core) * heads, heads, 0)
        q = jnp.concatenate([mine, swap(sent, 0)], axis=1)
    q, scal = lax.optimization_barrier(
        (q[None], jnp.broadcast_to(jnp.stack([length, accepted]), (2, LANES)))
    )
    if split == 2:
        q, drafts_own, *late = lax.optimization_barrier((q, drafts_own, ck, cv))
        drafts_other = [swap(drafts_own, 0)]
        caches += [swap(c, 0) for c in late]

    rel, near = [0], bits[-1]
    for bit in bits[:-1]:
        new = swap(q, bit)
        q = jnp.concatenate([q, new], axis=0)
        if split == 2 and bit == bits[0]:
            q, drafts_own, drafts_other, *own = lax.optimization_barrier(
                (q, drafts_own, drafts_other, ck, cv)
            )
            caches[:2] = [
                lax.dynamic_slice_in_dim(c, core * heads * HD, heads * HD, 1) for c in own
            ]
        rel = rel + [r | (1 << bit) // split for r in rel]
    drafts, chip_rows = chip_drafts(split, heads, drafts_own, drafts_other)
    rel_far = [r | (1 << near) // split for r in rel]
    q_far = swap(q, near)

    run = functools.partial(attend, scal)
    (message,) = run(q, rel, unit_rows, split, caches, drafts, True)
    num, stats = run(q_far, rel_far, unit_rows, split, caches, drafts, False, (message,))
    message = swap(message, near)

    dkv, order = chip_rows[None], [0]

    for bit in reversed(bits[:-1]):
        mode = "all" if bit == bits[0] else "half"
        num, stats, message = merge(unit, mode, num, stats, message)
        if bit in (bits[-2], bits[0]):
            num, dkv = lax.optimization_barrier((num, dkv))
            for late in bits[-2:-1] if bit == bits[-2] else bits[:-2]:
                dkv = jnp.concatenate([dkv, swap(dkv, late)], axis=0)
                order = order + [r ^ (1 << late) // split for r in order]
        message = swap(message, bit)

    att = merge(unit, "final", num, stats, message).reshape(-1, heads, unit, LANES)
    for bit in bits[1:-1]:
        att = jnp.concatenate([att, swap(att, bit)], axis=0)
    att, dkv = lax.optimization_barrier((att, dkv))
    att_near = swap(att, near)
    dkv = jnp.concatenate([dkv, swap(dkv, near)], axis=0)
    order = order + [r ^ (1 << near) // split for r in order]
    halves = (rel_far, rel)
    if split == 2:
        begun = project(
            halves,
            split,
            n_head,
            ((0, 0), (0, 1), (1, 0)),
            [att, att_near, swap(att, 0)],
            weight,
        )
        begun, dkv = lax.optimization_barrier((begun, dkv))
        result = project(
            halves, split, n_head, ((1, 1),), [swap(att_near, 0)], weight, begun, True
        )
    else:
        result = project(
            halves, split, n_head, ((0, 0), (0, 1)), [att, att_near], weight, (), True
        )
    if n_head == 2:
        keep, send = result
        projected = keep + lax.ppermute(send, "head", [(0, 1), (1, 0)]).astype(f32)
    else:
        projected = lax.psum_scatter(result[0], "head", scatter_dimension=0, tiled=True)
    every = [dkv, swap(dkv, 0)] if split == 2 else [dkv]
    new_key, new_value = append(
        order, split, unit_rows, scal, ck, cv, every, (result[-1],)
    )
    return projected.astype(bf16), new_key, new_value


def on_device(n_seq, n_head, dq, dk, dv, ck, cv, accepted, cache_len, weight):
    results = [
        one_request(
            n_seq, n_head, dq[r], dk[r], dv[r], ck[r], cv[r], accepted[r : r + 1], cache_len[r : r + 1], weight
        )
        for r in range(dq.shape[0])
    ]
    return tuple(jnp.stack(parts) for parts in zip(*results))


def solution(mesh):
    in_specs = (
        P(None, "seq", "head"),
        P(None, "seq", "head"),
        P(None, "seq", "head"),
        P(None, "seq", "head"),
        P(None, "seq", "head"),
        P(),
        P(),
        P("head", "seq"),
    )
    out_specs = (P(None, "head", "seq"), P(None, "seq", "head"), P(None, "seq", "head"))
    return jax.shard_map(
        functools.partial(on_device, mesh.shape["seq"], mesh.shape["head"]),
        mesh=mesh,
        in_specs=in_specs,
        out_specs=out_specs,
        check_vma=False,
    )
```

```python
import functools
import math

import jax
import jax.numpy as jnp
from jax import lax
from jax.experimental import pallas as pl
from jax.experimental.pallas import tpu as pltpu
from jax.sharding import PartitionSpec as P

QH = 64
KVH = 8
HD = 128
GROUP = QH // KVH
LANES = 128

DEAD = -1e30
FLOOR = -(2.0**96)
LOG2_SCALE = math.log2(math.e) / math.sqrt(HD)
VMEM_BYTES = 48 * 1024 * 1024

bf16 = jnp.bfloat16
f32 = jnp.float32


def round_up(n, m):
    return -(-n // m) * m


def stat_rows(units):
    return round_up(3 * round_up(units, 8), 16)


def pad_rows(x, rows):
    if x.shape[0] == rows:
        return x
    return jnp.concatenate([x, jnp.zeros((rows - x.shape[0], x.shape[1]), x.dtype)], axis=0)


def columns_to_rows(columns, unit):
    lane = lax.broadcasted_iota(jnp.int32, (unit, LANES), 1)
    square = jnp.zeros((unit, LANES), f32)
    for place, column in columns:
        square = jnp.where(lane == place, column, square)
    return jnp.transpose(pad_rows(square, LANES))


def split_total(total):
    high = total.astype(bf16)
    return high, (total - high.astype(f32)).astype(bf16)


def write_message(out_ref, row, shift, total):
    high, low = split_total(total)
    rows = jnp.concatenate([shift, high.astype(f32), low.astype(f32)], axis=0)
    out_ref[row : row + stat_rows(shift.shape[0]), :] = pad_rows(
        rows, stat_rows(shift.shape[0])
    ).astype(bf16)


def row_of(place, local_rows, core):
    return place + jnp.where(place < local_rows, core, -core) * local_rows


def attend_kernel(rel, unit_rows, split, as_message, n_after, scal, q_ref, *rest):
    caches = rest[: 2 * split]
    d_ref = rest[2 * split]
    outs = rest[2 * split + 1 + n_after :]
    units, heads = q_ref.shape[:2]
    unit = unit_rows * GROUP
    keys = caches[0].shape[0]
    seq, length = lax.axis_index("seq"), scal[0:1, 0:1]
    chip = lax.div(seq, split)
    count = units * heads
    count8 = round_up(count, 8)
    step = max(n for n in range(1, units + 1) if units % n == 0 and n * unit <= 384)
    columns = []
    out_ref = outs[0]
    key_index = lax.broadcasted_iota(jnp.int32, (1, keys), 1)
    core = lax.rem(seq, split)
    local_rows = unit_rows // split
    ones = jnp.ones((keys, LANES), bf16)
    draft = lax.broadcasted_iota(jnp.int32, (1, LANES), 1)
    draft_row = unit_rows * chip + row_of(draft, local_rows, core)
    unit_row = row_of(
        lax.shift_right_logical(lax.broadcasted_iota(jnp.int32, (unit, LANES), 0), 3),
        local_rows,
        core,
    )
    def lanes_of(head, side):
        if side == 0:
            return slice(head * HD, (head + 1) * HD)
        return pl.ds(pl.multiple_of((core * heads + head) * HD, HD), HD)

    def score_of(chunk):
        head, start, side = chunk
        queries = q_ref[start : start + step, head].reshape(step * unit, HD)
        return lax.dot_general(
            queries, caches[2 * side][:, lanes_of(head, side)], (((1,), (1,)), ((), ())), preferred_element_type=f32
        )

    chunks = [
        (head, start, side)
        for head in range(heads)
        for start in range(0, units, step)
        for side in range(split)
    ]
    tops, sums = [], []
    following = score_of(chunks[0])
    for at, (head, start, side) in enumerate(chunks):
        raw = following
        if at + 1 < len(chunks):
            following = score_of(chunks[at + 1])
        draft_values = jnp.concatenate([d_ref[head, LANES:], ones[:LANES]], axis=1)
        if side == 0:
            time = jnp.concatenate(
                [
                    unit_row + unit_rows * jnp.bitwise_xor(chip, rel[start + n])
                    for n in range(step)
                ],
                axis=0,
            )
            draft_scores = lax.dot_general(
                q_ref[start : start + step, head].reshape(step * unit, HD),
                d_ref[head, :LANES],
                (((1,), (1,)), ((), ())),
                preferred_element_type=f32,
            )
            draft_scores = jnp.where(draft_row <= time, draft_scores * LOG2_SCALE, DEAD)
        block = seq if side == 0 else seq + 1 - 2 * core
        score = jnp.where(key_index + block * keys < length, raw * LOG2_SCALE, DEAD)
        inside = (draft >= side * local_rows) & (draft < (side + 1) * local_rows)
        own_drafts = jnp.where(inside, draft_scores, DEAD)
        top = jnp.maximum(
            jnp.max(score, axis=1, keepdims=True), jnp.max(own_drafts, axis=1, keepdims=True)
        )
        top = jnp.maximum(top, FLOOR)
        tops.append(top)
        values_ones = jnp.concatenate(
            [caches[2 * side + 1][:, lanes_of(head, side)], ones], axis=1
        )
        sums.append(
            jnp.dot(jnp.exp2(score - top).astype(bf16), values_ones, preferred_element_type=f32)
            + jnp.dot(
                jnp.exp2(own_drafts - top).astype(bf16), draft_values, preferred_element_type=f32
            )
        )
        if side + 1 < split:
            continue
        shift = functools.reduce(jnp.maximum, tops).astype(bf16).astype(f32)
        both = sum(part * jnp.exp2(top - shift) for part, top in zip(sums, tops))
        weighted, total = both[:, :HD], both[:, HD : HD + 1]
        for n in range(step):
            place = (start + n) * heads + head
            part = slice(n * unit, (n + 1) * unit)
            out_ref[place * unit : (place + 1) * unit, :] = weighted[part].astype(out_ref.dtype)
            columns.append((place, shift[part]))
            columns.append((count8 + place, total[part]))
        tops, sums = [], []
    stats = columns_to_rows(columns, unit)
    if as_message:
        write_message(out_ref, count * unit, stats[:count8], stats[count8 : 2 * count8])
    else:
        outs[1][...] = stats[: 2 * count8]


def attend(scal, q, rel, unit_rows, split, caches, drafts, as_message, after=()):
    units, heads = q.shape[:2]
    unit = unit_rows * GROUP
    keys = caches[0].shape[0]
    count = units * heads
    if as_message:
        out_shape = (jax.ShapeDtypeStruct((count * unit + stat_rows(count), LANES), bf16),)
    else:
        out_shape = (
            jax.ShapeDtypeStruct((count * unit, LANES), f32),
            jax.ShapeDtypeStruct((2 * round_up(count, 8), LANES), f32),
        )
    whole = pl.BlockSpec(memory_space=pltpu.VMEM)
    in_specs = [whole] * (3 + len(caches))
    in_specs += [pl.BlockSpec(memory_space=pl.ANY)] * len(after)
    scores = count * unit * (split * keys + LANES)
    return pl.pallas_call(
        functools.partial(attend_kernel, rel, unit_rows, split, as_message, len(after)),
        in_specs=in_specs,
        out_specs=(whole,) * len(out_shape),
        out_shape=out_shape,
        compiler_params=pltpu.CompilerParams(vmem_limit_bytes=VMEM_BYTES),
        cost_estimate=pl.CostEstimate(
            flops=4 * scores * HD, bytes_accessed=4 * split * keys * heads * HD, transcendentals=scores
        ),
    )(scal, q, *caches, drafts, *after)


def merge_kernel(unit, mode, num_ref, stat_ref, msg_ref, *outs):
    rows = num_ref.shape[0]
    count = rows // unit
    count8 = stat_ref.shape[0] // 2
    own_shift, own_total = stat_ref[:count8], stat_ref[count8:]
    sent = msg_ref[rows:, :].astype(f32)
    shift = sent[:count8]
    total = sent[count8 : 2 * count8] + sent[2 * count8 : 3 * count8]
    half = count // 2
    if mode == "final":
        shift = pad_rows(jnp.concatenate([shift[half:count], shift[:half]], axis=0), count8)
        total = pad_rows(jnp.concatenate([total[half:count], total[:half]], axis=0), count8)
    new_shift = jnp.maximum(own_shift, shift)
    own_factor = jnp.exp2(own_shift - new_shift)
    factor = jnp.exp2(shift - new_shift)
    new_total = own_total * own_factor + total * factor
    if mode == "final":
        new_total = jnp.where(new_total > 0, new_total, 1.0)
        own_factor = own_factor / new_total
        factor = factor / new_total
    factors = jnp.transpose(pad_rows(jnp.concatenate([own_factor, factor], axis=0), LANES))
    for n in range(count):
        source = (n + half) % count if mode == "final" else n
        merged = num_ref[n * unit : (n + 1) * unit, :] * factors[:unit, n : n + 1]
        merged = merged + (
            msg_ref[source * unit : (source + 1) * unit, :].astype(f32)
            * factors[:unit, count8 + n : count8 + n + 1]
        )
        here = slice(n * unit, (n + 1) * unit)
        if mode == "final":
            outs[0][here, :] = merged.astype(bf16)
        elif mode == "all":
            outs[0][here, :] = merged
            outs[2][here, :] = merged.astype(bf16)
        elif n < half:
            outs[0][here, :] = merged
        else:
            outs[2][(n - half) * unit : (n - half + 1) * unit, :] = merged.astype(bf16)
    if mode == "all":
        outs[1][...] = jnp.concatenate([new_shift, new_total], axis=0)
        write_message(outs[2], rows, new_shift, new_total)
    elif mode == "half":
        half8 = round_up(half, 8)
        outs[1][...] = jnp.concatenate(
            [pad_rows(new_shift[:half], half8), pad_rows(new_total[:half], half8)], axis=0
        )
        write_message(
            outs[2],
            half * unit,
            pad_rows(new_shift[half:count], half8),
            pad_rows(new_total[half:count], half8),
        )


def merge(unit, mode, num, stats, message):
    rows = num.shape[0]
    if mode == "final":
        out_shape = jax.ShapeDtypeStruct((rows, LANES), bf16)
    else:
        rows = rows // 2 if mode == "half" else rows
        count = rows // unit
        out_shape = (
            jax.ShapeDtypeStruct((rows, LANES), f32),
            jax.ShapeDtypeStruct((2 * round_up(count, 8), LANES), f32),
            jax.ShapeDtypeStruct((rows + stat_rows(count), LANES), bf16),
        )
    return pl.pallas_call(
        functools.partial(merge_kernel, unit, mode),
        out_shape=out_shape,
        compiler_params=pltpu.CompilerParams(vmem_limit_bytes=VMEM_BYTES),
    )(num, stats, message)


def project_kernel(rel, split, n_head, parts, n_partial, *refs):
    sources, w_ref = refs[: len(parts)], refs[len(parts)]
    partial = refs[len(parts) + 1 : len(parts) + 1 + n_partial]
    outs, (rows_ref, lhs_ref) = refs[len(parts) + 1 + n_partial : -2], refs[-2:]
    seq, head = lax.axis_index("seq"), lax.axis_index("head")
    chip = lax.div(seq, split)
    core = lax.rem(seq, split)
    units, heads, unit, _ = sources[0].shape
    chips = 2 * units
    piece = unit // split
    first = head * (chips // n_head) if n_head == 2 else 0
    slots = rows_ref.shape[0] // heads
    if len(parts) < 2 * slots:
        rows_ref[...] = jnp.zeros_like(rows_ref)
    for (side, part), x_ref in zip(parts, sources):
        owner = core if side == 0 else 1 - core
        slot = owner if slots == split else 0
        for n in range(units):
            place = lax.rem(jnp.bitwise_xor(chip, rel[part][n]) - first + chips, chips)
            for part_of in range(split):
                row = place * unit + (owner if part_of == 0 else 1 - owner) * piece
                for h in range(heads):
                    rows_ref[slot * heads + h, pl.ds(pl.multiple_of(row, 16), piece), :] = x_ref[
                        n, h, part_of * piece : (part_of + 1) * piece
                    ].astype(f32)
    rows, depth = lhs_ref.shape
    for kv in range(rows_ref.shape[0]):
        for g in range(GROUP):
            lanes = slice((kv * GROUP + g) * HD, (kv * GROUP + g + 1) * HD)
            lhs_ref[:, lanes] = rows_ref[kv, pl.ds(g, rows, stride=GROUP), :].astype(bf16)
    if slots == split:
        weight = w_ref[...]
    else:
        weight = w_ref[pl.ds(pl.multiple_of((1 - core) * depth, LANES), depth), :]
    result = jnp.dot(lhs_ref[...], weight, preferred_element_type=f32)
    for ref in partial:
        result = result + ref[...]
    if len(outs) == 2:
        outs[0][...] = result[: rows // 2]
        outs[1][...] = result[rows // 2 :].astype(bf16)
    else:
        outs[0][...] = result


def project(rel, split, n_head, parts, sources, weight, partial=(), whole=False):
    units, heads, unit, _ = sources[0].shape
    slots = 1 if partial else split
    rows = 2 * units * unit // GROUP
    columns = weight.shape[1]
    if n_head == 2 and whole:
        out_shape = tuple(jax.ShapeDtypeStruct((rows // 2, columns), t) for t in (f32, bf16))
    else:
        out_shape = (jax.ShapeDtypeStruct((rows, columns), f32),)
    return pl.pallas_call(
        functools.partial(project_kernel, rel, split, n_head, parts, len(partial)),
        in_specs=[pl.BlockSpec(memory_space=pltpu.VMEM)] * (len(sources) + 1 + len(partial)),
        out_shape=out_shape,
        scratch_shapes=[
            pltpu.VMEM((heads * slots, 2 * units * unit, LANES), f32),
            pltpu.VMEM((rows, heads * slots * GROUP * HD), bf16),
        ],
        compiler_params=pltpu.CompilerParams(vmem_limit_bytes=VMEM_BYTES),
        cost_estimate=pl.CostEstimate(
            flops=2 * rows * columns * heads * slots * GROUP * HD,
            bytes_accessed=2 * columns * heads * slots * GROUP * HD,
            transcendentals=0,
        ),
    )(*sources, weight, *partial)


def drafts_kernel(split, own_ref, *rest):
    others, (draft_ref, unit_ref, rows_ref) = rest[:-3], rest[-3:]
    rows, width = own_ref.shape
    heads = draft_ref.shape[0]
    core = lax.rem(lax.axis_index("seq"), split)
    rows_ref[...] = jnp.zeros_like(rows_ref)
    for n, ref in enumerate((own_ref, *others)):
        rows_ref[n * rows : (n + 1) * rows, :] = ref[...].astype(f32)
    unit_rows = rows * (1 + len(others))
    for h in range(heads):
        for n in range(2):
            lanes = pl.ds(pl.multiple_of(n * (width // 2) + (core * heads + h) * HD, HD), HD)
            draft_ref[h, n * LANES : (n + 1) * LANES, :] = rows_ref[:, lanes].astype(bf16)
        chip_rows = jnp.concatenate(
            [
                rows_ref[
                    :unit_rows,
                    pl.ds(pl.multiple_of(n * (width // 2) + (core * heads + h) * HD, HD), HD),
                ]
                for n in range(2)
            ],
            axis=0,
        )
        unit_ref[h] = pad_rows(chip_rows, unit_ref.shape[1]).astype(bf16)


def chip_drafts(split, heads, own, others):
    rows, width = own.shape
    return pl.pallas_call(
        functools.partial(drafts_kernel, split),
        in_specs=[pl.BlockSpec(memory_space=pltpu.VMEM)] * (1 + len(others)),
        out_shape=(
            jax.ShapeDtypeStruct((heads, 2 * LANES, HD), bf16),
            jax.ShapeDtypeStruct((heads, round_up(2 * rows * split, 8), HD), bf16),
        ),
        scratch_shapes=[pltpu.VMEM((LANES, width), f32)],
        compiler_params=pltpu.CompilerParams(vmem_limit_bytes=VMEM_BYTES),
    )(own, *others)


def append_kernel(rel, split, unit_rows, scal, ck_ref, cv_ref, mine_ref, other_ref, *rest):
    nk_ref, nv_ref = rest[-2:]
    rows, width = ck_ref.shape
    chips, heads, both, _ = mine_ref.shape
    local_rows = unit_rows // split
    seq = lax.axis_index("seq")
    chip, core = lax.div(seq, split), lax.rem(seq, split)
    length, accepted = jnp.max(scal[0:1]), jnp.max(scal[1:2])
    first = (seq * pl.num_programs(0) + pl.program_id(0)) * rows - length
    touched = (first < accepted) & (first + rows > 0)

    @pl.when(jnp.logical_not(touched))
    def _():
        nk_ref[...] = ck_ref[...]
        nv_ref[...] = cv_ref[...]

    @pl.when(touched)
    def _():
        depth = chips * both
        place = first + lax.broadcasted_iota(jnp.int32, (rows, depth), 0)
        lane = lax.broadcasted_iota(jnp.int32, (1, depth), 1)
        base = jnp.zeros((1, depth), jnp.int32)
        row = lane
        for n in range(chips):
            here = (lane >= n * both) & (lane < (n + 1) * both)
            base = jnp.where(here, jnp.bitwise_xor(chip, rel[n]) * unit_rows, base)
            row = jnp.where(here, lane - n * both, row)
        chosen = first + lax.broadcasted_iota(jnp.int32, (rows, HD), 0)
        chosen = (chosen >= 0) & (chosen < accepted)
        for side in range(split):
            drafts = mine_ref if side == 0 else other_ref
            source_core = core if side == 0 else 1 - core
            values = [
                drafts[:, h].astype(f32).reshape(depth, HD).astype(bf16) for h in range(heads)
            ]
            for cache_ref, new_ref, start in ((ck_ref, nk_ref, 0), (cv_ref, nv_ref, unit_rows)):
                source = base + row_of(row - start, local_rows, source_core)
                source = jnp.where((row >= start) & (row < start + unit_rows), source, -(1 << 24))
                pick = jnp.where(source == place, 1.0, 0.0).astype(bf16)
                for h in range(heads):
                    lanes = pl.ds(pl.multiple_of((source_core * heads + h) * HD, HD), HD)
                    moved = jnp.dot(pick, values[h], preferred_element_type=f32)
                    new_ref[:, lanes] = jnp.where(
                        chosen, moved, cache_ref[:, lanes].astype(f32)
                    ).astype(bf16)


def append(rel, split, unit_rows, scal, ck, cv, drafts, after):
    rows = ck.shape[0]
    block = rows // 4 if rows % 64 == 0 else rows
    cache_spec = pl.BlockSpec((block, ck.shape[1]), lambda i: (i, 0))
    mine, other = drafts[0], drafts[-1]
    draft_spec = pl.BlockSpec(mine.shape, lambda i: (0, 0, 0, 0))
    shape = jax.ShapeDtypeStruct(ck.shape, bf16)
    return pl.pallas_call(
        functools.partial(append_kernel, rel, split, unit_rows),
        grid=(rows // block,),
        in_specs=[pl.BlockSpec(memory_space=pltpu.VMEM)]
        + [cache_spec, cache_spec, draft_spec, draft_spec]
        + [pl.BlockSpec(memory_space=pl.ANY)] * len(after),
        out_specs=(cache_spec, cache_spec),
        out_shape=(shape, shape),
        compiler_params=pltpu.CompilerParams(vmem_limit_bytes=VMEM_BYTES),
        cost_estimate=pl.CostEstimate(flops=0, bytes_accessed=8 * ck.size, transcendentals=0),
    )(scal, ck, cv, mine, other, *after)


def one_request(n_seq, n_head, dq, dk, dv, ck, cv, accepted, length, weight):
    seq = lax.axis_index("seq")
    local_rows = dq.shape[0]
    heads_kv = dk.shape[1] // HD
    split = 2 if heads_kv % 2 == 0 else 1
    heads = heads_kv // split
    unit_rows = local_rows * split
    unit = unit_rows * GROUP
    n_bits = n_seq.bit_length() - 1
    bits = list(range(n_bits - 1, split - 2, -1))

    def swap(x, bit):
        return lax.ppermute(x, "seq", [(i, i ^ (1 << bit)) for i in range(n_seq)])

    core = seq % split

    q4 = dq.reshape(local_rows, heads_kv, GROUP, LANES).transpose(1, 0, 2, 3)
    q4 = q4.reshape(heads_kv, local_rows * GROUP, LANES)
    drafts_own = jnp.concatenate([dk, dv], axis=1)
    caches, drafts_other = [ck, cv], []
    q = q4
    if split == 2:
        mine = lax.dynamic_slice_in_dim(q4, core * heads, heads, 0)
        sent = lax.dynamic_slice_in_dim(q4, (1 - core) * heads, heads, 0)
        q = jnp.concatenate([mine, swap(sent, 0)], axis=1)
    q, scal = lax.optimization_barrier(
        (q[None], jnp.broadcast_to(jnp.stack([length, accepted]), (2, LANES)))
    )
    if split == 2:
        q, drafts_own, *late = lax.optimization_barrier((q, drafts_own, ck, cv))
        drafts_other = [swap(drafts_own, 0)]
        caches += [swap(c, 0) for c in late]

    rel, near = [0], bits[-1]
    for bit in bits[:-1]:
        new = swap(q, bit)
        q = jnp.concatenate([q, new], axis=0)
        if split == 2 and bit == bits[0]:
            q, drafts_own, drafts_other, *own = lax.optimization_barrier(
                (q, drafts_own, drafts_other, ck, cv)
            )
            caches[:2] = [
                lax.dynamic_slice_in_dim(c, core * heads * HD, heads * HD, 1) for c in own
            ]
        rel = rel + [r | (1 << bit) // split for r in rel]
    drafts, chip_rows = chip_drafts(split, heads, drafts_own, drafts_other)
    rel_far = [r | (1 << near) // split for r in rel]
    q_far = swap(q, near)

    run = functools.partial(attend, scal)
    (message,) = run(q, rel, unit_rows, split, caches, drafts, True)
    num, stats = run(q_far, rel_far, unit_rows, split, caches, drafts, False, (message,))
    message = swap(message, near)

    dkv, order = chip_rows[None], [0]

    for bit in reversed(bits[:-1]):
        mode = "all" if bit == bits[0] else "half"
        num, stats, message = merge(unit, mode, num, stats, message)
        if bit in (bits[-2], bits[0]):
            num, dkv = lax.optimization_barrier((num, dkv))
            for late in bits[-2:-1] if bit == bits[-2] else bits[:-2]:
                dkv = jnp.concatenate([dkv, swap(dkv, late)], axis=0)
                order = order + [r ^ (1 << late) // split for r in order]
        message = swap(message, bit)

    att = merge(unit, "final", num, stats, message).reshape(-1, heads, unit, LANES)
    for bit in bits[1:-1]:
        att = jnp.concatenate([att, swap(att, bit)], axis=0)
    att, dkv = lax.optimization_barrier((att, dkv))
    att_near = swap(att, near)
    dkv = jnp.concatenate([dkv, swap(dkv, near)], axis=0)
    order = order + [r ^ (1 << near) // split for r in order]
    halves = (rel_far, rel)
    if split == 2:
        begun = project(
            halves,
            split,
            n_head,
            ((0, 0), (0, 1), (1, 0)),
            [att, att_near, swap(att, 0)],
            weight,
        )
        begun, dkv = lax.optimization_barrier((begun, dkv))
        result = project(
            halves, split, n_head, ((1, 1),), [swap(att_near, 0)], weight, begun, True
        )
    else:
        result = project(
            halves, split, n_head, ((0, 0), (0, 1)), [att, att_near], weight, (), True
        )
    if n_head == 2:
        keep, send = result
        projected = keep + lax.ppermute(send, "head", [(0, 1), (1, 0)]).astype(f32)
    else:
        projected = lax.psum_scatter(result[0], "head", scatter_dimension=0, tiled=True)
    every = [dkv, swap(dkv, 0)] if split == 2 else [dkv]
    new_key, new_value = append(
        order, split, unit_rows, scal, ck, cv, every, (result[-1],)
    )
    return projected.astype(bf16), new_key, new_value


def on_device(n_seq, n_head, dq, dk, dv, ck, cv, accepted, cache_len, weight):
    results = [
        one_request(
            n_seq, n_head, dq[r], dk[r], dv[r], ck[r], cv[r], accepted[r : r + 1], cache_len[r : r + 1], weight
        )
        for r in range(dq.shape[0])
    ]
    return tuple(jnp.stack(parts) for parts in zip(*results))


def solution(mesh):
    in_specs = (
        P(None, "seq", "head"),
        P(None, "seq", "head"),
        P(None, "seq", "head"),
        P(None, "seq", "head"),
        P(None, "seq", "head"),
        P(),
        P(),
        P("head", "seq"),
    )
    out_specs = (P(None, "head", "seq"), P(None, "seq", "head"), P(None, "seq", "head"))
    return jax.shard_map(
        functools.partial(on_device, mesh.shape["seq"], mesh.shape["head"]),
        mesh=mesh,
        in_specs=in_specs,
        out_specs=out_specs,
        check_vma=False,
    )
```

```python
import functools
import math

import jax
import jax.numpy as jnp
from jax import lax
from jax.experimental import pallas as pl
from jax.experimental.pallas import tpu as pltpu
from jax.sharding import PartitionSpec as P

QH = 64
KVH = 8
HD = 128
GROUP = QH // KVH
LANES = 128

DEAD = -1e30
FLOOR = -(2.0**96)
LOG2_SCALE = math.log2(math.e) / math.sqrt(HD)
VMEM_BYTES = 48 * 1024 * 1024

bf16 = jnp.bfloat16
f32 = jnp.float32


def round_up(n, m):
    return -(-n // m) * m


def stat_rows(units):
    return round_up(3 * round_up(units, 8), 16)


def pad_rows(x, rows):
    if x.shape[0] == rows:
        return x
    return jnp.concatenate([x, jnp.zeros((rows - x.shape[0], x.shape[1]), x.dtype)], axis=0)


def columns_to_rows(columns, unit):
    lane = lax.broadcasted_iota(jnp.int32, (unit, LANES), 1)
    square = jnp.zeros((unit, LANES), f32)
    for place, column in columns:
        square = jnp.where(lane == place, column, square)
    return jnp.transpose(pad_rows(square, LANES))


def split_total(total):
    high = total.astype(bf16)
    return high, (total - high.astype(f32)).astype(bf16)


def write_message(out_ref, row, shift, total):
    high, low = split_total(total)
    rows = jnp.concatenate([shift, high.astype(f32), low.astype(f32)], axis=0)
    out_ref[row : row + stat_rows(shift.shape[0]), :] = pad_rows(
        rows, stat_rows(shift.shape[0])
    ).astype(bf16)


def row_of(place, local_rows, core):
    return place + jnp.where(place < local_rows, core, -core) * local_rows


def attend_kernel(rel, unit_rows, split, as_message, n_after, scal, q_ref, *rest):
    caches = rest[: 2 * split]
    d_ref = rest[2 * split]
    outs = rest[2 * split + 1 + n_after :]
    units, heads = q_ref.shape[:2]
    unit = unit_rows * GROUP
    keys = caches[0].shape[0]
    seq, length = lax.axis_index("seq"), scal[0:1, 0:1]
    chip = lax.div(seq, split)
    count = units * heads
    count8 = round_up(count, 8)
    step = max(n for n in range(1, units + 1) if units % n == 0 and n * unit <= 384)
    columns = []
    out_ref = outs[0]
    key_index = lax.broadcasted_iota(jnp.int32, (1, keys), 1)
    core = lax.rem(seq, split)
    local_rows = unit_rows // split
    ones = jnp.ones((keys, LANES), bf16)
    draft = lax.broadcasted_iota(jnp.int32, (1, LANES), 1)
    draft_row = unit_rows * chip + row_of(draft, local_rows, core)
    unit_row = row_of(
        lax.shift_right_logical(lax.broadcasted_iota(jnp.int32, (unit, LANES), 0), 3),
        local_rows,
        core,
    )
    def lanes_of(head, side):
        if side == 0:
            return slice(head * HD, (head + 1) * HD)
        return pl.ds(pl.multiple_of((core * heads + head) * HD, HD), HD)

    def score_of(chunk):
        head, start, side = chunk
        queries = q_ref[start : start + step, head].reshape(step * unit, HD)
        return lax.dot_general(
            queries, caches[2 * side][:, lanes_of(head, side)], (((1,), (1,)), ((), ())), preferred_element_type=f32
        )

    chunks = [
        (head, start, side)
        for head in range(heads)
        for start in range(0, units, step)
        for side in range(split)
    ]
    tops, sums = [], []
    following = score_of(chunks[0])
    for at, (head, start, side) in enumerate(chunks):
        raw = following
        if at + 1 < len(chunks):
            following = score_of(chunks[at + 1])
        draft_values = jnp.concatenate([d_ref[head, LANES:], ones[:LANES]], axis=1)
        if side == 0:
            time = jnp.concatenate(
                [
                    unit_row + unit_rows * jnp.bitwise_xor(chip, rel[start + n])
                    for n in range(step)
                ],
                axis=0,
            )
            draft_scores = lax.dot_general(
                q_ref[start : start + step, head].reshape(step * unit, HD),
                d_ref[head, :LANES],
                (((1,), (1,)), ((), ())),
                preferred_element_type=f32,
            )
            draft_scores = jnp.where(draft_row <= time, draft_scores * LOG2_SCALE, DEAD)
        block = seq if side == 0 else seq + 1 - 2 * core
        score = jnp.where(key_index + block * keys < length, raw * LOG2_SCALE, DEAD)
        inside = (draft >= side * local_rows) & (draft < (side + 1) * local_rows)
        own_drafts = jnp.where(inside, draft_scores, DEAD)
        top = jnp.maximum(
            jnp.max(score, axis=1, keepdims=True), jnp.max(own_drafts, axis=1, keepdims=True)
        )
        top = jnp.maximum(top, FLOOR)
        tops.append(top)
        values_ones = jnp.concatenate(
            [caches[2 * side + 1][:, lanes_of(head, side)], ones], axis=1
        )
        sums.append(
            jnp.dot(jnp.exp2(score - top).astype(bf16), values_ones, preferred_element_type=f32)
            + jnp.dot(
                jnp.exp2(own_drafts - top).astype(bf16), draft_values, preferred_element_type=f32
            )
        )
        if side + 1 < split:
            continue
        shift = functools.reduce(jnp.maximum, tops).astype(bf16).astype(f32)
        both = sum(part * jnp.exp2(top - shift) for part, top in zip(sums, tops))
        weighted, total = both[:, :HD], both[:, HD : HD + 1]
        for n in range(step):
            place = (start + n) * heads + head
            part = slice(n * unit, (n + 1) * unit)
            out_ref[place * unit : (place + 1) * unit, :] = weighted[part].astype(out_ref.dtype)
            columns.append((place, shift[part]))
            columns.append((count8 + place, total[part]))
        tops, sums = [], []
    stats = columns_to_rows(columns, unit)
    if as_message:
        write_message(out_ref, count * unit, stats[:count8], stats[count8 : 2 * count8])
    else:
        outs[1][...] = stats[: 2 * count8]


def attend(scal, q, rel, unit_rows, split, caches, drafts, as_message, after=()):
    units, heads = q.shape[:2]
    unit = unit_rows * GROUP
    keys = caches[0].shape[0]
    count = units * heads
    if as_message:
        out_shape = (jax.ShapeDtypeStruct((count * unit + stat_rows(count), LANES), bf16),)
    else:
        out_shape = (
            jax.ShapeDtypeStruct((count * unit, LANES), f32),
            jax.ShapeDtypeStruct((2 * round_up(count, 8), LANES), f32),
        )
    whole = pl.BlockSpec(memory_space=pltpu.VMEM)
    in_specs = [whole] * (3 + len(caches))
    in_specs += [pl.BlockSpec(memory_space=pl.ANY)] * len(after)
    scores = count * unit * (split * keys + LANES)
    return pl.pallas_call(
        functools.partial(attend_kernel, rel, unit_rows, split, as_message, len(after)),
        in_specs=in_specs,
        out_specs=(whole,) * len(out_shape),
        out_shape=out_shape,
        compiler_params=pltpu.CompilerParams(vmem_limit_bytes=VMEM_BYTES),
        cost_estimate=pl.CostEstimate(
            flops=4 * scores * HD, bytes_accessed=4 * split * keys * heads * HD, transcendentals=scores
        ),
    )(scal, q, *caches, drafts, *after)


def merge_kernel(unit, mode, num_ref, stat_ref, msg_ref, *outs):
    rows = num_ref.shape[0]
    count = rows // unit
    count8 = stat_ref.shape[0] // 2
    own_shift, own_total = stat_ref[:count8], stat_ref[count8:]
    sent = msg_ref[rows:, :].astype(f32)
    shift = sent[:count8]
    total = sent[count8 : 2 * count8] + sent[2 * count8 : 3 * count8]
    half = count // 2
    if mode == "final":
        shift = pad_rows(jnp.concatenate([shift[half:count], shift[:half]], axis=0), count8)
        total = pad_rows(jnp.concatenate([total[half:count], total[:half]], axis=0), count8)
    new_shift = jnp.maximum(own_shift, shift)
    own_factor = jnp.exp2(own_shift - new_shift)
    factor = jnp.exp2(shift - new_shift)
    new_total = own_total * own_factor + total * factor
    if mode == "final":
        new_total = jnp.where(new_total > 0, new_total, 1.0)
        own_factor = own_factor / new_total
        factor = factor / new_total
    factors = jnp.transpose(pad_rows(jnp.concatenate([own_factor, factor], axis=0), LANES))
    for n in range(count):
        source = (n + half) % count if mode == "final" else n
        merged = num_ref[n * unit : (n + 1) * unit, :] * factors[:unit, n : n + 1]
        merged = merged + (
            msg_ref[source * unit : (source + 1) * unit, :].astype(f32)
            * factors[:unit, count8 + n : count8 + n + 1]
        )
        here = slice(n * unit, (n + 1) * unit)
        if mode == "final":
            outs[0][here, :] = merged.astype(bf16)
        elif mode == "all":
            outs[0][here, :] = merged
            outs[2][here, :] = merged.astype(bf16)
        elif n < half:
            outs[0][here, :] = merged
        else:
            outs[2][(n - half) * unit : (n - half + 1) * unit, :] = merged.astype(bf16)
    if mode == "all":
        outs[1][...] = jnp.concatenate([new_shift, new_total], axis=0)
        write_message(outs[2], rows, new_shift, new_total)
    elif mode == "half":
        half8 = round_up(half, 8)
        outs[1][...] = jnp.concatenate(
            [pad_rows(new_shift[:half], half8), pad_rows(new_total[:half], half8)], axis=0
        )
        write_message(
            outs[2],
            half * unit,
            pad_rows(new_shift[half:count], half8),
            pad_rows(new_total[half:count], half8),
        )


def merge(unit, mode, num, stats, message):
    rows = num.shape[0]
    if mode == "final":
        out_shape = jax.ShapeDtypeStruct((rows, LANES), bf16)
    else:
        rows = rows // 2 if mode == "half" else rows
        count = rows // unit
        out_shape = (
            jax.ShapeDtypeStruct((rows, LANES), f32),
            jax.ShapeDtypeStruct((2 * round_up(count, 8), LANES), f32),
            jax.ShapeDtypeStruct((rows + stat_rows(count), LANES), bf16),
        )
    return pl.pallas_call(
        functools.partial(merge_kernel, unit, mode),
        out_shape=out_shape,
        compiler_params=pltpu.CompilerParams(vmem_limit_bytes=VMEM_BYTES),
    )(num, stats, message)


def project_kernel(rel, split, n_head, parts, n_partial, *refs):
    sources, w_ref = refs[: len(parts)], refs[len(parts)]
    partial = refs[len(parts) + 1 : len(parts) + 1 + n_partial]
    outs, (rows_ref, lhs_ref) = refs[len(parts) + 1 + n_partial : -2], refs[-2:]
    seq, head = lax.axis_index("seq"), lax.axis_index("head")
    chip = lax.div(seq, split)
    core = lax.rem(seq, split)
    units, heads, unit, _ = sources[0].shape
    chips = 2 * units
    piece = unit // split
    first = head * (chips // n_head) if n_head == 2 else 0
    slots = rows_ref.shape[0] // heads
    if len(parts) < 2 * slots:
        rows_ref[...] = jnp.zeros_like(rows_ref)
    for (side, part), x_ref in zip(parts, sources):
        owner = core if side == 0 else 1 - core
        slot = owner if slots == split else 0
        for n in range(units):
            place = lax.rem(jnp.bitwise_xor(chip, rel[part][n]) - first + chips, chips)
            for part_of in range(split):
                row = place * unit + (owner if part_of == 0 else 1 - owner) * piece
                for h in range(heads):
                    rows_ref[slot * heads + h, pl.ds(pl.multiple_of(row, 16), piece), :] = x_ref[
                        n, h, part_of * piece : (part_of + 1) * piece
                    ].astype(f32)
    rows, depth = lhs_ref.shape
    for kv in range(rows_ref.shape[0]):
        for g in range(GROUP):
            lanes = slice((kv * GROUP + g) * HD, (kv * GROUP + g + 1) * HD)
            lhs_ref[:, lanes] = rows_ref[kv, pl.ds(g, rows, stride=GROUP), :].astype(bf16)
    if slots == split:
        weight = w_ref[...]
    else:
        weight = w_ref[pl.ds(pl.multiple_of((1 - core) * depth, LANES), depth), :]
    result = jnp.dot(lhs_ref[...], weight, preferred_element_type=f32)
    for ref in partial:
        result = result + ref[...]
    if len(outs) == 2:
        outs[0][...] = result[: rows // 2]
        outs[1][...] = result[rows // 2 :].astype(bf16)
    else:
        outs[0][...] = result


def project(rel, split, n_head, parts, sources, weight, partial=(), whole=False):
    units, heads, unit, _ = sources[0].shape
    slots = 1 if partial else split
    rows = 2 * units * unit // GROUP
    columns = weight.shape[1]
    if n_head == 2 and whole:
        out_shape = tuple(jax.ShapeDtypeStruct((rows // 2, columns), t) for t in (f32, bf16))
    else:
        out_shape = (jax.ShapeDtypeStruct((rows, columns), f32),)
    return pl.pallas_call(
        functools.partial(project_kernel, rel, split, n_head, parts, len(partial)),
        in_specs=[pl.BlockSpec(memory_space=pltpu.VMEM)] * (len(sources) + 1 + len(partial)),
        out_shape=out_shape,
        scratch_shapes=[
            pltpu.VMEM((heads * slots, 2 * units * unit, LANES), f32),
            pltpu.VMEM((rows, heads * slots * GROUP * HD), bf16),
        ],
        compiler_params=pltpu.CompilerParams(vmem_limit_bytes=VMEM_BYTES),
        cost_estimate=pl.CostEstimate(
            flops=2 * rows * columns * heads * slots * GROUP * HD,
            bytes_accessed=2 * columns * heads * slots * GROUP * HD,
            transcendentals=0,
        ),
    )(*sources, weight, *partial)


def drafts_kernel(split, *refs):
    sources, (draft_ref, unit_ref, rows_ref) = refs[:-3], refs[-3:]
    rows, half = sources[0].shape
    width = 2 * half
    heads = draft_ref.shape[0]
    core = lax.rem(lax.axis_index("seq"), split)
    rows_ref[...] = jnp.zeros_like(rows_ref)
    for n in range(split):
        rows_ref[n * rows : (n + 1) * rows, :half] = sources[2 * n][...].astype(f32)
        rows_ref[n * rows : (n + 1) * rows, half:] = sources[2 * n + 1][...].astype(f32)
    unit_rows = rows * split
    for h in range(heads):
        for n in range(2):
            lanes = pl.ds(pl.multiple_of(n * (width // 2) + (core * heads + h) * HD, HD), HD)
            draft_ref[h, n * LANES : (n + 1) * LANES, :] = rows_ref[:, lanes].astype(bf16)
        chip_rows = jnp.concatenate(
            [
                rows_ref[
                    :unit_rows,
                    pl.ds(pl.multiple_of(n * (width // 2) + (core * heads + h) * HD, HD), HD),
                ]
                for n in range(2)
            ],
            axis=0,
        )
        unit_ref[h] = pad_rows(chip_rows, unit_ref.shape[1]).astype(bf16)


def chip_drafts(split, heads, sources):
    rows, half = sources[0].shape
    return pl.pallas_call(
        functools.partial(drafts_kernel, split),
        in_specs=[pl.BlockSpec(memory_space=pltpu.VMEM)] * len(sources),
        out_shape=(
            jax.ShapeDtypeStruct((heads, 2 * LANES, HD), bf16),
            jax.ShapeDtypeStruct((heads, round_up(2 * rows * split, 8), HD), bf16),
        ),
        scratch_shapes=[pltpu.VMEM((LANES, 2 * half), f32)],
        compiler_params=pltpu.CompilerParams(vmem_limit_bytes=VMEM_BYTES),
    )(*sources)


def append_kernel(rel, split, unit_rows, scal, ck_ref, cv_ref, mine_ref, other_ref, *rest):
    nk_ref, nv_ref = rest[-2:]
    rows, width = ck_ref.shape
    chips, heads, both, _ = mine_ref.shape
    local_rows = unit_rows // split
    seq = lax.axis_index("seq")
    chip, core = lax.div(seq, split), lax.rem(seq, split)
    length, accepted = jnp.max(scal[0:1]), jnp.max(scal[1:2])
    first = (seq * pl.num_programs(0) + pl.program_id(0)) * rows - length
    touched = (first < accepted) & (first + rows > 0)

    @pl.when(jnp.logical_not(touched))
    def _():
        nk_ref[...] = ck_ref[...]
        nv_ref[...] = cv_ref[...]

    @pl.when(touched)
    def _():
        depth = chips * both
        place = first + lax.broadcasted_iota(jnp.int32, (rows, depth), 0)
        lane = lax.broadcasted_iota(jnp.int32, (1, depth), 1)
        base = jnp.zeros((1, depth), jnp.int32)
        row = lane
        for n in range(chips):
            here = (lane >= n * both) & (lane < (n + 1) * both)
            base = jnp.where(here, jnp.bitwise_xor(chip, rel[n]) * unit_rows, base)
            row = jnp.where(here, lane - n * both, row)
        chosen = first + lax.broadcasted_iota(jnp.int32, (rows, HD), 0)
        chosen = (chosen >= 0) & (chosen < accepted)
        for side in range(split):
            drafts = mine_ref if side == 0 else other_ref
            source_core = core if side == 0 else 1 - core
            values = [
                drafts[:, h].astype(f32).reshape(depth, HD).astype(bf16) for h in range(heads)
            ]
            for cache_ref, new_ref, start in ((ck_ref, nk_ref, 0), (cv_ref, nv_ref, unit_rows)):
                source = base + row_of(row - start, local_rows, source_core)
                source = jnp.where((row >= start) & (row < start + unit_rows), source, -(1 << 24))
                pick = jnp.where(source == place, 1.0, 0.0).astype(bf16)
                for h in range(heads):
                    lanes = pl.ds(pl.multiple_of((source_core * heads + h) * HD, HD), HD)
                    moved = jnp.dot(pick, values[h], preferred_element_type=f32)
                    new_ref[:, lanes] = jnp.where(
                        chosen, moved, cache_ref[:, lanes].astype(f32)
                    ).astype(bf16)


def append(rel, split, unit_rows, scal, ck, cv, drafts, after):
    rows = ck.shape[0]
    block = rows // 4 if rows % 64 == 0 else rows
    cache_spec = pl.BlockSpec((block, ck.shape[1]), lambda i: (i, 0))
    mine, other = drafts[0], drafts[-1]
    draft_spec = pl.BlockSpec(mine.shape, lambda i: (0, 0, 0, 0))
    shape = jax.ShapeDtypeStruct(ck.shape, bf16)
    return pl.pallas_call(
        functools.partial(append_kernel, rel, split, unit_rows),
        grid=(rows // block,),
        in_specs=[pl.BlockSpec(memory_space=pltpu.VMEM)]
        + [cache_spec, cache_spec, draft_spec, draft_spec]
        + [pl.BlockSpec(memory_space=pl.ANY)] * len(after),
        out_specs=(cache_spec, cache_spec),
        out_shape=(shape, shape),
        compiler_params=pltpu.CompilerParams(vmem_limit_bytes=VMEM_BYTES),
        cost_estimate=pl.CostEstimate(flops=0, bytes_accessed=8 * ck.size, transcendentals=0),
    )(scal, ck, cv, mine, other, *after)


def one_request(n_seq, n_head, dq, dk, dv, ck, cv, accepted, length, weight):
    seq = lax.axis_index("seq")
    local_rows = dq.shape[0]
    heads_kv = dk.shape[1] // HD
    split = 2 if heads_kv % 2 == 0 else 1
    heads = heads_kv // split
    unit_rows = local_rows * split
    unit = unit_rows * GROUP
    n_bits = n_seq.bit_length() - 1
    bits = list(range(n_bits - 1, split - 2, -1))

    def swap(x, bit):
        return lax.ppermute(x, "seq", [(i, i ^ (1 << bit)) for i in range(n_seq)])

    core = seq % split

    q4 = dq.reshape(local_rows, heads_kv, GROUP, LANES).transpose(1, 0, 2, 3)
    q4 = q4.reshape(heads_kv, local_rows * GROUP, LANES)
    drafts_own = [dk, dv]
    caches, drafts_other = [ck, cv], []
    q = q4
    if split == 2:
        mine = lax.dynamic_slice_in_dim(q4, core * heads, heads, 0)
        sent = lax.dynamic_slice_in_dim(q4, (1 - core) * heads, heads, 0)
        q = jnp.concatenate([mine, swap(sent, 0)], axis=1)
    q, scal = lax.optimization_barrier(
        (q[None], jnp.broadcast_to(jnp.stack([length, accepted]), (2, LANES)))
    )
    if split == 2:
        q, drafts_own, *late = lax.optimization_barrier((q, drafts_own, ck, cv))
        drafts_other = [swap(d, 0) for d in drafts_own]
        caches += [swap(c, 0) for c in late]

    rel, near = [0], bits[-1]
    for bit in bits[:-1]:
        new = swap(q, bit)
        q = jnp.concatenate([q, new], axis=0)
        if split == 2 and bit == bits[0]:
            q, drafts_own, drafts_other, *own = lax.optimization_barrier(
                (q, drafts_own, drafts_other, ck, cv)
            )
            caches[:2] = [
                lax.dynamic_slice_in_dim(c, core * heads * HD, heads * HD, 1) for c in own
            ]
        rel = rel + [r | (1 << bit) // split for r in rel]
    drafts, chip_rows = chip_drafts(split, heads, [*drafts_own, *drafts_other])
    rel_far = [r | (1 << near) // split for r in rel]
    q_far = swap(q, near)

    run = functools.partial(attend, scal)
    (message,) = run(q, rel, unit_rows, split, caches, drafts, True)
    num, stats = run(q_far, rel_far, unit_rows, split, caches, drafts, False, (message,))
    message = swap(message, near)

    dkv, order = chip_rows[None], [0]

    for bit in reversed(bits[:-1]):
        mode = "all" if bit == bits[0] else "half"
        num, stats, message = merge(unit, mode, num, stats, message)
        if bit in (bits[-2], bits[0]):
            num, dkv = lax.optimization_barrier((num, dkv))
            for late in bits[-2:-1] if bit == bits[-2] else bits[:-2]:
                dkv = jnp.concatenate([dkv, swap(dkv, late)], axis=0)
                order = order + [r ^ (1 << late) // split for r in order]
        message = swap(message, bit)

    att = merge(unit, "final", num, stats, message).reshape(-1, heads, unit, LANES)
    for bit in bits[1:-1]:
        att = jnp.concatenate([att, swap(att, bit)], axis=0)
    att, dkv = lax.optimization_barrier((att, dkv))
    att_near = swap(att, near)
    dkv = jnp.concatenate([dkv, swap(dkv, near)], axis=0)
    order = order + [r ^ (1 << near) // split for r in order]
    halves = (rel_far, rel)
    if split == 2:
        begun = project(
            halves,
            split,
            n_head,
            ((0, 0), (0, 1), (1, 0)),
            [att, att_near, swap(att, 0)],
            weight,
        )
        begun, dkv = lax.optimization_barrier((begun, dkv))
        result = project(
            halves, split, n_head, ((1, 1),), [swap(att_near, 0)], weight, begun, True
        )
    else:
        result = project(
            halves, split, n_head, ((0, 0), (0, 1)), [att, att_near], weight, (), True
        )
    if n_head == 2:
        keep, send = result
        projected = keep + lax.ppermute(send, "head", [(0, 1), (1, 0)]).astype(f32)
    else:
        projected = lax.psum_scatter(result[0], "head", scatter_dimension=0, tiled=True)
    every = [dkv, swap(dkv, 0)] if split == 2 else [dkv]
    new_key, new_value = append(
        order, split, unit_rows, scal, ck, cv, every, (result[-1],)
    )
    return projected.astype(bf16), new_key, new_value


def on_device(n_seq, n_head, dq, dk, dv, ck, cv, accepted, cache_len, weight):
    results = [
        one_request(
            n_seq, n_head, dq[r], dk[r], dv[r], ck[r], cv[r], accepted[r : r + 1], cache_len[r : r + 1], weight
        )
        for r in range(dq.shape[0])
    ]
    return tuple(jnp.stack(parts) for parts in zip(*results))


def solution(mesh):
    in_specs = (
        P(None, "seq", "head"),
        P(None, "seq", "head"),
        P(None, "seq", "head"),
        P(None, "seq", "head"),
        P(None, "seq", "head"),
        P(),
        P(),
        P("head", "seq"),
    )
    out_specs = (P(None, "head", "seq"), P(None, "seq", "head"), P(None, "seq", "head"))
    return jax.shard_map(
        functools.partial(on_device, mesh.shape["seq"], mesh.shape["head"]),
        mesh=mesh,
        in_specs=in_specs,
        out_specs=out_specs,
        check_vma=False,
    )
```

```python
import functools
import math

import jax
import jax.numpy as jnp
from jax import lax
from jax.experimental import pallas as pl
from jax.experimental.pallas import tpu as pltpu
from jax.sharding import PartitionSpec as P

QH = 64
KVH = 8
HD = 128
GROUP = QH // KVH
LANES = 128

DEAD = -1e30
FLOOR = -(2.0**96)
LOG2_SCALE = math.log2(math.e) / math.sqrt(HD)
VMEM_BYTES = 48 * 1024 * 1024

bf16 = jnp.bfloat16
f32 = jnp.float32


def round_up(n, m):
    return -(-n // m) * m


def stat_rows(units):
    return round_up(3 * round_up(units, 8), 16)


def pad_rows(x, rows):
    if x.shape[0] == rows:
        return x
    return jnp.concatenate([x, jnp.zeros((rows - x.shape[0], x.shape[1]), x.dtype)], axis=0)


def columns_to_rows(columns, unit):
    lane = lax.broadcasted_iota(jnp.int32, (unit, LANES), 1)
    square = jnp.zeros((unit, LANES), f32)
    for place, column in columns:
        square = jnp.where(lane == place, column, square)
    return jnp.transpose(pad_rows(square, LANES))


def split_total(total):
    high = total.astype(bf16)
    return high, (total - high.astype(f32)).astype(bf16)


def write_message(out_ref, row, shift, total):
    high, low = split_total(total)
    rows = jnp.concatenate([shift, high.astype(f32), low.astype(f32)], axis=0)
    out_ref[row : row + stat_rows(shift.shape[0]), :] = pad_rows(
        rows, stat_rows(shift.shape[0])
    ).astype(bf16)


def row_of(place, local_rows, core):
    return place + jnp.where(place < local_rows, core, -core) * local_rows


def attend_kernel(rel, unit_rows, split, as_message, n_after, scal, q_ref, *rest):
    caches = rest[: 2 * split]
    d_ref = rest[2 * split]
    outs = rest[2 * split + 1 + n_after :]
    units, heads = q_ref.shape[:2]
    unit = unit_rows * GROUP
    keys = caches[0].shape[0]
    seq, length = lax.axis_index("seq"), scal[0:1, 0:1]
    chip = lax.div(seq, split)
    count = units * heads
    count8 = round_up(count, 8)
    step = max(n for n in range(1, units + 1) if units % n == 0 and n * unit <= 384)
    columns = []
    out_ref = outs[0]
    key_index = lax.broadcasted_iota(jnp.int32, (1, keys), 1)
    core = lax.rem(seq, split)
    local_rows = unit_rows // split
    ones = jnp.ones((keys, LANES), bf16)
    draft = lax.broadcasted_iota(jnp.int32, (1, LANES), 1)
    draft_row = unit_rows * chip + row_of(draft, local_rows, core)
    unit_row = row_of(
        lax.shift_right_logical(lax.broadcasted_iota(jnp.int32, (unit, LANES), 0), 3),
        local_rows,
        core,
    )
    def lanes_of(head, side):
        if side == 0:
            return slice(head * HD, (head + 1) * HD)
        return pl.ds(pl.multiple_of((core * heads + head) * HD, HD), HD)

    def score_of(chunk):
        head, start, side = chunk
        queries = q_ref[start : start + step, head].reshape(step * unit, HD)
        return lax.dot_general(
            queries, caches[2 * side][:, lanes_of(head, side)], (((1,), (1,)), ((), ())), preferred_element_type=f32
        )

    chunks = [
        (head, start, side)
        for head in range(heads)
        for start in range(0, units, step)
        for side in range(split)
    ]
    tops, sums = [], []
    following = score_of(chunks[0])
    for at, (head, start, side) in enumerate(chunks):
        raw = following
        if at + 1 < len(chunks):
            following = score_of(chunks[at + 1])
        draft_values = jnp.concatenate([d_ref[head, LANES:], ones[:LANES]], axis=1)
        if side == 0:
            time = jnp.concatenate(
                [
                    unit_row + unit_rows * jnp.bitwise_xor(chip, rel[start + n])
                    for n in range(step)
                ],
                axis=0,
            )
            draft_scores = lax.dot_general(
                q_ref[start : start + step, head].reshape(step * unit, HD),
                d_ref[head, :LANES],
                (((1,), (1,)), ((), ())),
                preferred_element_type=f32,
            )
            draft_scores = jnp.where(draft_row <= time, draft_scores * LOG2_SCALE, DEAD)
        block = seq if side == 0 else seq + 1 - 2 * core
        score = jnp.where(key_index + block * keys < length, raw * LOG2_SCALE, DEAD)
        inside = (draft >= side * local_rows) & (draft < (side + 1) * local_rows)
        own_drafts = jnp.where(inside, draft_scores, DEAD)
        top = jnp.maximum(
            jnp.max(score, axis=1, keepdims=True), jnp.max(own_drafts, axis=1, keepdims=True)
        )
        top = jnp.maximum(top, FLOOR)
        tops.append(top)
        values_ones = jnp.concatenate(
            [caches[2 * side + 1][:, lanes_of(head, side)], ones], axis=1
        )
        sums.append(
            jnp.dot(jnp.exp2(score - top).astype(bf16), values_ones, preferred_element_type=f32)
            + jnp.dot(
                jnp.exp2(own_drafts - top).astype(bf16), draft_values, preferred_element_type=f32
            )
        )
        if side + 1 < split:
            continue
        shift = functools.reduce(jnp.maximum, tops).astype(bf16).astype(f32)
        both = sum(part * jnp.exp2(top - shift) for part, top in zip(sums, tops))
        weighted, total = both[:, :HD], both[:, HD : HD + 1]
        for n in range(step):
            place = (start + n) * heads + head
            part = slice(n * unit, (n + 1) * unit)
            out_ref[place * unit : (place + 1) * unit, :] = weighted[part].astype(out_ref.dtype)
            columns.append((place, shift[part]))
            columns.append((count8 + place, total[part]))
        tops, sums = [], []
    stats = columns_to_rows(columns, unit)
    if as_message:
        write_message(out_ref, count * unit, stats[:count8], stats[count8 : 2 * count8])
    else:
        outs[1][...] = stats[: 2 * count8]


def attend(scal, q, rel, unit_rows, split, caches, drafts, as_message, after=()):
    units, heads = q.shape[:2]
    unit = unit_rows * GROUP
    keys = caches[0].shape[0]
    count = units * heads
    if as_message:
        out_shape = (jax.ShapeDtypeStruct((count * unit + stat_rows(count), LANES), bf16),)
    else:
        out_shape = (
            jax.ShapeDtypeStruct((count * unit, LANES), f32),
            jax.ShapeDtypeStruct((2 * round_up(count, 8), LANES), f32),
        )
    whole = pl.BlockSpec(memory_space=pltpu.VMEM)
    in_specs = [whole] * (3 + len(caches))
    in_specs += [pl.BlockSpec(memory_space=pl.ANY)] * len(after)
    scores = count * unit * (split * keys + LANES)
    return pl.pallas_call(
        functools.partial(attend_kernel, rel, unit_rows, split, as_message, len(after)),
        in_specs=in_specs,
        out_specs=(whole,) * len(out_shape),
        out_shape=out_shape,
        compiler_params=pltpu.CompilerParams(vmem_limit_bytes=VMEM_BYTES),
        cost_estimate=pl.CostEstimate(
            flops=4 * scores * HD, bytes_accessed=4 * split * keys * heads * HD, transcendentals=scores
        ),
    )(scal, q, *caches, drafts, *after)


def merge_kernel(unit, mode, num_ref, stat_ref, msg_ref, *outs):
    rows = num_ref.shape[0]
    count = rows // unit
    count8 = stat_ref.shape[0] // 2
    own_shift, own_total = stat_ref[:count8], stat_ref[count8:]
    sent = msg_ref[rows:, :].astype(f32)
    shift = sent[:count8]
    total = sent[count8 : 2 * count8] + sent[2 * count8 : 3 * count8]
    half = count // 2
    if mode == "final":
        shift = pad_rows(jnp.concatenate([shift[half:count], shift[:half]], axis=0), count8)
        total = pad_rows(jnp.concatenate([total[half:count], total[:half]], axis=0), count8)
    new_shift = jnp.maximum(own_shift, shift)
    own_factor = jnp.exp2(own_shift - new_shift)
    factor = jnp.exp2(shift - new_shift)
    new_total = own_total * own_factor + total * factor
    if mode == "final":
        new_total = jnp.where(new_total > 0, new_total, 1.0)
        own_factor = own_factor / new_total
        factor = factor / new_total
    factors = jnp.transpose(pad_rows(jnp.concatenate([own_factor, factor], axis=0), LANES))
    for n in range(count):
        source = (n + half) % count if mode == "final" else n
        merged = num_ref[n * unit : (n + 1) * unit, :] * factors[:unit, n : n + 1]
        merged = merged + (
            msg_ref[source * unit : (source + 1) * unit, :].astype(f32)
            * factors[:unit, count8 + n : count8 + n + 1]
        )
        here = slice(n * unit, (n + 1) * unit)
        if mode == "final":
            outs[0][here, :] = merged.astype(bf16)
        elif mode == "all":
            outs[0][here, :] = merged
            outs[2][here, :] = merged.astype(bf16)
        elif n < half:
            outs[0][here, :] = merged
        else:
            outs[2][(n - half) * unit : (n - half + 1) * unit, :] = merged.astype(bf16)
    if mode == "all":
        outs[1][...] = jnp.concatenate([new_shift, new_total], axis=0)
        write_message(outs[2], rows, new_shift, new_total)
    elif mode == "half":
        half8 = round_up(half, 8)
        outs[1][...] = jnp.concatenate(
            [pad_rows(new_shift[:half], half8), pad_rows(new_total[:half], half8)], axis=0
        )
        write_message(
            outs[2],
            half * unit,
            pad_rows(new_shift[half:count], half8),
            pad_rows(new_total[half:count], half8),
        )


def merge(unit, mode, num, stats, message):
    rows = num.shape[0]
    if mode == "final":
        out_shape = jax.ShapeDtypeStruct((rows, LANES), bf16)
    else:
        rows = rows // 2 if mode == "half" else rows
        count = rows // unit
        out_shape = (
            jax.ShapeDtypeStruct((rows, LANES), f32),
            jax.ShapeDtypeStruct((2 * round_up(count, 8), LANES), f32),
            jax.ShapeDtypeStruct((rows + stat_rows(count), LANES), bf16),
        )
    return pl.pallas_call(
        functools.partial(merge_kernel, unit, mode),
        out_shape=out_shape,
        compiler_params=pltpu.CompilerParams(vmem_limit_bytes=VMEM_BYTES),
    )(num, stats, message)


def project_kernel(rel, split, n_head, parts, n_partial, *refs):
    sources, w_ref = refs[: len(parts)], refs[len(parts)]
    partial = refs[len(parts) + 1 : len(parts) + 1 + n_partial]
    outs, (rows_ref, lhs_ref) = refs[len(parts) + 1 + n_partial : -2], refs[-2:]
    seq, head = lax.axis_index("seq"), lax.axis_index("head")
    chip = lax.div(seq, split)
    core = lax.rem(seq, split)
    units, heads, unit, _ = sources[0].shape
    chips = 2 * units
    piece = unit // split
    first = head * (chips // n_head) if n_head == 2 else 0
    slots = rows_ref.shape[0] // heads
    if len(parts) < 2 * slots:
        rows_ref[...] = jnp.zeros_like(rows_ref)
    for (side, part), x_ref in zip(parts, sources):
        owner = core if side == 0 else 1 - core
        slot = owner if slots == split else 0
        for n in range(units):
            place = lax.rem(jnp.bitwise_xor(chip, rel[part][n]) - first + chips, chips)
            for part_of in range(split):
                row = place * unit + (owner if part_of == 0 else 1 - owner) * piece
                for h in range(heads):
                    rows_ref[slot * heads + h, pl.ds(pl.multiple_of(row, 16), piece), :] = x_ref[
                        n, h, part_of * piece : (part_of + 1) * piece
                    ].astype(f32)
    rows, depth = lhs_ref.shape
    for kv in range(rows_ref.shape[0]):
        for g in range(GROUP):
            lanes = slice((kv * GROUP + g) * HD, (kv * GROUP + g + 1) * HD)
            lhs_ref[:, lanes] = rows_ref[kv, pl.ds(g, rows, stride=GROUP), :].astype(bf16)
    if slots == split:
        weight = w_ref[...]
    else:
        weight = w_ref[pl.ds(pl.multiple_of((1 - core) * depth, LANES), depth), :]
    result = jnp.dot(lhs_ref[...], weight, preferred_element_type=f32)
    for ref in partial:
        result = result + ref[...]
    if len(outs) == 2:
        outs[0][...] = result[: rows // 2]
        outs[1][...] = result[rows // 2 :].astype(bf16)
    else:
        outs[0][...] = result


def project(rel, split, n_head, parts, sources, weight, partial=(), whole=False):
    units, heads, unit, _ = sources[0].shape
    slots = 1 if partial else split
    rows = 2 * units * unit // GROUP
    columns = weight.shape[1]
    if n_head == 2 and whole:
        out_shape = tuple(jax.ShapeDtypeStruct((rows // 2, columns), t) for t in (f32, bf16))
    else:
        out_shape = (jax.ShapeDtypeStruct((rows, columns), f32),)
    return pl.pallas_call(
        functools.partial(project_kernel, rel, split, n_head, parts, len(partial)),
        in_specs=[pl.BlockSpec(memory_space=pltpu.VMEM)] * (len(sources) + 1 + len(partial)),
        out_shape=out_shape,
        scratch_shapes=[
            pltpu.VMEM((heads * slots, 2 * units * unit, LANES), f32),
            pltpu.VMEM((rows, heads * slots * GROUP * HD), bf16),
        ],
        compiler_params=pltpu.CompilerParams(vmem_limit_bytes=VMEM_BYTES),
        cost_estimate=pl.CostEstimate(
            flops=2 * rows * columns * heads * slots * GROUP * HD,
            bytes_accessed=2 * columns * heads * slots * GROUP * HD,
            transcendentals=0,
        ),
    )(*sources, weight, *partial)


def drafts_kernel(split, *refs):
    sources, (draft_ref, unit_ref, rows_ref) = refs[:-3], refs[-3:]
    rows, half = sources[0].shape
    width = 2 * half
    heads = draft_ref.shape[0]
    core = lax.rem(lax.axis_index("seq"), split)
    rows_ref[...] = jnp.zeros_like(rows_ref)
    for n in range(split):
        rows_ref[n * rows : (n + 1) * rows, :half] = sources[2 * n][...].astype(f32)
        rows_ref[n * rows : (n + 1) * rows, half:] = sources[2 * n + 1][...].astype(f32)
    unit_rows = rows * split
    for h in range(heads):
        for n in range(2):
            lanes = pl.ds(pl.multiple_of(n * (width // 2) + (core * heads + h) * HD, HD), HD)
            draft_ref[h, n * LANES : (n + 1) * LANES, :] = rows_ref[:, lanes].astype(bf16)
        chip_rows = jnp.concatenate(
            [
                rows_ref[
                    :unit_rows,
                    pl.ds(pl.multiple_of(n * (width // 2) + (core * heads + h) * HD, HD), HD),
                ]
                for n in range(2)
            ],
            axis=0,
        )
        unit_ref[h] = pad_rows(chip_rows, unit_ref.shape[1]).astype(bf16)


def chip_drafts(split, heads, sources):
    rows, half = sources[0].shape
    return pl.pallas_call(
        functools.partial(drafts_kernel, split),
        in_specs=[pl.BlockSpec(memory_space=pltpu.VMEM)] * len(sources),
        out_shape=(
            jax.ShapeDtypeStruct((heads, 2 * LANES, HD), bf16),
            jax.ShapeDtypeStruct((heads, round_up(2 * rows * split, 8), HD), bf16),
        ),
        scratch_shapes=[pltpu.VMEM((LANES, 2 * half), f32)],
        compiler_params=pltpu.CompilerParams(vmem_limit_bytes=VMEM_BYTES),
    )(*sources)


def append_kernel(rel, split, unit_rows, scal, ck_ref, cv_ref, mine_ref, other_ref, *rest):
    nk_ref, nv_ref = rest[-2:]
    rows, width = ck_ref.shape
    chips, heads, both, _ = mine_ref.shape
    local_rows = unit_rows // split
    seq = lax.axis_index("seq")
    chip, core = lax.div(seq, split), lax.rem(seq, split)
    length, accepted = jnp.max(scal[0:1]), jnp.max(scal[1:2])
    first = (seq * pl.num_programs(0) + pl.program_id(0)) * rows - length
    touched = (first < accepted) & (first + rows > 0)

    @pl.when(jnp.logical_not(touched))
    def _():
        nk_ref[...] = ck_ref[...]
        nv_ref[...] = cv_ref[...]

    @pl.when(touched)
    def _():
        depth = chips * both
        place = first + lax.broadcasted_iota(jnp.int32, (rows, depth), 0)
        lane = lax.broadcasted_iota(jnp.int32, (1, depth), 1)
        base = jnp.zeros((1, depth), jnp.int32)
        row = lane
        for n in range(chips):
            here = (lane >= n * both) & (lane < (n + 1) * both)
            base = jnp.where(here, jnp.bitwise_xor(chip, rel[n]) * unit_rows, base)
            row = jnp.where(here, lane - n * both, row)
        chosen = first + lax.broadcasted_iota(jnp.int32, (rows, HD), 0)
        chosen = (chosen >= 0) & (chosen < accepted)
        for side in range(split):
            drafts = mine_ref if side == 0 else other_ref
            source_core = core if side == 0 else 1 - core
            values = [
                drafts[:, h].astype(f32).reshape(depth, HD).astype(bf16) for h in range(heads)
            ]
            for cache_ref, new_ref, start in ((ck_ref, nk_ref, 0), (cv_ref, nv_ref, unit_rows)):
                source = base + row_of(row - start, local_rows, source_core)
                source = jnp.where((row >= start) & (row < start + unit_rows), source, -(1 << 24))
                pick = jnp.where(source == place, 1.0, 0.0).astype(bf16)
                for h in range(heads):
                    lanes = pl.ds(pl.multiple_of((source_core * heads + h) * HD, HD), HD)
                    moved = jnp.dot(pick, values[h], preferred_element_type=f32)
                    new_ref[:, lanes] = jnp.where(
                        chosen, moved, cache_ref[:, lanes].astype(f32)
                    ).astype(bf16)


def append(rel, split, unit_rows, scal, ck, cv, drafts, after):
    rows = ck.shape[0]
    block = rows // 2 if rows % 128 == 0 else rows
    cache_spec = pl.BlockSpec((block, ck.shape[1]), lambda i: (i, 0))
    mine, other = drafts[0], drafts[-1]
    draft_spec = pl.BlockSpec(mine.shape, lambda i: (0, 0, 0, 0))
    shape = jax.ShapeDtypeStruct(ck.shape, bf16)
    return pl.pallas_call(
        functools.partial(append_kernel, rel, split, unit_rows),
        grid=(rows // block,),
        in_specs=[pl.BlockSpec(memory_space=pltpu.VMEM)]
        + [cache_spec, cache_spec, draft_spec, draft_spec]
        + [pl.BlockSpec(memory_space=pl.ANY)] * len(after),
        out_specs=(cache_spec, cache_spec),
        out_shape=(shape, shape),
        compiler_params=pltpu.CompilerParams(vmem_limit_bytes=VMEM_BYTES),
        cost_estimate=pl.CostEstimate(flops=0, bytes_accessed=8 * ck.size, transcendentals=0),
    )(scal, ck, cv, mine, other, *after)


def one_request(n_seq, n_head, dq, dk, dv, ck, cv, accepted, length, weight):
    seq = lax.axis_index("seq")
    local_rows = dq.shape[0]
    heads_kv = dk.shape[1] // HD
    split = 2 if heads_kv % 2 == 0 else 1
    heads = heads_kv // split
    unit_rows = local_rows * split
    unit = unit_rows * GROUP
    n_bits = n_seq.bit_length() - 1
    bits = list(range(n_bits - 1, split - 2, -1))

    def swap(x, bit):
        return lax.ppermute(x, "seq", [(i, i ^ (1 << bit)) for i in range(n_seq)])

    core = seq % split

    q4 = dq.reshape(local_rows, heads_kv, GROUP, LANES).transpose(1, 0, 2, 3)
    q4 = q4.reshape(heads_kv, local_rows * GROUP, LANES)
    drafts_own = [dk, dv]
    caches, drafts_other = [ck, cv], []
    q = q4
    if split == 2:
        mine = lax.dynamic_slice_in_dim(q4, core * heads, heads, 0)
        sent = lax.dynamic_slice_in_dim(q4, (1 - core) * heads, heads, 0)
        q = jnp.concatenate([mine, swap(sent, 0)], axis=1)
    q, scal = lax.optimization_barrier(
        (q[None], jnp.broadcast_to(jnp.stack([length, accepted]), (2, LANES)))
    )
    if split == 2:
        q, drafts_own, *late = lax.optimization_barrier((q, drafts_own, ck, cv))
        drafts_other = [swap(d, 0) for d in drafts_own]
        caches += [swap(c, 0) for c in late]

    rel, near = [0], bits[-1]
    for bit in bits[:-1]:
        new = swap(q, bit)
        q = jnp.concatenate([q, new], axis=0)
        if split == 2 and bit == bits[0]:
            q, drafts_own, drafts_other, *own = lax.optimization_barrier(
                (q, drafts_own, drafts_other, ck, cv)
            )
            caches[:2] = [
                lax.dynamic_slice_in_dim(c, core * heads * HD, heads * HD, 1) for c in own
            ]
        rel = rel + [r | (1 << bit) // split for r in rel]
    drafts, chip_rows = chip_drafts(split, heads, [*drafts_own, *drafts_other])
    rel_far = [r | (1 << near) // split for r in rel]
    q_far = swap(q, near)

    run = functools.partial(attend, scal)
    (message,) = run(q, rel, unit_rows, split, caches, drafts, True)
    num, stats = run(q_far, rel_far, unit_rows, split, caches, drafts, False, (message,))
    message = swap(message, near)

    dkv, order = chip_rows[None], [0]

    for bit in reversed(bits[:-1]):
        mode = "all" if bit == bits[0] else "half"
        num, stats, message = merge(unit, mode, num, stats, message)
        if bit in (bits[-2], bits[0]):
            num, dkv = lax.optimization_barrier((num, dkv))
            for late in bits[-2:-1] if bit == bits[-2] else bits[:-2]:
                dkv = jnp.concatenate([dkv, swap(dkv, late)], axis=0)
                order = order + [r ^ (1 << late) // split for r in order]
        message = swap(message, bit)

    att = merge(unit, "final", num, stats, message).reshape(-1, heads, unit, LANES)
    for bit in bits[1:-1]:
        att = jnp.concatenate([att, swap(att, bit)], axis=0)
    att, dkv = lax.optimization_barrier((att, dkv))
    att_near = swap(att, near)
    dkv = jnp.concatenate([dkv, swap(dkv, near)], axis=0)
    order = order + [r ^ (1 << near) // split for r in order]
    halves = (rel_far, rel)
    if split == 2:
        begun = project(
            halves,
            split,
            n_head,
            ((0, 0), (0, 1), (1, 0)),
            [att, att_near, swap(att, 0)],
            weight,
        )
        begun, dkv = lax.optimization_barrier((begun, dkv))
        result = project(
            halves, split, n_head, ((1, 1),), [swap(att_near, 0)], weight, begun, True
        )
    else:
        result = project(
            halves, split, n_head, ((0, 0), (0, 1)), [att, att_near], weight, (), True
        )
    if n_head == 2:
        keep, send = result
        projected = keep + lax.ppermute(send, "head", [(0, 1), (1, 0)]).astype(f32)
    else:
        projected = lax.psum_scatter(result[0], "head", scatter_dimension=0, tiled=True)
    every = [dkv, swap(dkv, 0)] if split == 2 else [dkv]
    new_key, new_value = append(
        order, split, unit_rows, scal, ck, cv, every, (result[-1],)
    )
    return projected.astype(bf16), new_key, new_value


def on_device(n_seq, n_head, dq, dk, dv, ck, cv, accepted, cache_len, weight):
    results = [
        one_request(
            n_seq, n_head, dq[r], dk[r], dv[r], ck[r], cv[r], accepted[r : r + 1], cache_len[r : r + 1], weight
        )
        for r in range(dq.shape[0])
    ]
    return tuple(jnp.stack(parts) for parts in zip(*results))


def solution(mesh):
    in_specs = (
        P(None, "seq", "head"),
        P(None, "seq", "head"),
        P(None, "seq", "head"),
        P(None, "seq", "head"),
        P(None, "seq", "head"),
        P(),
        P(),
        P("head", "seq"),
    )
    out_specs = (P(None, "head", "seq"), P(None, "seq", "head"), P(None, "seq", "head"))
    return jax.shard_map(
        functools.partial(on_device, mesh.shape["seq"], mesh.shape["head"]),
        mesh=mesh,
        in_specs=in_specs,
        out_specs=out_specs,
        check_vma=False,
    )
```

```python
import functools
import math

import jax
import jax.numpy as jnp
from jax import lax
from jax.experimental import pallas as pl
from jax.experimental.pallas import tpu as pltpu
from jax.sharding import PartitionSpec as P

QH = 64
KVH = 8
HD = 128
GROUP = QH // KVH
LANES = 128

DEAD = -1e30
FLOOR = -(2.0**96)
LOG2_SCALE = math.log2(math.e) / math.sqrt(HD)
VMEM_BYTES = 48 * 1024 * 1024

bf16 = jnp.bfloat16
f32 = jnp.float32


def round_up(n, m):
    return -(-n // m) * m


def stat_rows(units):
    return round_up(3 * round_up(units, 8), 16)


def pad_rows(x, rows):
    if x.shape[0] == rows:
        return x
    return jnp.concatenate([x, jnp.zeros((rows - x.shape[0], x.shape[1]), x.dtype)], axis=0)


def columns_to_rows(columns, unit):
    lane = lax.broadcasted_iota(jnp.int32, (unit, LANES), 1)
    square = jnp.zeros((unit, LANES), f32)
    for place, column in columns:
        square = jnp.where(lane == place, column, square)
    return jnp.transpose(pad_rows(square, LANES))


def split_total(total):
    high = total.astype(bf16)
    return high, (total - high.astype(f32)).astype(bf16)


def write_message(out_ref, row, shift, total):
    high, low = split_total(total)
    rows = jnp.concatenate([shift, high.astype(f32), low.astype(f32)], axis=0)
    out_ref[row : row + stat_rows(shift.shape[0]), :] = pad_rows(
        rows, stat_rows(shift.shape[0])
    ).astype(bf16)


def row_of(place, local_rows, core):
    return place + jnp.where(place < local_rows, core, -core) * local_rows


def attend_kernel(rel, unit_rows, split, as_message, n_after, scal, q_ref, *rest):
    caches = rest[: 2 * split]
    d_ref = rest[2 * split]
    outs = rest[2 * split + 1 + n_after :]
    units, heads = q_ref.shape[:2]
    unit = unit_rows * GROUP
    keys = caches[0].shape[0]
    seq, length = lax.axis_index("seq"), scal[0:1, 0:1]
    chip = lax.div(seq, split)
    count = units * heads
    count8 = round_up(count, 8)
    step = max(n for n in range(1, units + 1) if units % n == 0 and n * unit <= 384)
    columns = []
    out_ref = outs[0]
    key_index = lax.broadcasted_iota(jnp.int32, (1, keys), 1)
    core = lax.rem(seq, split)
    local_rows = unit_rows // split
    ones = jnp.ones((keys, LANES), bf16)
    draft = lax.broadcasted_iota(jnp.int32, (1, LANES), 1)
    draft_row = unit_rows * chip + row_of(draft, local_rows, core)
    unit_row = row_of(
        lax.shift_right_logical(lax.broadcasted_iota(jnp.int32, (unit, LANES), 0), 3),
        local_rows,
        core,
    )
    def lanes_of(head, side):
        if side == 0:
            return slice(head * HD, (head + 1) * HD)
        return pl.ds(pl.multiple_of((core * heads + head) * HD, HD), HD)

    def score_of(chunk):
        head, start, side = chunk
        queries = q_ref[start : start + step, head].reshape(step * unit, HD)
        return lax.dot_general(
            queries, caches[2 * side][:, lanes_of(head, side)], (((1,), (1,)), ((), ())), preferred_element_type=f32
        )

    chunks = [
        (head, start, side)
        for head in range(heads)
        for start in range(0, units, step)
        for side in range(split)
    ]
    tops, sums = [], []
    following = score_of(chunks[0])
    for at, (head, start, side) in enumerate(chunks):
        raw = following
        if at + 1 < len(chunks):
            following = score_of(chunks[at + 1])
        draft_values = jnp.concatenate([d_ref[head, LANES:], ones[:LANES]], axis=1)
        if side == 0:
            time = jnp.concatenate(
                [
                    unit_row + unit_rows * jnp.bitwise_xor(chip, rel[start + n])
                    for n in range(step)
                ],
                axis=0,
            )
            draft_scores = lax.dot_general(
                q_ref[start : start + step, head].reshape(step * unit, HD),
                d_ref[head, :LANES],
                (((1,), (1,)), ((), ())),
                preferred_element_type=f32,
            )
            draft_scores = jnp.where(draft_row <= time, draft_scores * LOG2_SCALE, DEAD)
        block = seq if side == 0 else seq + 1 - 2 * core
        score = jnp.where(key_index + block * keys < length, raw * LOG2_SCALE, DEAD)
        inside = (draft >= side * local_rows) & (draft < (side + 1) * local_rows)
        own_drafts = jnp.where(inside, draft_scores, DEAD)
        top = jnp.maximum(
            jnp.max(score, axis=1, keepdims=True), jnp.max(own_drafts, axis=1, keepdims=True)
        )
        top = jnp.maximum(top, FLOOR)
        tops.append(top)
        values_ones = jnp.concatenate(
            [caches[2 * side + 1][:, lanes_of(head, side)], ones], axis=1
        )
        sums.append(
            jnp.dot(jnp.exp2(score - top).astype(bf16), values_ones, preferred_element_type=f32)
            + jnp.dot(
                jnp.exp2(own_drafts - top).astype(bf16), draft_values, preferred_element_type=f32
            )
        )
        if side + 1 < split:
            continue
        shift = functools.reduce(jnp.maximum, tops).astype(bf16).astype(f32)
        both = sum(part * jnp.exp2(top - shift) for part, top in zip(sums, tops))
        weighted, total = both[:, :HD], both[:, HD : HD + 1]
        for n in range(step):
            place = (start + n) * heads + head
            part = slice(n * unit, (n + 1) * unit)
            out_ref[place * unit : (place + 1) * unit, :] = weighted[part].astype(out_ref.dtype)
            columns.append((place, shift[part]))
            columns.append((count8 + place, total[part]))
        tops, sums = [], []
    stats = columns_to_rows(columns, unit)
    if as_message:
        write_message(out_ref, count * unit, stats[:count8], stats[count8 : 2 * count8])
    else:
        outs[1][...] = stats[: 2 * count8]


def attend(scal, q, rel, unit_rows, split, caches, drafts, as_message, after=()):
    units, heads = q.shape[:2]
    unit = unit_rows * GROUP
    keys = caches[0].shape[0]
    count = units * heads
    if as_message:
        out_shape = (jax.ShapeDtypeStruct((count * unit + stat_rows(count), LANES), bf16),)
    else:
        out_shape = (
            jax.ShapeDtypeStruct((count * unit, LANES), f32),
            jax.ShapeDtypeStruct((2 * round_up(count, 8), LANES), f32),
        )
    whole = pl.BlockSpec(memory_space=pltpu.VMEM)
    in_specs = [whole] * (3 + len(caches))
    in_specs += [pl.BlockSpec(memory_space=pl.ANY)] * len(after)
    scores = count * unit * (split * keys + LANES)
    return pl.pallas_call(
        functools.partial(attend_kernel, rel, unit_rows, split, as_message, len(after)),
        in_specs=in_specs,
        out_specs=(whole,) * len(out_shape),
        out_shape=out_shape,
        compiler_params=pltpu.CompilerParams(vmem_limit_bytes=VMEM_BYTES),
        cost_estimate=pl.CostEstimate(
            flops=4 * scores * HD, bytes_accessed=4 * split * keys * heads * HD, transcendentals=scores
        ),
    )(scal, q, *caches, drafts, *after)


def merge_kernel(unit, mode, num_ref, stat_ref, msg_ref, *outs):
    rows = num_ref.shape[0]
    count = rows // unit
    count8 = stat_ref.shape[0] // 2
    own_shift, own_total = stat_ref[:count8], stat_ref[count8:]
    sent = msg_ref[rows:, :].astype(f32)
    shift = sent[:count8]
    total = sent[count8 : 2 * count8] + sent[2 * count8 : 3 * count8]
    half = count // 2
    if mode == "final":
        shift = pad_rows(jnp.concatenate([shift[half:count], shift[:half]], axis=0), count8)
        total = pad_rows(jnp.concatenate([total[half:count], total[:half]], axis=0), count8)
    new_shift = jnp.maximum(own_shift, shift)
    own_factor = jnp.exp2(own_shift - new_shift)
    factor = jnp.exp2(shift - new_shift)
    new_total = own_total * own_factor + total * factor
    if mode == "final":
        new_total = jnp.where(new_total > 0, new_total, 1.0)
        own_factor = own_factor / new_total
        factor = factor / new_total
    factors = jnp.transpose(pad_rows(jnp.concatenate([own_factor, factor], axis=0), LANES))
    for n in range(count):
        source = (n + half) % count if mode == "final" else n
        merged = num_ref[n * unit : (n + 1) * unit, :] * factors[:unit, n : n + 1]
        merged = merged + (
            msg_ref[source * unit : (source + 1) * unit, :].astype(f32)
            * factors[:unit, count8 + n : count8 + n + 1]
        )
        here = slice(n * unit, (n + 1) * unit)
        if mode == "final":
            outs[0][here, :] = merged.astype(bf16)
        elif mode == "all":
            outs[0][here, :] = merged
            outs[2][here, :] = merged.astype(bf16)
        elif n < half:
            outs[0][here, :] = merged
        else:
            outs[2][(n - half) * unit : (n - half + 1) * unit, :] = merged.astype(bf16)
    if mode == "all":
        outs[1][...] = jnp.concatenate([new_shift, new_total], axis=0)
        write_message(outs[2], rows, new_shift, new_total)
    elif mode == "half":
        half8 = round_up(half, 8)
        outs[1][...] = jnp.concatenate(
            [pad_rows(new_shift[:half], half8), pad_rows(new_total[:half], half8)], axis=0
        )
        write_message(
            outs[2],
            half * unit,
            pad_rows(new_shift[half:count], half8),
            pad_rows(new_total[half:count], half8),
        )


def merge(unit, mode, num, stats, message):
    rows = num.shape[0]
    if mode == "final":
        out_shape = jax.ShapeDtypeStruct((rows, LANES), bf16)
    else:
        rows = rows // 2 if mode == "half" else rows
        count = rows // unit
        out_shape = (
            jax.ShapeDtypeStruct((rows, LANES), f32),
            jax.ShapeDtypeStruct((2 * round_up(count, 8), LANES), f32),
            jax.ShapeDtypeStruct((rows + stat_rows(count), LANES), bf16),
        )
    return pl.pallas_call(
        functools.partial(merge_kernel, unit, mode),
        out_shape=out_shape,
        compiler_params=pltpu.CompilerParams(vmem_limit_bytes=VMEM_BYTES),
    )(num, stats, message)


def project_kernel(rel, split, n_head, parts, n_partial, *refs):
    sources, w_ref = refs[: len(parts)], refs[len(parts)]
    partial = refs[len(parts) + 1 : len(parts) + 1 + n_partial]
    outs, (rows_ref, lhs_ref) = refs[len(parts) + 1 + n_partial : -2], refs[-2:]
    seq, head = lax.axis_index("seq"), lax.axis_index("head")
    chip = lax.div(seq, split)
    core = lax.rem(seq, split)
    units, heads, unit, _ = sources[0].shape
    chips = 2 * units
    piece = unit // split
    first = head * (chips // n_head) if n_head == 2 else 0
    slots = rows_ref.shape[0] // heads
    if len(parts) < 2 * slots:
        rows_ref[...] = jnp.zeros_like(rows_ref)
    for (side, part), x_ref in zip(parts, sources):
        owner = core if side == 0 else 1 - core
        slot = owner if slots == split else 0
        for n in range(units):
            place = lax.rem(jnp.bitwise_xor(chip, rel[part][n]) - first + chips, chips)
            for part_of in range(split):
                row = place * unit + (owner if part_of == 0 else 1 - owner) * piece
                for h in range(heads):
                    rows_ref[slot * heads + h, pl.ds(pl.multiple_of(row, 16), piece), :] = x_ref[
                        n, h, part_of * piece : (part_of + 1) * piece
                    ].astype(f32)
    rows, depth = lhs_ref.shape
    for kv in range(rows_ref.shape[0]):
        for g in range(GROUP):
            lanes = slice((kv * GROUP + g) * HD, (kv * GROUP + g + 1) * HD)
            lhs_ref[:, lanes] = rows_ref[kv, pl.ds(g, rows, stride=GROUP), :].astype(bf16)
    if slots == split:
        weight = w_ref[...]
    else:
        weight = w_ref[pl.ds(pl.multiple_of((1 - core) * depth, LANES), depth), :]
    result = jnp.dot(lhs_ref[...], weight, preferred_element_type=f32)
    for ref in partial:
        result = result + ref[...]
    if len(outs) == 2:
        outs[0][...] = result[: rows // 2]
        outs[1][...] = result[rows // 2 :].astype(bf16)
    else:
        outs[0][...] = result


def project(rel, split, n_head, parts, sources, weight, partial=(), whole=False):
    units, heads, unit, _ = sources[0].shape
    slots = 1 if partial else split
    rows = 2 * units * unit // GROUP
    columns = weight.shape[1]
    if n_head == 2 and whole:
        out_shape = tuple(jax.ShapeDtypeStruct((rows // 2, columns), t) for t in (f32, bf16))
    else:
        out_shape = (jax.ShapeDtypeStruct((rows, columns), f32),)
    return pl.pallas_call(
        functools.partial(project_kernel, rel, split, n_head, parts, len(partial)),
        in_specs=[pl.BlockSpec(memory_space=pltpu.VMEM)] * (len(sources) + 1 + len(partial)),
        out_shape=out_shape,
        scratch_shapes=[
            pltpu.VMEM((heads * slots, 2 * units * unit, LANES), f32),
            pltpu.VMEM((rows, heads * slots * GROUP * HD), bf16),
        ],
        compiler_params=pltpu.CompilerParams(vmem_limit_bytes=VMEM_BYTES),
        cost_estimate=pl.CostEstimate(
            flops=2 * rows * columns * heads * slots * GROUP * HD,
            bytes_accessed=2 * columns * heads * slots * GROUP * HD,
            transcendentals=0,
        ),
    )(*sources, weight, *partial)


def drafts_kernel(split, *refs):
    sources, (draft_ref, unit_ref, rows_ref) = refs[:-3], refs[-3:]
    rows, half = sources[0].shape
    width = 2 * half
    heads = draft_ref.shape[0]
    core = lax.rem(lax.axis_index("seq"), split)
    rows_ref[...] = jnp.zeros_like(rows_ref)
    for n in range(split):
        rows_ref[n * rows : (n + 1) * rows, :half] = sources[2 * n][...].astype(f32)
        rows_ref[n * rows : (n + 1) * rows, half:] = sources[2 * n + 1][...].astype(f32)
    unit_rows = rows * split
    for h in range(heads):
        for n in range(2):
            lanes = pl.ds(pl.multiple_of(n * (width // 2) + (core * heads + h) * HD, HD), HD)
            draft_ref[h, n * LANES : (n + 1) * LANES, :] = rows_ref[:, lanes].astype(bf16)
        chip_rows = jnp.concatenate(
            [
                rows_ref[
                    :unit_rows,
                    pl.ds(pl.multiple_of(n * (width // 2) + (core * heads + h) * HD, HD), HD),
                ]
                for n in range(2)
            ],
            axis=0,
        )
        unit_ref[h] = pad_rows(chip_rows, unit_ref.shape[1]).astype(bf16)


def chip_drafts(split, heads, sources):
    rows, half = sources[0].shape
    return pl.pallas_call(
        functools.partial(drafts_kernel, split),
        in_specs=[pl.BlockSpec(memory_space=pltpu.VMEM)] * len(sources),
        out_shape=(
            jax.ShapeDtypeStruct((heads, 2 * LANES, HD), bf16),
            jax.ShapeDtypeStruct((heads, round_up(2 * rows * split, 8), HD), bf16),
        ),
        scratch_shapes=[pltpu.VMEM((LANES, 2 * half), f32)],
        compiler_params=pltpu.CompilerParams(vmem_limit_bytes=VMEM_BYTES),
    )(*sources)


def append_kernel(rel, split, unit_rows, scal, ck_ref, cv_ref, mine_ref, other_ref, *rest):
    nk_ref, nv_ref = rest[-2:]
    rows, width = ck_ref.shape
    chips, heads, both, _ = mine_ref.shape
    local_rows = unit_rows // split
    seq = lax.axis_index("seq")
    chip, core = lax.div(seq, split), lax.rem(seq, split)
    length, accepted = jnp.max(scal[0:1]), jnp.max(scal[1:2])
    first = (seq * pl.num_programs(0) + pl.program_id(0)) * rows - length
    touched = (first < accepted) & (first + rows > 0)

    @pl.when(jnp.logical_not(touched))
    def _():
        nk_ref[...] = ck_ref[...]
        nv_ref[...] = cv_ref[...]

    @pl.when(touched)
    def _():
        depth = chips * both
        place = first + lax.broadcasted_iota(jnp.int32, (rows, depth), 0)
        lane = lax.broadcasted_iota(jnp.int32, (1, depth), 1)
        base = jnp.zeros((1, depth), jnp.int32)
        row = lane
        for n in range(chips):
            here = (lane >= n * both) & (lane < (n + 1) * both)
            base = jnp.where(here, jnp.bitwise_xor(chip, rel[n]) * unit_rows, base)
            row = jnp.where(here, lane - n * both, row)
        chosen = first + lax.broadcasted_iota(jnp.int32, (rows, HD), 0)
        chosen = (chosen >= 0) & (chosen < accepted)
        for side in range(split):
            drafts = mine_ref if side == 0 else other_ref
            source_core = core if side == 0 else 1 - core
            values = [
                drafts[:, h].astype(f32).reshape(depth, HD).astype(bf16) for h in range(heads)
            ]
            for cache_ref, new_ref, start in ((ck_ref, nk_ref, 0), (cv_ref, nv_ref, unit_rows)):
                source = base + row_of(row - start, local_rows, source_core)
                source = jnp.where((row >= start) & (row < start + unit_rows), source, -(1 << 24))
                pick = jnp.where(source == place, 1.0, 0.0).astype(bf16)
                for h in range(heads):
                    lanes = pl.ds(pl.multiple_of((source_core * heads + h) * HD, HD), HD)
                    moved = jnp.dot(pick, values[h], preferred_element_type=f32)
                    new_ref[:, lanes] = jnp.where(
                        chosen, moved, cache_ref[:, lanes].astype(f32)
                    ).astype(bf16)


def append(rel, split, unit_rows, scal, ck, cv, drafts, after):
    rows = ck.shape[0]
    block = rows // 2 if rows % 128 == 0 else rows
    cache_spec = pl.BlockSpec((block, ck.shape[1]), lambda i: (i, 0))
    mine, other = drafts[0], drafts[-1]
    draft_spec = pl.BlockSpec(mine.shape, lambda i: (0, 0, 0, 0))
    shape = jax.ShapeDtypeStruct(ck.shape, bf16)
    return pl.pallas_call(
        functools.partial(append_kernel, rel, split, unit_rows),
        grid=(rows // block,),
        in_specs=[pl.BlockSpec(memory_space=pltpu.VMEM)]
        + [cache_spec, cache_spec, draft_spec, draft_spec]
        + [pl.BlockSpec(memory_space=pl.ANY)] * len(after),
        out_specs=(cache_spec, cache_spec),
        out_shape=(shape, shape),
        compiler_params=pltpu.CompilerParams(vmem_limit_bytes=VMEM_BYTES),
        cost_estimate=pl.CostEstimate(flops=0, bytes_accessed=8 * ck.size, transcendentals=0),
    )(scal, ck, cv, mine, other, *after)


def one_request(n_seq, n_head, dq, dk, dv, ck, cv, accepted, length, weight):
    seq = lax.axis_index("seq")
    local_rows = dq.shape[0]
    heads_kv = dk.shape[1] // HD
    split = 2 if heads_kv % 2 == 0 else 1
    heads = heads_kv // split
    unit_rows = local_rows * split
    unit = unit_rows * GROUP
    n_bits = n_seq.bit_length() - 1
    bits = list(range(n_bits - 1, split - 2, -1))

    def swap(x, bit):
        return lax.ppermute(x, "seq", [(i, i ^ (1 << bit)) for i in range(n_seq)])

    core = seq % split

    q4 = dq.reshape(local_rows, heads_kv, GROUP, LANES).transpose(1, 0, 2, 3)
    q4 = q4.reshape(heads_kv, local_rows * GROUP, LANES)
    drafts_own = [dk, dv]
    caches, drafts_other = [ck, cv], []
    q = q4
    if split == 2:
        mine = lax.dynamic_slice_in_dim(q4, core * heads, heads, 0)
        sent = lax.dynamic_slice_in_dim(q4, (1 - core) * heads, heads, 0)
        q = jnp.concatenate([mine, swap(sent, 0)], axis=1)
    q, scal = lax.optimization_barrier(
        (q[None], jnp.broadcast_to(jnp.stack([length, accepted]), (2, LANES)))
    )
    if split == 2:
        q, drafts_own, *late = lax.optimization_barrier((q, drafts_own, ck, cv))
        drafts_other = [swap(d, 0) for d in drafts_own]
        caches += [swap(c, 0) for c in late]

    rel, near = [0], bits[-1]
    for bit in bits[:-1]:
        new = swap(q, bit)
        q = jnp.concatenate([q, new], axis=0)
        if split == 2 and bit == bits[0]:
            q, *own = lax.optimization_barrier((q, ck, cv))
            caches[:2] = [
                lax.dynamic_slice_in_dim(c, core * heads * HD, heads * HD, 1) for c in own
            ]
        rel = rel + [r | (1 << bit) // split for r in rel]
    drafts, chip_rows = chip_drafts(split, heads, [*drafts_own, *drafts_other])
    rel_far = [r | (1 << near) // split for r in rel]
    q_far = swap(q, near)

    run = functools.partial(attend, scal)
    (message,) = run(q, rel, unit_rows, split, caches, drafts, True)
    num, stats = run(q_far, rel_far, unit_rows, split, caches, drafts, False, (message,))
    message = swap(message, near)

    dkv, order = chip_rows[None], [0]

    for bit in reversed(bits[:-1]):
        mode = "all" if bit == bits[0] else "half"
        num, stats, message = merge(unit, mode, num, stats, message)
        if bit in (bits[-2], bits[0]):
            num, dkv = lax.optimization_barrier((num, dkv))
            for late in bits[-2:-1] if bit == bits[-2] else bits[:-2]:
                dkv = jnp.concatenate([dkv, swap(dkv, late)], axis=0)
                order = order + [r ^ (1 << late) // split for r in order]
        message = swap(message, bit)

    att = merge(unit, "final", num, stats, message).reshape(-1, heads, unit, LANES)
    for bit in bits[1:-1]:
        att = jnp.concatenate([att, swap(att, bit)], axis=0)
    att, dkv = lax.optimization_barrier((att, dkv))
    att_near = swap(att, near)
    dkv = jnp.concatenate([dkv, swap(dkv, near)], axis=0)
    order = order + [r ^ (1 << near) // split for r in order]
    halves = (rel_far, rel)
    if split == 2:
        begun = project(
            halves,
            split,
            n_head,
            ((0, 0), (0, 1), (1, 0)),
            [att, att_near, swap(att, 0)],
            weight,
        )
        begun, dkv = lax.optimization_barrier((begun, dkv))
        result = project(
            halves, split, n_head, ((1, 1),), [swap(att_near, 0)], weight, begun, True
        )
    else:
        result = project(
            halves, split, n_head, ((0, 0), (0, 1)), [att, att_near], weight, (), True
        )
    if n_head == 2:
        keep, send = result
        projected = keep + lax.ppermute(send, "head", [(0, 1), (1, 0)]).astype(f32)
    else:
        projected = lax.psum_scatter(result[0], "head", scatter_dimension=0, tiled=True)
    every = [dkv, swap(dkv, 0)] if split == 2 else [dkv]
    new_key, new_value = append(
        order, split, unit_rows, scal, ck, cv, every, (result[-1],)
    )
    return projected.astype(bf16), new_key, new_value


def on_device(n_seq, n_head, dq, dk, dv, ck, cv, accepted, cache_len, weight):
    results = [
        one_request(
            n_seq, n_head, dq[r], dk[r], dv[r], ck[r], cv[r], accepted[r : r + 1], cache_len[r : r + 1], weight
        )
        for r in range(dq.shape[0])
    ]
    return tuple(jnp.stack(parts) for parts in zip(*results))


def solution(mesh):
    in_specs = (
        P(None, "seq", "head"),
        P(None, "seq", "head"),
        P(None, "seq", "head"),
        P(None, "seq", "head"),
        P(None, "seq", "head"),
        P(),
        P(),
        P("head", "seq"),
    )
    out_specs = (P(None, "head", "seq"), P(None, "seq", "head"), P(None, "seq", "head"))
    return jax.shard_map(
        functools.partial(on_device, mesh.shape["seq"], mesh.shape["head"]),
        mesh=mesh,
        in_specs=in_specs,
        out_specs=out_specs,
        check_vma=False,
    )
```
